32 devices in a mesh: seq: 2 (over x), fsdp: 16 (over z, y, core).
Axes of the slice: x: 2, y: 2, z: 4, core: 2. Of those that a mesh axis runs over, the one named last changes fastest.
Arguments:
- inputs: bfloat16 [16, 4096, 1024], P('fsdp', 'seq'), may hold values from -6 to 6
- targets: bfloat16 [16, 4096, 1024], P('fsdp', 'seq'), may hold values from -6 to 6
- valid_count: int32 [16], replicated, may hold values from 1024 to 4096, as said below
- gain_mix: bfloat16 [1024], P(('seq', 'fsdp')), may hold values from 0.5 to 1.5
- w_query: bfloat16 [1024, 256], P(('seq', 'fsdp')), may hold values from -0.1875 to 0.1875
- w_key: bfloat16 [1024, 256], P(('seq', 'fsdp')), may hold values from -0.1875 to 0.1875
- w_value: bfloat16 [1024, 1024], P(('seq', 'fsdp')), may hold values from -0.1875 to 0.1875
- w_out: bfloat16 [1024, 1024], P(('seq', 'fsdp')), may hold values from -3 to 3
- gain_ffn: bfloat16 [1024], P(('seq', 'fsdp')), may hold values from 0.5 to 1.5
- w_gate: bfloat16 [1024, 2752], P(('seq', 'fsdp')), may hold values from -0.1875 to 0.1875
- w_up: bfloat16 [1024, 2752], P(('seq', 'fsdp')), may hold values from -0.1875 to 0.1875
- w_down: bfloat16 [1024, 2752], P(('seq', 'fsdp')), may hold values from -0.109375 to 0.109375
Outputs:
- result: bfloat16 [16, 4096, 1024], P('fsdp', 'seq')
- loss: float32 [], replicated
- input_grad: float32 [16, 4096, 1024], P('fsdp', 'seq')
- grad_gain_mix: float32 [1024], P(('seq', 'fsdp'))
- grad_query: float32 [1024, 256], P(('seq', 'fsdp'))
- grad_key: float32 [1024, 256], P(('seq', 'fsdp'))
- grad_value: float32 [1024, 1024], P(('seq', 'fsdp'))
- grad_out: float32 [1024, 1024], P(('seq', 'fsdp'))
- grad_gain_ffn: float32 [1024], P(('seq', 'fsdp'))
- grad_gate: float32 [1024, 2752], P(('seq', 'fsdp'))
- grad_up: float32 [1024, 2752], P(('seq', 'fsdp'))
- grad_down: float32 [1024, 2752], P(('seq', 'fsdp'))
The draws below stay inside these ranges and needn't reach their ends.
Inputs may be any that keep to these rules, and one draw needn't show every extreme that they name: Tokens of sequence s from position valid_count[s] on carry no target; one sequence has all 4096 and one has 1024.
All inputs are finite; a program needn't handle non-finite values.
Results may differ from the reference program's by a relative error of at most 0.012.
The reference program's roundings to bfloat16 on the way count: a program that leaves them out, or rounds other values in their place, can miss the bound.
Values may be sent and summed in bfloat16 or wider, within the bound.
A program may use at most 384 MiB of HBM per device.

```python
import math
import jax
import jax.numpy as jnp
import numpy as np
from jax import lax

D = 1024
HEADS = 16
FEAT = 16
HEAD_DIM = 64
FF = 2752
BLK = 512
SEQ_LEN = 4096
PHI = 153
SEQS = 16


def draw_valid_count(key, part):
    key_counts, key_ranks = jax.random.split(key)
    counts = jax.random.randint(key_counts, (SEQS,), SEQ_LEN // 4, SEQ_LEN + 1)
    ranking = jax.random.permutation(key_ranks, SEQS)
    counts = jnp.where(ranking == 0, SEQ_LEN, counts)
    counts = jnp.where(ranking == 1, SEQ_LEN // 4, counts)
    return counts.astype(jnp.int32)


def block_levels(rng, shape, shards, least, high):
    level = 1.0
    for axis_at, shards_of in shards:
        steps = jax.random.uniform(jax.random.fold_in(jax.random.fold_in(rng, 6), axis_at), (shards_of,), jnp.float32, least / len(shards), high / len(shards))
        level = level * jnp.repeat(jnp.exp(steps), shape[axis_at] // shards_of).reshape((-1,) + (1,) * (len(shape) - 1 - axis_at))
    return level


def bell_draw(key, shape, spread, reach, cuts=(), kind=jnp.bfloat16):
    result = spread * jax.random.normal(key, shape, jnp.float32)
    if cuts:
        result = result * block_levels(key, shape, cuts, -0.22, 0.18)
    return jnp.clip(result, -reach, reach).astype(kind)


def setup_inputs(seed: int = 0) -> dict:
    streams_of = jax.random.split(jax.random.key(seed), 13)
    return {
        "inputs": bell_draw(streams_of[0], (SEQS, SEQ_LEN, D), 1.0, 6.0, ((0, 16), (1, 2))),
        "targets": bell_draw(streams_of[1], (SEQS, SEQ_LEN, D), 1.0, 6.0, ((0, 16), (1, 2))),
        "valid_count": draw_valid_count(jax.random.fold_in(streams_of[12], 71), 0),
        "gain_mix": jnp.clip(1.0 + 0.1 * jax.random.normal(streams_of[3], (D,), jnp.float32), 0.5, 1.5).astype(jnp.bfloat16),
        "w_query": bell_draw(streams_of[4], (D, HEADS * FEAT), D ** -0.5, 0.1875, ((0, 32),)),
        "w_key": bell_draw(streams_of[5], (D, HEADS * FEAT), D ** -0.5, 0.1875, ((0, 32),)),
        "w_value": bell_draw(streams_of[6], (D, D), D ** -0.5, 0.1875, ((0, 32),)),
        "w_out": bell_draw(streams_of[7], (D, D), (D // 256) ** -0.5, 3.0, ((0, 32),)),
        "gain_ffn": jnp.clip(1.0 + 0.1 * jax.random.normal(streams_of[8], (D,), jnp.float32), 0.5, 1.5).astype(jnp.bfloat16),
        "w_gate": bell_draw(streams_of[9], (D, FF), D ** -0.5, 0.1875, ((0, 32),)),
        "w_up": bell_draw(streams_of[10], (D, FF), D ** -0.5, 0.1875, ((0, 32),)),
        "w_down": bell_draw(streams_of[11], (D, FF), FF ** -0.5, 0.109375, ((0, 32),)),
    }


epsilon = 1e-05
highest = lax.Precision.HIGHEST

@jax.custom_vjp
def low(v):
    return lax.optimization_barrier(v.astype(jnp.bfloat16)).astype(jnp.float32)

@jax.custom_vjp
def low_back(v):
    return v

def low_keep(v):
    return (low(v), None)

def low_pass(kept, grad):
    return (grad,)

def back_keep(v):
    return (v, None)

def back_low(kept, grad):
    return (low(grad),)
low.defvjp(low_keep, low_pass)
low_back.defvjp(back_keep, back_low)

def pair_tables(width):
    upper_rows, upper_cols = np.triu_indices(width, 1)
    count_pairs = upper_rows.size
    left = np.zeros((width, count_pairs), np.float32)
    right = np.zeros((width, count_pairs), np.float32)
    left[upper_rows, np.arange(count_pairs)] = 1.0
    right[upper_cols, np.arange(count_pairs)] = 1.0
    return (jnp.asarray(left), jnp.asarray(right))

def features(values):
    width = values.shape[-1]
    left, right = pair_tables(width)
    square = values * values * (1.0 / math.sqrt(2.0 * width))
    cross = jnp.dot(values, left, precision=highest) * jnp.dot(values, right, precision=highest) * (1.0 / math.sqrt(width))
    linear = values * width ** (-0.25)
    ones = jnp.ones(values.shape[:-1] + (1,), values.dtype)
    return jnp.concatenate([ones, linear, square, cross], -1)

def product(left, right):
    return jnp.dot(left, right, precision=highest, preferred_element_type=jnp.float32)

def rms_norm(values, gain):
    return values * lax.rsqrt(lax.optimization_barrier(jnp.mean(values * values, -1, keepdims=True)) + epsilon) * gain

def attention(query, key, value):
    length = query.shape[0]
    blocks = length // BLK
    factor = 1.0 / math.sqrt(query.shape[-1])
    causal = (jnp.arange(BLK)[:, None] >= jnp.arange(BLK)[None, :]).astype(jnp.float32)

    def step(carry, pieces):
        state, total = carry
        q_blk, k_blk, v_blk = pieces
        scores = low_back(jnp.einsum('thf,shf->hts', q_blk, k_blk, precision=highest) * factor)
        weights = (1.0 + scores + 0.5 * scores * scores) * causal
        query_feat = features(q_blk)
        numerator = jnp.einsum('hts,she->the', low(weights), v_blk, precision=highest)
        numerator = numerator + jnp.einsum('thp,hpe->the', query_feat, state, precision=highest)
        denominator = lax.optimization_barrier(jnp.sum(weights, -1)).T + jnp.einsum('thp,hp->th', query_feat, total, precision=highest)
        output = low_back(numerator) / denominator[..., None]
        key_feat = features(k_blk)
        state = state + jnp.einsum('shp,she->hpe', key_feat, v_blk, precision=highest)
        total = total + lax.optimization_barrier(jnp.sum(key_feat, 0))
        return ((state, total), output)

    def blocked(array):
        return array.reshape((blocks, BLK) + array.shape[1:])
    state_zero = jnp.zeros((HEADS, PHI, HEAD_DIM), jnp.float32)
    total_zero = jnp.zeros((HEADS, PHI), jnp.float32)
    _, outputs = lax.scan(jax.checkpoint(step), (state_zero, total_zero), (blocked(query), blocked(key), blocked(value)))
    return outputs.reshape((length,) + outputs.shape[2:])

def layer(tokens, gain_mix, w_query, w_key, w_value, w_out, gain_ffn, w_gate, w_up, w_down):
    length = tokens.shape[0]
    normed = low(rms_norm(tokens, gain_mix))
    query = low_back(low(product(normed, w_query)))
    key = low_back(low(product(normed, w_key)))
    value = low_back(low(product(normed, w_value)))
    mixed = attention(query.reshape(length, HEADS, FEAT), key.reshape(length, HEADS, FEAT), value.reshape(length, HEADS, HEAD_DIM))
    mixed = low_back(low(mixed.reshape(length, HEADS * HEAD_DIM)))
    resid = tokens + low_back(product(mixed, w_out))
    normed_ffn = low(rms_norm(resid, gain_ffn))
    gate = low_back(product(normed_ffn, w_gate))
    up = low_back(product(normed_ffn, w_up))
    hidden = low_back(low(jax.nn.silu(gate) * up))
    return resid + low_back(product(hidden, w_down.T))

def reference(inputs, targets, valid_count, gain_mix, w_query, w_key, w_value, w_out, gain_ffn, w_gate, w_up, w_down):
    params = tuple((weight.astype(jnp.float32) for weight in (gain_mix, w_query, w_key, w_value, w_out, gain_ffn, w_gate, w_up, w_down)))
    total_valid = jnp.sum(valid_count).astype(jnp.float32)
    places = jnp.arange(SEQ_LEN).astype(jnp.int32)

    def one_sequence(sums, items):
        tokens, target, count = items
        valid = (places < count).astype(jnp.float32)[:, None]
        target = target.astype(jnp.float32)

        def objective(tokens, *weights):
            full = layer(tokens, *weights)
            error = 0.5 * jnp.sum(valid * (full - target) ** 2)
            return (error, full)
        error, pull, full = jax.vjp(objective, tokens.astype(jnp.float32), *params, has_aux=True)
        grads = pull(jnp.ones((), jnp.float32))
        sums = tuple((held + fresh for held, fresh in zip(sums, grads[1:])))
        return (sums, (full.astype(jnp.bfloat16), grads[0], error))
    zero_sums = tuple((jnp.zeros_like(weight) for weight in params))
    sums, (results, input_grad, errors) = lax.scan(one_sequence, zero_sums, (inputs, targets, valid_count))
    loss = 2.0 * jnp.sum(errors) / (D * total_valid)
    return (results, loss, input_grad, sums[0], sums[1], sums[2], sums[3], sums[4], sums[5], sums[6], sums[7], sums[8])
```

```python
import functools
import math

import jax
import jax.numpy as jnp
import numpy as np
from jax import lax
from jax.experimental import pallas as pl
from jax.experimental.pallas import tpu as pltpu
from jax.sharding import PartitionSpec as P

HEADS = 16
FEAT = 16
HEAD_DIM = 64
HROWS = 2 * FEAT + HEAD_DIM
CUT = 256
GROUPS = 11
FROWS = GROUPS * FEAT
VROWS = HEAD_DIM + 16
HG = 4

epsilon = 1e-05
F32 = jnp.float32
BF16 = jnp.bfloat16
NN = (((1,), (0,)), ((), ()))
NT = (((1,), (1,)), ((), ()))
TN = (((0,), (0,)), ((), ()))


def dot(left, right, dims):
    return lax.dot_general(left, right, dims, preferred_element_type=F32)


def first_row(rows, cols, count=1):
    return (lax.broadcasted_iota(jnp.int32, (rows, cols), 0) < count).astype(F32)


def rolled(u, shift):
    return pltpu.roll(u, (FEAT - shift) % FEAT, 0)


def phi_rows(u, const):
    groups = [u * u]
    for d in range(1, 9):
        groups.append(u * rolled(u, d))
    groups.append(u)
    groups.append(const)
    return jnp.concatenate([g.astype(BF16) for g in groups], 0)


def phi_pull(grad, u):
    total = grad[9 * FEAT : 10 * FEAT] + 2.0 * grad[0:FEAT] * u
    for d in range(1, 9):
        g = grad[d * FEAT : (d + 1) * FEAT]
        total = total + g * rolled(u, d) + rolled(g * u, FEAT - d)
    return total


def lane_scale():
    group = lax.broadcasted_iota(jnp.int32, (1, FROWS), 1) // FEAT
    scale = jnp.where((group == 0) | (group == 8), 1.0 / 32.0, 1.0 / 16.0)
    scale = jnp.where(group == 9, 0.25, scale)
    return jnp.where(group == 10, 1.0, scale)


def causal_mask():
    s = lax.broadcasted_iota(jnp.int32, (CUT, CUT), 0)
    t = lax.broadcasted_iota(jnp.int32, (CUT, CUT), 1)
    return s <= t


def state_kernel(blocks, qkv_ref, out_ref):
    ones2 = first_row(16, CUT, 2).astype(BF16)
    const = first_row(FEAT, CUT)

    def step(b, sums):
        cols = pl.ds(pl.multiple_of(b * CUT, CUT), CUT)
        fresh = []
        for h in range(HG):
            base = h * HROWS
            k = qkv_ref[base + FEAT : base + 2 * FEAT, cols].astype(F32)
            v = qkv_ref[base + 2 * FEAT : base + HROWS, cols]
            v_aug = jnp.concatenate([v, ones2], 0)
            fresh.append(sums[h] + dot(v_aug, phi_rows(k, const), NT))
        return tuple(fresh)

    zero = jnp.zeros((VROWS, FROWS), F32)
    sums = lax.fori_loop(0, blocks, step, (zero,) * HG)
    for h in range(HG):
        out_ref[h] = sums[h]


def forward_kernel(blocks, qkv_ref, init_ref, mixed_ref, den_ref, saved_ref, state):
    ones2 = first_row(16, CUT, 2).astype(BF16)
    const = first_row(FEAT, CUT)
    one_low = const.astype(BF16)
    scale = 2.0 * lane_scale()
    mask = causal_mask()
    state[...] = init_ref[...]

    def step(b, carry):
        cols = pl.ds(pl.multiple_of(b * CUT, CUT), CUT)
        for h in range(HG):
            base = h * HROWS
            q = qkv_ref[base : base + FEAT, cols]
            k = qkv_ref[base + FEAT : base + 2 * FEAT, cols]
            v = qkv_ref[base + 2 * FEAT : base + HROWS, cols]
            v_aug = jnp.concatenate([v, ones2], 0)
            k_aug = jnp.concatenate([k, one_low], 0)
            q_aug = jnp.concatenate([q * 0.25, one_low], 0)
            u = dot(k_aug, q_aug, TN)
            weight = jnp.where(mask, u * u + 1.0, 0.0).astype(BF16)
            low = (state[h] * scale).astype(BF16)
            saved_ref[h, b] = low
            numer = dot(v_aug, weight, NN) + dot(low, phi_rows(q.astype(F32), const), NN)
            den = numer[HEAD_DIM : HEAD_DIM + 1]
            mixed_ref[h * HEAD_DIM : (h + 1) * HEAD_DIM, cols] = (
                numer[:HEAD_DIM] / den
            ).astype(BF16)
            den_ref[0, h : h + 1, cols] = 0.5 * den
            state[h] += dot(v_aug, phi_rows(k.astype(F32), const), NT)
        return carry

    lax.fori_loop(0, blocks, step, 0)


def back_state_kernel(blocks, qkv_ref, grad_ref, mixed_ref, den_ref, nb_ref, out_ref):
    const = first_row(FEAT, CUT)
    row = lax.broadcasted_iota(jnp.int32, (16, CUT), 0)

    def step(b, sums):
        cols = pl.ds(pl.multiple_of(b * CUT, CUT), CUT)
        fresh = []
        for h in range(HG):
            base = h * HROWS
            q = qkv_ref[base : base + FEAT, cols].astype(F32)
            rows = slice(h * HEAD_DIM, (h + 1) * HEAD_DIM)
            g = grad_ref[rows, cols].astype(F32)
            inverse = 1.0 / den_ref[0, h : h + 1, cols]
            db = -inverse * jnp.sum(
                g * mixed_ref[rows, cols].astype(F32), axis=0, keepdims=True
            )
            nb = (g * inverse).astype(BF16)
            high = db.astype(BF16).astype(F32)
            tail = jnp.where(row == 0, high, jnp.where(row == 1, db - high, 0.0)).astype(BF16)
            nb_aug = jnp.concatenate([nb, tail], 0)
            nb_ref[h, :, cols] = nb_aug
            fresh.append(sums[h] + dot(nb_aug, phi_rows(q, const), NT))
        return tuple(fresh)

    zero = jnp.zeros((VROWS, FROWS), F32)
    sums = lax.fori_loop(0, blocks, step, (zero,) * HG)
    for h in range(HG):
        out_ref[h] = sums[h]


def backward_kernel(blocks, qkv_ref, nb_ref, saved_ref, init_ref, out_ref, state):
    ones2 = first_row(16, CUT, 2).astype(BF16)
    const = first_row(FEAT, CUT)
    one_low = const.astype(BF16)
    scale = lane_scale()
    mask = causal_mask()
    state[...] = init_ref[...]

    def step(i, carry):
        b = blocks - 1 - i
        cols = pl.ds(pl.multiple_of(b * CUT, CUT), CUT)
        for h in range(HG):
            base = h * HROWS
            q = qkv_ref[base : base + FEAT, cols]
            k = qkv_ref[base + FEAT : base + 2 * FEAT, cols]
            v = qkv_ref[base + 2 * FEAT : base + HROWS, cols]
            qf = q.astype(F32)
            kf = k.astype(F32)
            q4 = q * 0.25
            nb = nb_ref[h, :, cols]
            v_aug = jnp.concatenate([v, ones2], 0)
            k_aug = jnp.concatenate([k, one_low], 0)
            q_aug = jnp.concatenate([q4, one_low], 0)
            u = dot(k_aug, q_aug, TN)
            weight = jnp.where(mask, u * u + 1.0, 0.0).astype(BF16)
            wb = dot(v_aug, nb, TN)
            sb = jnp.where(mask, wb * u, 0.0).astype(BF16)
            q_feat_back = dot(saved_ref[h, b], nb, TN)
            dq = 0.25 * dot(k, sb, NN) + 0.5 * phi_pull(q_feat_back, qf)
            low = (state[h] * scale).astype(BF16)
            k_feat_back = dot(low, v_aug, TN)
            dk = dot(q4, sb, NT) + phi_pull(k_feat_back, kf)
            dv = 0.5 * dot(nb[:HEAD_DIM], weight, NT) + dot(
                low[:HEAD_DIM], phi_rows(kf, const), NN
            )
            out_ref[base : base + FEAT, cols] = dq.astype(BF16)
            out_ref[base + FEAT : base + 2 * FEAT, cols] = dk.astype(BF16)
            out_ref[base + 2 * FEAT : base + HROWS, cols] = dv.astype(BF16)
            state[h] += dot(nb, phi_rows(qf, const), NT)
        return carry

    lax.fori_loop(0, blocks, step, 0)


def head_spec(rows, cols):
    return pl.BlockSpec((HG * rows, cols), lambda g: (g, 0))


def lead_spec(*tail):
    return pl.BlockSpec((HG,) + tail, lambda g: (g,) + (0,) * len(tail))


VMEM_LIMIT = pltpu.CompilerParams(vmem_limit_bytes=56 * 1024 * 1024)


def local_state(qkv):
    cols = qkv.shape[1]
    return pl.pallas_call(
        functools.partial(state_kernel, cols // CUT),
        grid=(HEADS // HG,),
        in_specs=[head_spec(HROWS, cols)],
        out_specs=lead_spec(VROWS, FROWS),
        out_shape=jax.ShapeDtypeStruct((HEADS, VROWS, FROWS), F32),
        compiler_params=VMEM_LIMIT,
        name="key_state",
    )(qkv)


def attention_forward(qkv, init):
    cols = qkv.shape[1]
    blocks = cols // CUT
    return pl.pallas_call(
        functools.partial(forward_kernel, blocks),
        grid=(HEADS // HG,),
        in_specs=[head_spec(HROWS, cols), lead_spec(VROWS, FROWS)],
        out_specs=[
            head_spec(HEAD_DIM, cols),
            pl.BlockSpec((1, HG, cols), lambda g: (g, 0, 0)),
            lead_spec(blocks, VROWS, FROWS),
        ],
        out_shape=[
            jax.ShapeDtypeStruct((HEADS * HEAD_DIM, cols), BF16),
            jax.ShapeDtypeStruct((HEADS // HG, HG, cols), F32),
            jax.ShapeDtypeStruct((HEADS, blocks, VROWS, FROWS), BF16),
        ],
        scratch_shapes=[pltpu.VMEM((HG, VROWS, FROWS), F32)],
        compiler_params=VMEM_LIMIT,
        name="attend",
    )(qkv, init)


def local_back_state(qkv, grad, mixed, den):
    cols = qkv.shape[1]
    return pl.pallas_call(
        functools.partial(back_state_kernel, cols // CUT),
        grid=(HEADS // HG,),
        in_specs=[
            head_spec(HROWS, cols),
            head_spec(HEAD_DIM, cols),
            head_spec(HEAD_DIM, cols),
            pl.BlockSpec((1, HG, cols), lambda g: (g, 0, 0)),
        ],
        out_specs=[lead_spec(VROWS, cols), lead_spec(VROWS, FROWS)],
        out_shape=[
            jax.ShapeDtypeStruct((HEADS, VROWS, cols), BF16),
            jax.ShapeDtypeStruct((HEADS, VROWS, FROWS), F32),
        ],
        compiler_params=VMEM_LIMIT,
        name="query_state",
    )(qkv, grad, mixed, den)


def attention_backward(qkv, nb, saved, init):
    cols = qkv.shape[1]
    blocks = cols // CUT
    return pl.pallas_call(
        functools.partial(backward_kernel, blocks),
        grid=(HEADS // HG,),
        in_specs=[
            head_spec(HROWS, cols),
            lead_spec(VROWS, cols),
            lead_spec(blocks, VROWS, FROWS),
            lead_spec(VROWS, FROWS),
        ],
        out_specs=head_spec(HROWS, cols),
        out_shape=jax.ShapeDtypeStruct((HEADS * HROWS, cols), BF16),
        scratch_shapes=[pltpu.VMEM((HG, VROWS, FROWS), F32)],
        compiler_params=VMEM_LIMIT,
        name="attend_back",
    )(qkv, nb, saved, init)


def shifted_sum(array, parts, sign):
    total = jnp.zeros_like(array)
    for shift in range(1, parts):
        if sign > 0:
            pairs = [(i, i + shift) for i in range(parts - shift)]
        else:
            pairs = [(i + shift, i) for i in range(parts - shift)]
        total = total + lax.ppermute(array, "seq", pairs)
    return total


def body(
    inputs,
    targets,
    valid_count,
    gain_mix,
    w_query,
    w_key,
    w_value,
    w_out,
    gain_ffn,
    w_gate,
    w_up,
    w_down,
):
    both = ("seq", "fsdp")
    seq_parts = lax.axis_size("seq")
    seq_index = lax.axis_index("seq")
    batch_index = lax.axis_index("fsdp")
    rows, width = inputs.shape[1:]
    hidden_units = w_gate.shape[1]
    tokens = inputs[0].astype(F32)
    target = targets[0].astype(F32)
    owners = jnp.arange(valid_count.shape[0])
    count = jnp.sum(jnp.where(owners == batch_index, valid_count, 0))
    total_valid = jnp.sum(valid_count).astype(F32)
    positions = seq_index * rows + jnp.arange(rows)
    valid = (positions < count).astype(F32)[:, None]
    gains = jnp.pad(jnp.stack([gain_mix, gain_ffn], 1), ((0, 0), (0, 126)))
    early = jnp.concatenate([gains, w_query, w_key, w_value], 1)
    early = lax.all_gather(early, both, axis=0, tiled=True)
    gain_one = early[:, 0].astype(F32)
    gain_two = early[:, 1].astype(F32)
    late = lax.all_gather(
        jnp.concatenate([w_out, w_gate, w_up, w_down], 1), both, axis=0, tiled=True
    )
    full_out = late[:, :width]
    full_gate = late[:, width : width + hidden_units]
    full_up = late[:, width + hidden_units : width + 2 * hidden_units]
    full_down = late[:, width + 2 * hidden_units :]
    lead = HEADS * FEAT
    w_qkv = jnp.concatenate(
        [
            early[:, 128 : 128 + lead].reshape(width, HEADS, FEAT),
            early[:, 128 + lead : 128 + 2 * lead].reshape(width, HEADS, FEAT),
            early[:, 128 + 2 * lead :].reshape(width, HEADS, HEAD_DIM),
        ],
        2,
    ).reshape(width, HEADS * HROWS)
    w_qkv_t = w_qkv.T
    scale_mix = lax.rsqrt(jnp.mean(tokens * tokens, -1, keepdims=True) + epsilon)
    unit_mix = tokens * scale_mix
    normed = (unit_mix * gain_one).astype(BF16)
    qkv = dot(w_qkv_t, normed, NT).astype(BF16)
    state = shifted_sum(local_state(qkv), seq_parts, 1)
    mixed, den, saved = attention_forward(qkv, state)
    resid = tokens + dot(mixed, full_out, TN)
    scale_ffn = lax.rsqrt(jnp.mean(resid * resid, -1, keepdims=True) + epsilon)
    unit_ffn = resid * scale_ffn
    normed_ffn = (unit_ffn * gain_two).astype(BF16)
    gate = dot(normed_ffn, full_gate, NN)
    upward = dot(normed_ffn, full_up, NN)
    sigmoid = jax.nn.sigmoid(gate)
    activated = gate * sigmoid
    hidden = (activated * upward).astype(BF16)
    full_result = resid + dot(hidden, full_down, NT)
    difference = valid * (full_result - target)
    local_error = 0.5 * jnp.sum(difference * difference)
    error = lax.psum(local_error, both)
    loss = 2.0 * error / (width * total_valid)
    branch_back = difference.astype(BF16)
    grad_down = dot(branch_back, hidden, TN)
    hidden_back = dot(branch_back, full_down, NN).astype(BF16).astype(F32)
    gate_back = (hidden_back * upward * sigmoid * (1.0 + gate * (1.0 - sigmoid))).astype(BF16)
    up_back = (hidden_back * activated).astype(BF16)
    grad_gate = dot(normed_ffn, gate_back, TN)
    grad_up = dot(normed_ffn, up_back, TN)
    ffn_back = dot(gate_back, full_gate, NT) + dot(up_back, full_up, NT)
    grad_gain_two = jnp.sum(ffn_back * unit_ffn, 0)
    scaled_back = ffn_back * gain_two
    resid_back = difference + scale_ffn * (
        scaled_back - unit_ffn * jnp.mean(scaled_back * unit_ffn, -1, keepdims=True)
    )
    attended_back = resid_back.astype(BF16)
    grad_out = dot(mixed, attended_back, NN)
    late_grads = jnp.concatenate(
        [g.astype(BF16) for g in (grad_out, grad_gate, grad_up, grad_down)], 1
    )
    late_sums = scatter(late_grads)
    mixed_back = dot(full_out, attended_back, NT).astype(BF16)
    nb, back = local_back_state(qkv, mixed_back, mixed, den)
    later = shifted_sum(back, seq_parts, -1)
    qkv_back = attention_backward(qkv, nb, saved, later)
    grad_qkv = dot(qkv_back, normed, NN)
    normed_back = dot(qkv_back, w_qkv_t, TN)
    grad_gain_one = jnp.sum(normed_back * unit_mix, 0)
    mix_back = normed_back * gain_one
    input_back = resid_back + scale_mix * (
        mix_back - unit_mix * jnp.mean(mix_back * unit_mix, -1, keepdims=True)
    )
    grad_gains = jnp.pad(jnp.stack([grad_gain_one, grad_gain_two], 1), ((0, 0), (0, 126)))
    early_grads = jnp.concatenate([grad_gains.astype(BF16), grad_qkv.astype(BF16).T], 1)
    early_sums = scatter(early_grads)
    qkv_sums = early_sums[:, 128:].reshape(-1, HEADS, HROWS)
    own = early_sums.shape[0]
    return (
        full_result.astype(BF16)[None],
        loss,
        input_back[None],
        early_sums[:, 0],
        qkv_sums[:, :, :FEAT].reshape(own, lead),
        qkv_sums[:, :, FEAT : 2 * FEAT].reshape(own, lead),
        qkv_sums[:, :, 2 * FEAT :].reshape(own, HEADS * HEAD_DIM),
        late_sums[:, :width],
        early_sums[:, 1],
        late_sums[:, width : width + hidden_units],
        late_sums[:, width + hidden_units : width + 2 * hidden_units],
        late_sums[:, width + 2 * hidden_units :],
    )


def scatter(grads):
    seq_parts = lax.axis_size("seq")
    fsdp_parts = lax.axis_size("fsdp")
    grouped = grads.reshape((seq_parts, fsdp_parts, -1) + grads.shape[1:])
    part = lax.psum_scatter(grouped, "seq", scatter_dimension=0, tiled=True)
    part = lax.psum_scatter(part, "fsdp", scatter_dimension=1, tiled=True)
    return part.reshape((-1,) + grads.shape[1:]).astype(F32)


def solution(mesh):
    both = P(("seq", "fsdp"))
    rows = P(("seq", "fsdp"), None)
    tokens = P("fsdp", "seq", None)
    return jax.shard_map(
        body,
        mesh=mesh,
        in_specs=(tokens, tokens, P(), both, rows, rows, rows, rows, both, rows, rows, rows),
        out_specs=(tokens, P(), tokens, both, rows, rows, rows, rows, both, rows, rows, rows),
        check_vma=False,
    )
```

```python
import functools
import math

import jax
import jax.numpy as jnp
import numpy as np
from jax import lax
from jax.experimental import pallas as pl
from jax.experimental.pallas import tpu as pltpu
from jax.sharding import PartitionSpec as P

HEADS = 16
FEAT = 16
HEAD_DIM = 64
HROWS = 2 * FEAT + HEAD_DIM
CUT = 256
GROUPS = 11
FROWS = GROUPS * FEAT
VROWS = HEAD_DIM + 16
PAIR = 2 * VROWS
HG = 4

epsilon = 1e-05
F32 = jnp.float32
BF16 = jnp.bfloat16
NN = (((1,), (0,)), ((), ()))
NT = (((1,), (1,)), ((), ()))
TN = (((0,), (0,)), ((), ()))


def dot(left, right, dims):
    return lax.dot_general(left, right, dims, preferred_element_type=F32)


def first_row(rows, cols, count=1):
    return (lax.broadcasted_iota(jnp.int32, (rows, cols), 0) < count).astype(F32)


def rolled(u, shift):
    return pltpu.roll(u, (FEAT - shift) % FEAT, 0)


def phi_rows(u, const):
    groups = [u * u]
    for d in range(1, 9):
        groups.append(u * rolled(u, d))
    groups.append(u)
    groups.append(const)
    return jnp.concatenate([g.astype(BF16) for g in groups], 0)


def phi_pull(grad, u):
    total = grad[9 * FEAT : 10 * FEAT] + 2.0 * grad[0:FEAT] * u
    for d in range(1, 9):
        g = grad[d * FEAT : (d + 1) * FEAT]
        total = total + g * rolled(u, d) + rolled(g * u, FEAT - d)
    return total


def lane_scale():
    group = lax.broadcasted_iota(jnp.int32, (1, FROWS), 1) // FEAT
    scale = jnp.where((group == 0) | (group == 8), 1.0 / 32.0, 1.0 / 16.0)
    scale = jnp.where(group == 9, 0.25, scale)
    return jnp.where(group == 10, 1.0, scale)


def causal_mask():
    s = lax.broadcasted_iota(jnp.int32, (CUT, CUT), 0)
    t = lax.broadcasted_iota(jnp.int32, (CUT, CUT), 1)
    return s <= t


def split_pair(wide):
    high = wide.astype(BF16)
    return jnp.concatenate([high, (wide - high.astype(F32)).astype(BF16)], 0)


def twice(rows):
    return jnp.concatenate([rows, rows], 0)


def state_kernel(blocks, qkv_ref, out_ref):
    ones2 = first_row(16, CUT, 2).astype(BF16)
    const = first_row(FEAT, CUT)

    def step(b, sums):
        cols = pl.ds(pl.multiple_of(b * CUT, CUT), CUT)
        fresh = []
        for h in range(HG):
            base = h * HROWS
            k = qkv_ref[base + FEAT : base + 2 * FEAT, cols].astype(F32)
            v = qkv_ref[base + 2 * FEAT : base + HROWS, cols]
            v_aug = jnp.concatenate([v, ones2], 0)
            fresh.append(sums[h] + dot(v_aug, phi_rows(k, const), NT))
        return tuple(fresh)

    zero = jnp.zeros((VROWS, FROWS), F32)
    sums = lax.fori_loop(0, blocks, step, (zero,) * HG)
    for h in range(HG):
        out_ref[h] = sums[h]


def forward_kernel(blocks, qkv_ref, init_ref, mixed_ref, den_ref, saved_ref, state):
    ones2 = first_row(16, CUT, 2).astype(BF16)
    const = first_row(FEAT, CUT)
    one_low = const.astype(BF16)
    scale = 2.0 * lane_scale()
    mask = causal_mask()
    state[...] = init_ref[...]

    def step(b, carry):
        cols = pl.ds(pl.multiple_of(b * CUT, CUT), CUT)
        for h in range(HG):
            base = h * HROWS
            q = qkv_ref[base : base + FEAT, cols]
            k = qkv_ref[base + FEAT : base + 2 * FEAT, cols]
            v = qkv_ref[base + 2 * FEAT : base + HROWS, cols]
            v_aug = jnp.concatenate([v, ones2], 0)
            k_aug = jnp.concatenate([k, one_low], 0)
            q_aug = jnp.concatenate([q * 0.25, one_low], 0)
            u = dot(k_aug, q_aug, TN)
            weight = jnp.where(mask, u * u + 1.0, 0.0).astype(BF16)
            low = split_pair(state[h] * scale)
            saved_ref[h, b] = low
            earlier = dot(low, phi_rows(q.astype(F32), const), NN)
            numer = dot(v_aug, weight, NN) + (earlier[:VROWS] + earlier[VROWS:])
            den = numer[HEAD_DIM : HEAD_DIM + 1]
            mixed_ref[h * HEAD_DIM : (h + 1) * HEAD_DIM, cols] = (
                numer[:HEAD_DIM] / den
            ).astype(BF16)
            den_ref[0, h : h + 1, cols] = 0.5 * den
            state[h] += dot(v_aug, phi_rows(k.astype(F32), const), NT)
        return carry

    lax.fori_loop(0, blocks, step, 0)


def back_state_kernel(blocks, qkv_ref, grad_ref, mixed_ref, den_ref, nb_ref, out_ref):
    const = first_row(FEAT, CUT)
    row = lax.broadcasted_iota(jnp.int32, (16, CUT), 0)

    def step(b, sums):
        cols = pl.ds(pl.multiple_of(b * CUT, CUT), CUT)
        fresh = []
        for h in range(HG):
            base = h * HROWS
            q = qkv_ref[base : base + FEAT, cols].astype(F32)
            rows = slice(h * HEAD_DIM, (h + 1) * HEAD_DIM)
            g = grad_ref[rows, cols].astype(F32)
            inverse = 1.0 / den_ref[0, h : h + 1, cols]
            db = -inverse * jnp.sum(
                g * mixed_ref[rows, cols].astype(F32), axis=0, keepdims=True
            )
            nb = (g * inverse).astype(BF16)
            high = db.astype(BF16).astype(F32)
            tail = jnp.where(row == 0, high, jnp.where(row == 1, db - high, 0.0)).astype(BF16)
            nb_aug = jnp.concatenate([nb, tail], 0)
            nb_ref[h, :, cols] = nb_aug
            fresh.append(sums[h] + dot(nb_aug, phi_rows(q, const), NT))
        return tuple(fresh)

    zero = jnp.zeros((VROWS, FROWS), F32)
    sums = lax.fori_loop(0, blocks, step, (zero,) * HG)
    for h in range(HG):
        out_ref[h] = sums[h]


def backward_kernel(blocks, qkv_ref, nb_ref, saved_ref, init_ref, out_ref, state):
    ones2 = first_row(16, CUT, 2).astype(BF16)
    const = first_row(FEAT, CUT)
    one_low = const.astype(BF16)
    scale = lane_scale()
    mask = causal_mask()
    state[...] = init_ref[...]

    def step(i, carry):
        b = blocks - 1 - i
        cols = pl.ds(pl.multiple_of(b * CUT, CUT), CUT)
        for h in range(HG):
            base = h * HROWS
            q = qkv_ref[base : base + FEAT, cols]
            k = qkv_ref[base + FEAT : base + 2 * FEAT, cols]
            v = qkv_ref[base + 2 * FEAT : base + HROWS, cols]
            qf = q.astype(F32)
            kf = k.astype(F32)
            q4 = q * 0.25
            nb = nb_ref[h, :, cols]
            v_aug = jnp.concatenate([v, ones2], 0)
            k_aug = jnp.concatenate([k, one_low], 0)
            q_aug = jnp.concatenate([q4, one_low], 0)
            u = dot(k_aug, q_aug, TN)
            weight = jnp.where(mask, u * u + 1.0, 0.0).astype(BF16)
            wb = dot(v_aug, nb, TN)
            sb = jnp.where(mask, wb * u, 0.0).astype(BF16)
            q_feat_back = dot(saved_ref[h, b], twice(nb), TN)
            dq = 0.25 * dot(k, sb, NN) + 0.5 * phi_pull(q_feat_back, qf)
            low = split_pair(state[h] * scale)
            k_feat_back = dot(low, twice(v_aug), TN)
            later = dot(low, phi_rows(kf, const), NN)
            dk = dot(q4, sb, NT) + phi_pull(k_feat_back, kf)
            dv = 0.5 * dot(nb[:HEAD_DIM], weight, NT) + (
                later[:HEAD_DIM] + later[VROWS : VROWS + HEAD_DIM]
            )
            out_ref[base : base + FEAT, cols] = dq.astype(BF16)
            out_ref[base + FEAT : base + 2 * FEAT, cols] = dk.astype(BF16)
            out_ref[base + 2 * FEAT : base + HROWS, cols] = dv.astype(BF16)
            state[h] += dot(nb, phi_rows(qf, const), NT)
        return carry

    lax.fori_loop(0, blocks, step, 0)


def cost(flops):
    return pl.CostEstimate(flops=int(flops), bytes_accessed=0, transcendentals=0)


def head_spec(rows, cols):
    return pl.BlockSpec((HG * rows, cols), lambda g: (g, 0))


def lead_spec(*tail):
    return pl.BlockSpec((HG,) + tail, lambda g: (g,) + (0,) * len(tail))


VMEM_LIMIT = pltpu.CompilerParams(vmem_limit_bytes=56 * 1024 * 1024)


def local_state(qkv):
    cols = qkv.shape[1]
    return pl.pallas_call(
        functools.partial(state_kernel, cols // CUT),
        grid=(HEADS // HG,),
        in_specs=[head_spec(HROWS, cols)],
        out_specs=lead_spec(VROWS, FROWS),
        out_shape=jax.ShapeDtypeStruct((HEADS, VROWS, FROWS), F32),
        compiler_params=VMEM_LIMIT,
        cost_estimate=cost(10e9 * cols / 2048),
        name="key_state",
    )(qkv)


def attention_forward(qkv, init):
    cols = qkv.shape[1]
    blocks = cols // CUT
    return pl.pallas_call(
        functools.partial(forward_kernel, blocks),
        grid=(HEADS // HG,),
        in_specs=[head_spec(HROWS, cols), lead_spec(VROWS, FROWS)],
        out_specs=[
            head_spec(HEAD_DIM, cols),
            pl.BlockSpec((1, HG, cols), lambda g: (g, 0, 0)),
            lead_spec(blocks, PAIR, FROWS),
        ],
        out_shape=[
            jax.ShapeDtypeStruct((HEADS * HEAD_DIM, cols), BF16),
            jax.ShapeDtypeStruct((HEADS // HG, HG, cols), F32),
            jax.ShapeDtypeStruct((HEADS, blocks, PAIR, FROWS), BF16),
        ],
        scratch_shapes=[pltpu.VMEM((HG, VROWS, FROWS), F32)],
        compiler_params=VMEM_LIMIT,
        cost_estimate=cost(36e9 * cols / 2048),
        name="attend",
    )(qkv, init)


def local_back_state(qkv, grad, mixed, den):
    cols = qkv.shape[1]
    return pl.pallas_call(
        functools.partial(back_state_kernel, cols // CUT),
        grid=(HEADS // HG,),
        in_specs=[
            head_spec(HROWS, cols),
            head_spec(HEAD_DIM, cols),
            head_spec(HEAD_DIM, cols),
            pl.BlockSpec((1, HG, cols), lambda g: (g, 0, 0)),
        ],
        out_specs=[lead_spec(VROWS, cols), lead_spec(VROWS, FROWS)],
        out_shape=[
            jax.ShapeDtypeStruct((HEADS, VROWS, cols), BF16),
            jax.ShapeDtypeStruct((HEADS, VROWS, FROWS), F32),
        ],
        compiler_params=VMEM_LIMIT,
        cost_estimate=cost(13e9 * cols / 2048),
        name="query_state",
    )(qkv, grad, mixed, den)


def attention_backward(qkv, nb, saved, init):
    cols = qkv.shape[1]
    blocks = cols // CUT
    return pl.pallas_call(
        functools.partial(backward_kernel, blocks),
        grid=(HEADS // HG,),
        in_specs=[
            head_spec(HROWS, cols),
            lead_spec(VROWS, cols),
            lead_spec(blocks, PAIR, FROWS),
            lead_spec(VROWS, FROWS),
        ],
        out_specs=head_spec(HROWS, cols),
        out_shape=jax.ShapeDtypeStruct((HEADS * HROWS, cols), BF16),
        scratch_shapes=[pltpu.VMEM((HG, VROWS, FROWS), F32)],
        compiler_params=VMEM_LIMIT,
        cost_estimate=cost(53e9 * cols / 2048),
        name="attend_back",
    )(qkv, nb, saved, init)


def project_kernel(tokens_ref, weight_ref, gain_ref, qkv_ref, normed_ref, flipped_ref):
    width = tokens_ref.shape[2]
    lead = HEADS * FEAT

    @pl.when(pl.program_id(0) == 0)
    def _():
        for c in range(HEADS * HROWS // 128):
            piece = weight_ref[:, 128 * (c + 1) : 128 * (c + 2)].T
            start = 128 * c
            if start < 2 * lead:
                each, first = FEAT, FEAT * (start // lead)
                head = (start % lead) // FEAT
            else:
                each, first = HEAD_DIM, 2 * FEAT
                head = (start - 2 * lead) // HEAD_DIM
            for j in range(128 // each):
                at = (head + j) * HROWS + first
                flipped_ref[at : at + each, :] = piece[j * each : (j + 1) * each]

    tokens = tokens_ref[0].astype(F32)
    scale = lax.rsqrt(jnp.sum(tokens * tokens, -1, keepdims=True) * (1.0 / width) + epsilon)
    normed = (tokens * scale * gain_ref[...]).astype(BF16)
    normed_ref[...] = normed
    qkv_ref[...] = dot(flipped_ref[...], normed, NT).astype(BF16)


def project(tokens, early, gain):
    rows, width = tokens.shape[1:]
    tile = min(rows, 512)
    return pl.pallas_call(
        project_kernel,
        grid=(rows // tile,),
        in_specs=[
            pl.BlockSpec((1, tile, width), lambda i: (0, i, 0)),
            pl.BlockSpec(early.shape, lambda i: (0, 0), pipeline_mode=pl.Buffered(1)),
            pl.BlockSpec((1, width), lambda i: (0, 0)),
        ],
        out_specs=[
            pl.BlockSpec((HEADS * HROWS, tile), lambda i: (0, i)),
            pl.BlockSpec((tile, width), lambda i: (i, 0)),
            pl.BlockSpec((HEADS * HROWS, width), lambda i: (0, 0)),
        ],
        out_shape=[
            jax.ShapeDtypeStruct((HEADS * HROWS, rows), BF16),
            jax.ShapeDtypeStruct((rows, width), BF16),
            jax.ShapeDtypeStruct((HEADS * HROWS, width), BF16),
        ],
        compiler_params=VMEM_LIMIT,
        cost_estimate=cost(2 * HEADS * HROWS * rows * width),
        name="project",
    )(tokens, early, gain)


def input_kernel(back_ref, flipped_ref, tokens_ref, resid_ref, gain_ref, out_ref, sum_ref):
    width = tokens_ref.shape[2]
    tokens = tokens_ref[0].astype(F32)
    scale = lax.rsqrt(jnp.sum(tokens * tokens, -1, keepdims=True) * (1.0 / width) + epsilon)
    unit = tokens * scale
    normed_back = dot(back_ref[...], flipped_ref[...], TN)
    terms = normed_back * unit

    @pl.when(pl.program_id(0) == 0)
    def _():
        sum_ref[...] = jnp.zeros_like(sum_ref)

    sum_ref[...] += jnp.sum(terms, 0, keepdims=True)
    gain = gain_ref[...]
    middle = jnp.sum(terms * gain, -1, keepdims=True) * (1.0 / width)
    out_ref[0] = resid_ref[...] + scale * (normed_back * gain - unit * middle)


def input_gradient(back, flipped, tokens, resid_back, gain):
    rows, width = tokens.shape[1:]
    tile = min(rows, 512)
    return pl.pallas_call(
        input_kernel,
        grid=(rows // tile,),
        in_specs=[
            pl.BlockSpec((HEADS * HROWS, tile), lambda i: (0, i)),
            pl.BlockSpec(flipped.shape, lambda i: (0, 0), pipeline_mode=pl.Buffered(1)),
            pl.BlockSpec((1, tile, width), lambda i: (0, i, 0)),
            pl.BlockSpec((tile, width), lambda i: (i, 0)),
            pl.BlockSpec((1, width), lambda i: (0, 0)),
        ],
        out_specs=[
            pl.BlockSpec((1, tile, width), lambda i: (0, i, 0)),
            pl.BlockSpec((1, width), lambda i: (0, 0)),
        ],
        out_shape=[
            jax.ShapeDtypeStruct((1, rows, width), F32),
            jax.ShapeDtypeStruct((1, width), F32),
        ],
        compiler_params=VMEM_LIMIT,
        cost_estimate=cost(2 * HEADS * HROWS * rows * width),
        name="input_gradient",
    )(back, flipped, tokens, resid_back, gain)


def ffn_kernel(
    padded,
    count_ref,
    tokens_ref,
    target_ref,
    mixed_ref,
    gain_ref,
    late_ref,
    result_ref,
    normed_ref,
    hidden_ref,
    branch_ref,
    both_ref,
    attended_ref,
    resid_back_ref,
    mixed_back_ref,
    gain_sum_ref,
    error_ref,
    w_out,
    w_gate,
    w_up,
    w_down,
    slope,
    active,
    sems,
):
    step = pl.program_id(0)
    tile, width = tokens_ref.shape[1:]
    starts = (0, width, width + padded, width + 2 * padded)
    copies = [
        pltpu.make_async_copy(
            late_ref.at[:, pl.ds(start, held.shape[1])], held, sems.at[k]
        )
        for k, (start, held) in enumerate(zip(starts, (w_out, w_gate, w_up, w_down)))
    ]

    @pl.when(step == 0)
    def _():
        for copy in copies:
            copy.start()
        gain_sum_ref[...] = jnp.zeros_like(gain_sum_ref)
        error_ref[...] = jnp.zeros_like(error_ref)
        copies[0].wait()

    gain = gain_ref[...]
    resid = tokens_ref[0].astype(F32) + dot(mixed_ref[...], w_out[...], TN)
    scale = lax.rsqrt(jnp.sum(resid * resid, -1, keepdims=True) * (1.0 / width) + epsilon)
    unit = resid * scale
    normed = (unit * gain).astype(BF16)
    normed_ref[...] = normed

    @pl.when(step == 0)
    def _():
        copies[1].wait()
        copies[2].wait()

    for c in range(padded // 256):
        cols = slice(c * 256, (c + 1) * 256)
        gate = dot(normed, w_gate[:, cols], NN)
        up = dot(normed, w_up[:, cols], NN)
        sigmoid = jax.nn.sigmoid(gate)
        activated = gate * sigmoid
        hidden_ref[:, cols] = (activated * up).astype(BF16)
        active[:, cols] = activated
        slope[:, cols] = up * sigmoid * (1.0 + gate * (1.0 - sigmoid))

    @pl.when(step == 0)
    def _():
        copies[3].wait()

    full = resid + dot(hidden_ref[...], w_down[...], NT)
    result_ref[0] = full.astype(BF16)
    position = step * tile + lax.broadcasted_iota(jnp.int32, (tile, 1), 0)
    difference = jnp.where(
        position < count_ref[0], full - target_ref[0].astype(F32), 0.0
    )
    error_ref[...] += jnp.sum(difference * difference, 0, keepdims=True)
    branch = difference.astype(BF16)
    branch_ref[...] = branch
    for c in range(padded // 256):
        cols = slice(c * 256, (c + 1) * 256)
        hidden_back = dot(branch, w_down[:, cols], NN).astype(BF16).astype(F32)
        both_ref[:, cols] = (hidden_back * slope[:, cols]).astype(BF16)
        both_ref[:, padded + c * 256 : padded + (c + 1) * 256] = (
            hidden_back * active[:, cols]
        ).astype(BF16)
    ffn_back = dot(both_ref[:, :padded], w_gate[...], NT) + dot(
        both_ref[:, padded:], w_up[...], NT
    )
    terms = ffn_back * unit
    gain_sum_ref[...] += jnp.sum(terms, 0, keepdims=True)
    middle = jnp.sum(terms * gain, -1, keepdims=True) * (1.0 / width)
    resid_back = difference + scale * (ffn_back * gain - unit * middle)
    resid_back_ref[...] = resid_back
    attended = resid_back.astype(BF16)
    attended_ref[...] = attended
    mixed_back_ref[...] = dot(w_out[...], attended, NT).astype(BF16)


def feed_forward(count, tokens, targets, mixed, gain, late, padded):
    rows, width = tokens.shape[1:]
    tile = min(rows, 256)
    token_spec = pl.BlockSpec((1, tile, width), lambda i, c: (0, i, 0))

    def flat(cols):
        return pl.BlockSpec((tile, cols), lambda i, c: (i, 0))

    tall = pl.BlockSpec((width, tile), lambda i, c: (0, i))
    line = pl.BlockSpec((1, width), lambda i, c: (0, 0))
    return pl.pallas_call(
        functools.partial(ffn_kernel, padded),
        grid_spec=pltpu.PrefetchScalarGridSpec(
            num_scalar_prefetch=1,
            grid=(rows // tile,),
            in_specs=[
                token_spec,
                token_spec,
                tall,
                line,
                pl.BlockSpec(memory_space=pl.ANY),
            ],
            out_specs=[
                token_spec,
                flat(width),
                flat(padded),
                flat(width),
                flat(2 * padded),
                flat(width),
                flat(width),
                tall,
                line,
                line,
            ],
            scratch_shapes=[
                pltpu.VMEM((width, width), BF16),
                pltpu.VMEM((width, padded), BF16),
                pltpu.VMEM((width, padded), BF16),
                pltpu.VMEM((width, padded), BF16),
                pltpu.VMEM((tile, padded), F32),
                pltpu.VMEM((tile, padded), F32),
                pltpu.SemaphoreType.DMA((4,)),
            ],
        ),
        out_shape=[
            jax.ShapeDtypeStruct((1, rows, width), BF16),
            jax.ShapeDtypeStruct((rows, width), BF16),
            jax.ShapeDtypeStruct((rows, padded), BF16),
            jax.ShapeDtypeStruct((rows, width), BF16),
            jax.ShapeDtypeStruct((rows, 2 * padded), BF16),
            jax.ShapeDtypeStruct((rows, width), BF16),
            jax.ShapeDtypeStruct((rows, width), F32),
            jax.ShapeDtypeStruct((width, rows), BF16),
            jax.ShapeDtypeStruct((1, width), F32),
            jax.ShapeDtypeStruct((1, width), F32),
        ],
        compiler_params=pltpu.CompilerParams(vmem_limit_bytes=60 * 1024 * 1024),
        cost_estimate=cost(4 * rows * width * (width + 3 * padded)),
        name="feed_forward",
    )(count, tokens, targets, mixed, gain, late)


def weight_grad_kernel(form, pick_ref, left_ref, right_ref, *refs):
    if form == "flip":
        total = dot(right_ref[...], left_ref[...], NN).T
    else:
        total = dot(left_ref[...], right_ref[...], NN if form == "rows" else TN)
    if len(refs) > 1:
        total = total + refs[0][...].astype(F32)
    refs[-1][...] = total.astype(BF16)


def weight_grad(left, right, pick, cols, tile, extra=None, form="plain"):
    depth = right.shape[1] if form == "flip" else right.shape[0]
    rows = left.shape[0] if form == "rows" else left.shape[1]
    step = min(rows, 512)
    each = cols // tile
    if form == "rows":
        left_spec = pl.BlockSpec((step, depth), lambda j, i, p: (i, 0))
    else:
        left_spec = pl.BlockSpec((depth, step), lambda j, i, p: (0, i))
    if form == "flip":
        right_spec = pl.BlockSpec((tile, depth), lambda j, i, p: (p[0] * each + j, 0))
    else:
        right_spec = pl.BlockSpec((depth, tile), lambda j, i, p: (0, p[0] * each + j))
    out_spec = pl.BlockSpec((step, tile), lambda j, i, p: (i, j))
    in_specs = [left_spec, right_spec]
    operands = [left, right]
    if extra is not None:
        in_specs.append(out_spec)
        operands.append(extra)
    return pl.pallas_call(
        functools.partial(weight_grad_kernel, form),
        grid_spec=pltpu.PrefetchScalarGridSpec(
            num_scalar_prefetch=1,
            grid=(each, rows // step),
            in_specs=in_specs,
            out_specs=out_spec,
        ),
        out_shape=jax.ShapeDtypeStruct((rows, cols), BF16),
        compiler_params=VMEM_LIMIT,
        cost_estimate=cost(2 * rows * cols * depth),
        name="weight_grad",
    )(pick, *operands)


def swap_core(array):
    return lax.ppermute(array, "core", [(i, 1 - i) for i in range(2)])


def halves_sum(left, right, core, cols, tile, form="plain"):
    theirs = weight_grad(left, right, jnp.reshape(1 - core, (1,)), cols, tile, None, form)
    arrived = swap_core(theirs)
    return weight_grad(left, right, jnp.reshape(core, (1,)), cols, tile, arrived, form)


def sum_over(pieces, axis, dim):
    parts = lax.axis_size(axis)
    index = lax.axis_index(axis)
    total = lax.dynamic_index_in_dim(pieces, index, dim, keepdims=False).astype(F32)
    for shift in range(1, parts):
        sent = lax.dynamic_index_in_dim(
            pieces, lax.rem(index + shift, parts), dim, keepdims=False
        )
        pairs = [(i, (i + shift) % parts) for i in range(parts)]
        total = total + lax.ppermute(sent, axis, pairs).astype(F32)
    return total.astype(BF16)


def rows_sum(block, seq_first):
    seq_parts, z_parts = lax.axis_size("seq"), lax.axis_size("z")
    cols = block.shape[1]
    pieces = block.reshape(seq_parts, z_parts, 2, -1, cols)
    if seq_first:
        pieces = sum_over(pieces, "seq", 0)
        pieces = sum_over(pieces, "y", 1)
    else:
        pieces = sum_over(pieces, "y", 2)
        pieces = sum_over(pieces, "seq", 0)
    own = sum_over(pieces, "z", 0)
    return own.reshape(2, -1, cols)


def whole_rows(own, core):
    kept = lax.dynamic_index_in_dim(own, core, 0, keepdims=False)
    other = swap_core(lax.dynamic_index_in_dim(own, 1 - core, 0, keepdims=False))
    first = jnp.where(core == 0, kept, other)
    second = jnp.where(core == 0, other, kept)
    return first, second


def shifted_sum(array, parts, sign):
    total = jnp.zeros_like(array)
    for shift in range(1, parts):
        if sign > 0:
            pairs = [(i, i + shift) for i in range(parts - shift)]
        else:
            pairs = [(i + shift, i) for i in range(parts - shift)]
        total = total + lax.ppermute(array, "seq", pairs)
    return total


def body(
    inputs,
    targets,
    valid_count,
    gain_mix,
    w_query,
    w_key,
    w_value,
    w_out,
    gain_ffn,
    w_gate,
    w_up,
    w_down,
):
    everyone = ("seq", "z", "y", "core")
    seq_parts = lax.axis_size("seq")
    devices = lax.axis_size(everyone)
    seq_index = lax.axis_index("seq")
    batch_index = lax.axis_index(("z", "y", "core"))
    core = lax.axis_index("core")
    rows, width = inputs.shape[1:]
    hidden_units = w_gate.shape[1]
    padded = -(-hidden_units // 256) * 256
    owners = jnp.arange(valid_count.shape[0])
    count = jnp.sum(jnp.where(owners == batch_index, valid_count, 0))
    total_valid = jnp.sum(valid_count).astype(F32)
    valid_here = jnp.reshape(count - seq_index * rows, (1,))
    gains = jnp.pad(jnp.stack([gain_mix, gain_ffn], 1), ((0, 0), (0, 126)))
    early = jnp.concatenate([gains, w_query, w_key, w_value], 1)
    early = lax.all_gather(early, everyone, axis=0, tiled=True)
    gain_one = early[:, 0].astype(F32)[None]
    gain_two = early[:, 1].astype(F32)[None]
    fill = ((0, 0), (0, padded - hidden_units))
    late = lax.all_gather(
        jnp.concatenate(
            [w_out, jnp.pad(w_gate, fill), jnp.pad(w_up, fill), jnp.pad(w_down, fill)], 1
        ),
        everyone,
        axis=0,
        tiled=True,
    )
    lead = HEADS * FEAT
    qkv, normed, flipped = project(inputs, early, gain_one)
    state = shifted_sum(local_state(qkv), seq_parts, 1)
    mixed, den, saved = attention_forward(qkv, state)
    (
        result,
        normed_ffn,
        hidden,
        branch_back,
        both_back,
        attended_back,
        resid_back,
        mixed_back,
        gain_two_sum,
        squares,
    ) = feed_forward(valid_here, inputs, targets, mixed, gain_two, late, padded)
    local_error = 0.5 * jnp.sum(squares)
    gate_up_half = halves_sum(normed_ffn, both_back, core, padded, padded // 2)
    down_half = halves_sum(branch_back, hidden, core, padded // 2, padded // 2)
    out_half = halves_sum(mixed, attended_back, core, width // 2, width // 2, "rows")
    mixed_back, gate_up_half, down_half, out_half = lax.optimization_barrier(
        (mixed_back, gate_up_half, down_half, out_half)
    )
    gate_up_own = rows_sum(gate_up_half, True)
    down_out_own = rows_sum(jnp.concatenate([down_half, out_half], 1), False)
    nb, back = local_back_state(qkv, mixed_back, mixed, den)
    later = shifted_sum(back, seq_parts, -1)
    qkv_back = attention_backward(qkv, nb, saved, later)
    qkv_cols = HEADS * HROWS // 2
    qkv_half = halves_sum(normed, qkv_back, core, qkv_cols, qkv_cols, "flip")
    input_back, gain_one_sum = input_gradient(qkv_back, flipped, inputs, resid_back, gain_one)
    high = lax.reduce_precision(local_error, 8, 7)
    middle = lax.reduce_precision(local_error - high, 8, 7)
    low = lax.reduce_precision(local_error - high - middle, 8, 7)
    extra = -(-(2 + 3 * devices) // 128) * 128
    column = lax.broadcasted_iota(jnp.int32, (width, extra), 1)
    place = 2 + 3 * lax.axis_index(everyone)
    side = jnp.where(column == 0, gain_one_sum.T, 0.0)
    side = jnp.where(column == 1, gain_two_sum.T, side)
    side = jnp.where(column == place, high, side)
    side = jnp.where(column == place + 1, middle, side)
    side = jnp.where(column == place + 2, low, side).astype(BF16)
    side = (side.astype(F32) + swap_core(side).astype(F32)).astype(BF16)
    qkv_own = rows_sum(jnp.concatenate([qkv_half, side], 1), True)
    gate_sum, up_sum = whole_rows(gate_up_own, core)
    pair = jnp.concatenate(whole_rows(down_out_own, core), 0).reshape(2, -1, (padded + width) // 2)
    down_sum = jnp.concatenate([pair[0, :, : padded // 2], pair[1, :, : padded // 2]], 1)
    out_sum = jnp.concatenate([pair[0, :, padded // 2 :], pair[1, :, padded // 2 :]], 1)
    first, second = whole_rows(qkv_own, core)
    side_sum = first[:, qkv_cols:].astype(F32)
    loss = 2.0 * jnp.sum(side_sum[0, 2 : 2 + 3 * devices]) / (width * total_valid)
    qkv_sum = jnp.concatenate([first[:, :qkv_cols], second[:, :qkv_cols]], 1).astype(F32)
    own = qkv_sum.shape[0]
    qkv_sum = qkv_sum.reshape(own, HEADS, HROWS)
    return (
        result,
        loss,
        input_back,
        side_sum[:, 0],
        qkv_sum[:, :, :FEAT].reshape(own, lead),
        qkv_sum[:, :, FEAT : 2 * FEAT].reshape(own, lead),
        qkv_sum[:, :, 2 * FEAT :].reshape(own, HEADS * HEAD_DIM),
        out_sum.astype(F32),
        side_sum[:, 1],
        gate_sum[:, :hidden_units].astype(F32),
        up_sum[:, :hidden_units].astype(F32),
        down_sum[:, :hidden_units].astype(F32),
    )


def solution(mesh):
    seq_parts, fsdp_parts = mesh.shape["seq"], mesh.shape["fsdp"]
    fine = jax.sharding.Mesh(
        mesh.devices.reshape(seq_parts, fsdp_parts // 4, 2, 2), ("seq", "z", "y", "core")
    )
    both = P(("seq", "z", "y", "core"))
    rows = P(("seq", "z", "y", "core"), None)
    tokens = P(("z", "y", "core"), "seq", None)
    return jax.shard_map(
        body,
        mesh=fine,
        in_specs=(tokens, tokens, P(), both, rows, rows, rows, rows, both, rows, rows, rows),
        out_specs=(tokens, P(), tokens, both, rows, rows, rows, rows, both, rows, rows, rows),
        check_vma=False,
    )
```

```python
import functools
import math

import jax
import jax.numpy as jnp
import numpy as np
from jax import lax
from jax.experimental import pallas as pl
from jax.experimental.pallas import tpu as pltpu
from jax.sharding import PartitionSpec as P

HEADS = 16
FEAT = 16
HEAD_DIM = 64
HROWS = 2 * FEAT + HEAD_DIM
CUT = 256
GROUPS = 11
FROWS = GROUPS * FEAT
VROWS = HEAD_DIM + 16
PAIR = 2 * VROWS
SENT = HEAD_DIM + 8
HG = 4

epsilon = 1e-05
F32 = jnp.float32
BF16 = jnp.bfloat16
NN = (((1,), (0,)), ((), ()))
NT = (((1,), (1,)), ((), ()))
TN = (((0,), (0,)), ((), ()))


def dot(left, right, dims):
    return lax.dot_general(left, right, dims, preferred_element_type=F32)


def first_row(rows, cols, count=1):
    return (lax.broadcasted_iota(jnp.int32, (rows, cols), 0) < count).astype(F32)


def rolled(u, shift):
    return pltpu.roll(u, (FEAT - shift) % FEAT, 0)


def phi_rows(u, const):
    groups = [u * u]
    for d in range(1, 9):
        groups.append(u * rolled(u, d))
    groups.append(u)
    groups.append(const)
    return jnp.concatenate([g.astype(BF16) for g in groups], 0)


def phi_pull(grad, u):
    total = grad[9 * FEAT : 10 * FEAT] + 2.0 * grad[0:FEAT] * u
    for d in range(1, 9):
        g = grad[d * FEAT : (d + 1) * FEAT]
        total = total + g * rolled(u, d) + rolled(g * u, FEAT - d)
    return total


def lane_scale():
    group = lax.broadcasted_iota(jnp.int32, (1, FROWS), 1) // FEAT
    scale = jnp.where((group == 0) | (group == 8), 1.0 / 32.0, 1.0 / 16.0)
    scale = jnp.where(group == 9, 0.25, scale)
    return jnp.where(group == 10, 1.0, scale)


def causal_mask():
    s = lax.broadcasted_iota(jnp.int32, (CUT, CUT), 0)
    t = lax.broadcasted_iota(jnp.int32, (CUT, CUT), 1)
    return s <= t


def split_pair(wide):
    high = wide.astype(BF16)
    return jnp.concatenate([high, (wide - high.astype(F32)).astype(BF16)], 0)


def twice(rows):
    return jnp.concatenate([rows, rows], 0)


def pack_states(sums, out_ref):
    fill = jnp.zeros((SENT, 2 * 128 - 2 * (FROWS - 128) - 128), F32)
    for i in range(len(sums) // 2):
        a, b = sums[2 * i][:SENT], sums[2 * i + 1][:SENT]
        out_ref[i, 0] = a[:, :128]
        out_ref[i, 1] = b[:, :128]
        out_ref[i, 2] = jnp.concatenate([a[:, 128:], b[:, 128:], fill], 1)


def unpack_states(packed_ref, state):
    side = FROWS - 128
    state[...] = jnp.zeros_like(state)
    for i in range(state.shape[0] // 2):
        for j in range(2):
            state[2 * i + j, :SENT, :128] = packed_ref[i, j]
            state[2 * i + j, :SENT, 128:] = packed_ref[i, 2][:, j * side : (j + 1) * side]


def state_kernel(blocks, qkv_ref, out_ref):
    ones2 = first_row(16, CUT, 2).astype(BF16)
    const = first_row(FEAT, CUT)

    def step(b, sums):
        cols = pl.ds(pl.multiple_of(b * CUT, CUT), CUT)
        fresh = []
        for h in range(HG):
            base = h * HROWS
            k = qkv_ref[base + FEAT : base + 2 * FEAT, cols].astype(F32)
            v = qkv_ref[base + 2 * FEAT : base + HROWS, cols]
            v_aug = jnp.concatenate([v, ones2], 0)
            fresh.append(sums[h] + dot(v_aug, phi_rows(k, const), NT))
        return tuple(fresh)

    zero = jnp.zeros((VROWS, FROWS), F32)
    sums = lax.fori_loop(0, blocks, step, (zero,) * HG)
    pack_states(sums, out_ref)


def forward_kernel(blocks, qkv_ref, init_ref, *refs):
    ones2 = first_row(16, CUT, 2).astype(BF16)
    const = first_row(FEAT, CUT)
    one_low = const.astype(BF16)
    mixed_ref, rest_ref, den_ref, saved_ref, state = refs[-5:]
    scale = 2.0 * lane_scale()
    mask = causal_mask()
    unpack_states(init_ref, state)

    def step(b, carry):
        cols = pl.ds(pl.multiple_of(b * CUT, CUT), CUT)
        for h in range(HG):
            base = h * HROWS
            q = qkv_ref[base : base + FEAT, cols]
            k = qkv_ref[base + FEAT : base + 2 * FEAT, cols]
            v = qkv_ref[base + 2 * FEAT : base + HROWS, cols]
            v_aug = jnp.concatenate([v, ones2], 0)
            k_aug = jnp.concatenate([k, one_low], 0)
            q_aug = jnp.concatenate([q * 0.25, one_low], 0)
            u = dot(k_aug, q_aug, TN)
            weight = jnp.where(mask, u * u + 1.0, 0.0).astype(BF16)
            low = split_pair(state[h] * scale)
            saved_ref[h, b] = low
            earlier = dot(low, phi_rows(q.astype(F32), const), NN)
            numer = dot(v_aug, weight, NN) + (earlier[:VROWS] + earlier[VROWS:])
            den = numer[HEAD_DIM : HEAD_DIM + 1]
            wide = numer[:HEAD_DIM] * (1.0 / den)
            mixed_low = wide.astype(BF16)
            rows = slice(h * HEAD_DIM, (h + 1) * HEAD_DIM)
            mixed_ref[rows, cols] = mixed_low
            rest_ref[rows, cols] = (wide - mixed_low.astype(F32)).astype(BF16)
            den_ref[0, h : h + 1, cols] = 0.5 * den
            state[h] += dot(v_aug, phi_rows(k.astype(F32), const), NT)
        return carry

    lax.fori_loop(0, blocks, step, 0)


def back_state_kernel(
    blocks, qkv_ref, grad_ref, mixed_ref, rest_ref, den_ref, nb_ref, out_ref
):
    const = first_row(FEAT, CUT)
    row = lax.broadcasted_iota(jnp.int32, (16, CUT), 0)

    def step(b, sums):
        cols = pl.ds(pl.multiple_of(b * CUT, CUT), CUT)
        fresh = []
        for h in range(HG):
            base = h * HROWS
            q = qkv_ref[base : base + FEAT, cols].astype(F32)
            rows = slice(h * HEAD_DIM, (h + 1) * HEAD_DIM)
            g = grad_ref[rows, cols].astype(F32)
            inverse = 1.0 / den_ref[0, h : h + 1, cols]
            db = -inverse * jnp.sum(
                g * (mixed_ref[rows, cols].astype(F32) + rest_ref[rows, cols].astype(F32)),
                axis=0,
                keepdims=True,
            )
            nb = (g * inverse).astype(BF16)
            high = db.astype(BF16).astype(F32)
            tail = jnp.where(row == 0, high, jnp.where(row == 1, db - high, 0.0)).astype(BF16)
            nb_aug = jnp.concatenate([nb, tail], 0)
            nb_ref[h, :, cols] = nb_aug
            fresh.append(sums[h] + dot(nb_aug, phi_rows(q, const), NT))
        return tuple(fresh)

    zero = jnp.zeros((VROWS, FROWS), F32)
    sums = lax.fori_loop(0, blocks, step, (zero,) * HG)
    pack_states(sums, out_ref)


def backward_kernel(blocks, qkv_ref, nb_ref, saved_ref, init_ref, *refs):
    ones2 = first_row(16, CUT, 2).astype(BF16)
    const = first_row(FEAT, CUT)
    one_low = const.astype(BF16)
    out_ref, state = refs[-2:]
    scale = lane_scale()
    mask = causal_mask()
    unpack_states(init_ref, state)

    def step(i, carry):
        b = blocks - 1 - i
        cols = pl.ds(pl.multiple_of(b * CUT, CUT), CUT)
        for h in range(HG):
            base = h * HROWS
            q = qkv_ref[base : base + FEAT, cols]
            k = qkv_ref[base + FEAT : base + 2 * FEAT, cols]
            v = qkv_ref[base + 2 * FEAT : base + HROWS, cols]
            qf = q.astype(F32)
            kf = k.astype(F32)
            q4 = q * 0.25
            nb = nb_ref[h, :, cols]
            v_aug = jnp.concatenate([v, ones2], 0)
            k_aug = jnp.concatenate([k, one_low], 0)
            q_aug = jnp.concatenate([q4, one_low], 0)
            u = dot(k_aug, q_aug, TN)
            weight = jnp.where(mask, u * u + 1.0, 0.0).astype(BF16)
            wb = dot(v_aug, nb, TN)
            sb = jnp.where(mask, wb * u, 0.0).astype(BF16)
            q_feat_back = dot(saved_ref[h, b], twice(nb), TN)
            dq = 0.25 * dot(k, sb, NN) + 0.5 * phi_pull(q_feat_back, qf)
            low = split_pair(state[h] * scale)
            k_feat_back = dot(low, twice(v_aug), TN)
            later = dot(low, phi_rows(kf, const), NN)
            dk = dot(q4, sb, NT) + phi_pull(k_feat_back, kf)
            dv = 0.5 * dot(nb[:HEAD_DIM], weight, NT) + (
                later[:HEAD_DIM] + later[VROWS : VROWS + HEAD_DIM]
            )
            out_ref[base : base + FEAT, cols] = dq.astype(BF16)
            out_ref[base + FEAT : base + 2 * FEAT, cols] = dk.astype(BF16)
            out_ref[base + 2 * FEAT : base + HROWS, cols] = dv.astype(BF16)
            state[h] += dot(nb, phi_rows(qf, const), NT)
        return carry

    lax.fori_loop(0, blocks, step, 0)


def cost(flops):
    return pl.CostEstimate(flops=int(flops), bytes_accessed=0, transcendentals=0)


def head_spec(rows, cols):
    return pl.BlockSpec((HG * rows, cols), lambda g: (g, 0))


def lead_spec(*tail):
    return pl.BlockSpec((HG,) + tail, lambda g: (g,) + (0,) * len(tail))


VMEM_LIMIT = pltpu.CompilerParams(vmem_limit_bytes=56 * 1024 * 1024)


def packed_shape(heads):
    return jax.ShapeDtypeStruct((heads // 2, 3, SENT, 128), F32)


def packed_spec():
    return pl.BlockSpec((HG // 2, 3, SENT, 128), lambda g: (g, 0, 0, 0))


def local_state(qkv, start, count):
    cols = qkv.shape[1]
    first = start // HG
    return pl.pallas_call(
        functools.partial(state_kernel, cols // CUT),
        grid=(count // HG,),
        in_specs=[pl.BlockSpec((HG * HROWS, cols), lambda g: (first + g, 0))],
        out_specs=packed_spec(),
        out_shape=packed_shape(count),
        compiler_params=VMEM_LIMIT,
        cost_estimate=cost(11e9 * cols / 2048 * count / HEADS),
        name="key_state",
    )(qkv)


def attention_forward(qkv, init, start, count, filled=()):
    cols = qkv.shape[1]
    blocks = cols // CUT
    first = start // HG

    def head_rows(rows):
        return pl.BlockSpec((HG * rows, cols), lambda g: (first + g, 0))

    def lead(*tail):
        return pl.BlockSpec((HG,) + tail, lambda g: (first + g,) + (0,) * len(tail))

    return pl.pallas_call(
        functools.partial(forward_kernel, blocks),
        grid=(count // HG,),
        in_specs=[head_rows(HROWS), packed_spec()]
        + [pl.BlockSpec(memory_space=pl.ANY)] * len(filled),
        out_specs=[
            head_rows(HEAD_DIM),
            head_rows(HEAD_DIM),
            pl.BlockSpec((1, HG, cols), lambda g: (first + g, 0, 0)),
            lead(blocks, PAIR, FROWS),
        ],
        out_shape=[
            jax.ShapeDtypeStruct((HEADS * HEAD_DIM, cols), BF16),
            jax.ShapeDtypeStruct((HEADS * HEAD_DIM, cols), BF16),
            jax.ShapeDtypeStruct((HEADS // HG, HG, cols), F32),
            jax.ShapeDtypeStruct((HEADS, blocks, PAIR, FROWS), BF16),
        ],
        scratch_shapes=[pltpu.VMEM((HG, VROWS, FROWS), F32)],
        compiler_params=VMEM_LIMIT,
        cost_estimate=cost(36e9 * cols / 2048 * count / HEADS),
        input_output_aliases={2 + i: i for i in range(len(filled))},
        name="attend",
    )(qkv, init, *filled)


def local_back_state(qkv, grad, mixed, rest, den):
    cols = qkv.shape[1]
    return pl.pallas_call(
        functools.partial(back_state_kernel, cols // CUT),
        grid=(HEADS // HG,),
        in_specs=[
            head_spec(HROWS, cols),
            head_spec(HEAD_DIM, cols),
            head_spec(HEAD_DIM, cols),
            head_spec(HEAD_DIM, cols),
            pl.BlockSpec((1, HG, cols), lambda g: (g, 0, 0)),
        ],
        out_specs=[lead_spec(VROWS, cols), packed_spec()],
        out_shape=[
            jax.ShapeDtypeStruct((HEADS, VROWS, cols), BF16),
            packed_shape(HEADS),
        ],
        compiler_params=VMEM_LIMIT,
        cost_estimate=cost(13e9 * cols / 2048),
        name="query_state",
    )(qkv, grad, mixed, rest, den)


def attention_backward(qkv, nb, saved, init, start, count, filled=None):
    cols = qkv.shape[1]
    blocks = cols // CUT
    first = start // HG

    def head_rows(rows):
        return pl.BlockSpec((HG * rows, cols), lambda g: (first + g, 0))

    def lead(*tail):
        return pl.BlockSpec((HG,) + tail, lambda g: (first + g,) + (0,) * len(tail))

    operands = [qkv, nb, saved, init]
    in_specs = [
        head_rows(HROWS),
        lead(VROWS, cols),
        lead(blocks, PAIR, FROWS),
        pl.BlockSpec((HG // 2, 3, SENT, 128), lambda g: (first + g, 0, 0, 0)),
    ]
    aliases = {}
    if filled is not None:
        operands.append(filled)
        in_specs.append(pl.BlockSpec(memory_space=pl.ANY))
        aliases = {4: 0}
    return pl.pallas_call(
        functools.partial(backward_kernel, blocks),
        grid=(count // HG,),
        in_specs=in_specs,
        out_specs=head_rows(HROWS),
        out_shape=jax.ShapeDtypeStruct((HEADS * HROWS, cols), BF16),
        scratch_shapes=[pltpu.VMEM((HG, VROWS, FROWS), F32)],
        compiler_params=VMEM_LIMIT,
        cost_estimate=cost(53e9 * cols / 2048 * count / HEADS),
        input_output_aliases=aliases,
        name="attend_back",
    )(*operands)


MESH = pl.DeviceIdType.MESH


def gather_kernel(shape, split, shard_ref, out_ref, local_sem, *sems):
    seq_parts, z_parts = shape
    s, z = lax.axis_index("seq"), lax.axis_index("z")
    y, c = lax.axis_index("y"), lax.axis_index("core")
    cols = shard_ref.shape[1]
    left, right = pl.ds(0, split), pl.ds(split, cols - split)
    every = slice(None)

    def peer(ds=0, dz=0, dy=0, dc=0):
        return (
            lax.rem(s + ds, seq_parts),
            lax.rem(z + dz, z_parts),
            lax.rem(y + dy, 2),
            lax.rem(c + dc, 2),
        )

    def send(kind, slot, src, dst, device):
        return pltpu.make_async_remote_copy(
            src_ref=src,
            dst_ref=dst,
            send_sem=sems[2 * kind].at[slot],
            recv_sem=sems[2 * kind + 1].at[slot],
            device_id=device,
            device_id_type=MESH,
        )

    barrier = pltpu.get_barrier_semaphore()
    peers = [peer(ds=j) for j in range(1, seq_parts)]
    peers += [peer(dz=k) for k in range(1, z_parts)]
    peers += [peer(dy=1), peer(dc=1)]
    for device in peers:
        pl.semaphore_signal(barrier, inc=1, device_id=device, device_id_type=MESH)
    own = pltpu.make_async_copy(shard_ref, out_ref.at[s, z, y, c], local_sem)
    own.start()
    pl.semaphore_wait(barrier, len(peers))

    order = [0] + sorted(range(1, z_parts), key=lambda k: min(k, z_parts - k))
    slab = {k: lax.rem(z + z_parts - k, z_parts) for k in order}
    along = {
        k: send(0, k, shard_ref, out_ref.at[s, z, y, c], peer(dz=k)) for k in order[1:]
    }
    for k in order[1:]:
        along[k].start()
    own.wait()
    first_y, first_x = {}, {}
    for k in order:
        if k:
            along[k].wait_recv()
        at = out_ref.at[s, slab[k], y, c, :, left]
        first_y[k] = send(1, k, at, at, peer(dy=1))
        first_y[k].start()
        at = out_ref.at[s, slab[k], y, c, :, right]
        first_x[k] = [
            send(2, k * seq_parts + j, at, at, peer(ds=j)) for j in range(1, seq_parts)
        ]
        for copy in first_x[k]:
            copy.start()
    then_x, then_y, across = {}, {}, {}
    for k in order:
        first_y[k].wait_recv()
        at = out_ref.at[s, slab[k], :, c, :, left]
        then_x[k] = [
            send(3, k * seq_parts + j, at, at, peer(ds=j)) for j in range(1, seq_parts)
        ]
        for copy in then_x[k]:
            copy.start()
        for copy in first_x[k]:
            copy.wait_recv()
        at = out_ref.at[:, slab[k], y, c, :, right]
        then_y[k] = send(4, k, at, at, peer(dy=1))
        then_y[k].start()
    for k in order:
        for copy in then_x[k]:
            copy.wait_recv()
        then_y[k].wait_recv()
        at = out_ref.at[:, slab[k], :, c]
        across[k] = send(5, k, at, at, peer(dc=1))
        across[k].start()
    for k in order:
        across[k].wait_recv()
    for k in order:
        if k:
            along[k].wait_send()
        first_y[k].wait_send()
        then_y[k].wait_send()
        across[k].wait_send()
        for copy in first_x[k] + then_x[k]:
            copy.wait_send()


def gather_rows(shard):
    own, cols = shard.shape
    seq_parts, z_parts = lax.axis_size("seq"), lax.axis_size("z")
    split = cols // 256 * 128
    counts = (z_parts, z_parts, z_parts * seq_parts, z_parts * seq_parts, z_parts, z_parts)
    out = pl.pallas_call(
        functools.partial(gather_kernel, (seq_parts, z_parts), split),
        in_specs=[pl.BlockSpec(memory_space=pl.ANY)],
        out_specs=pl.BlockSpec(memory_space=pl.ANY),
        out_shape=jax.ShapeDtypeStruct((seq_parts, z_parts, 2, 2, own, cols), BF16),
        scratch_shapes=[pltpu.SemaphoreType.DMA]
        + [pltpu.SemaphoreType.DMA((n,)) for n in counts for _ in range(2)],
        compiler_params=pltpu.CompilerParams(collective_id=0, has_side_effects=True),
        cost_estimate=cost(25e9),
        name="gather_rows",
    )(shard)
    return out.reshape(-1, cols)


def project_kernel(tokens_ref, weight_ref, gain_ref, qkv_ref, normed_ref, flipped_ref):
    width = tokens_ref.shape[2]
    lead = HEADS * FEAT

    @pl.when(pl.program_id(0) == 0)
    def _():
        for c in range(HEADS * HROWS // 128):
            piece = weight_ref[:, 128 * (c + 1) : 128 * (c + 2)].T
            start = 128 * c
            if start < 2 * lead:
                each, first = FEAT, FEAT * (start // lead)
                head = (start % lead) // FEAT
            else:
                each, first = HEAD_DIM, 2 * FEAT
                head = (start - 2 * lead) // HEAD_DIM
            for j in range(128 // each):
                at = (head + j) * HROWS + first
                flipped_ref[at : at + each, :] = piece[j * each : (j + 1) * each]

    tokens = tokens_ref[0].astype(F32)
    scale = lax.rsqrt(jnp.sum(tokens * tokens, -1, keepdims=True) * (1.0 / width) + epsilon)
    normed = (tokens * scale * gain_ref[...]).astype(BF16)
    normed_ref[...] = normed.T
    qkv_ref[...] = dot(flipped_ref[...], normed, NT).astype(BF16)


def project(tokens, early, gain):
    rows, width = tokens.shape[1:]
    tile = min(rows, 512)
    return pl.pallas_call(
        project_kernel,
        grid=(rows // tile,),
        in_specs=[
            pl.BlockSpec((1, tile, width), lambda i: (0, i, 0)),
            pl.BlockSpec(
                (width, 128 + HEADS * HROWS), lambda i: (0, 0), pipeline_mode=pl.Buffered(1)
            ),
            pl.BlockSpec((1, width), lambda i: (0, 0)),
        ],
        out_specs=[
            pl.BlockSpec((HEADS * HROWS, tile), lambda i: (0, i)),
            pl.BlockSpec((width, tile), lambda i: (0, i)),
            pl.BlockSpec((HEADS * HROWS, width), lambda i: (0, 0)),
        ],
        out_shape=[
            jax.ShapeDtypeStruct((HEADS * HROWS, rows), BF16),
            jax.ShapeDtypeStruct((width, rows), BF16),
            jax.ShapeDtypeStruct((HEADS * HROWS, width), BF16),
        ],
        compiler_params=VMEM_LIMIT,
        cost_estimate=cost(2 * HEADS * HROWS * rows * width),
        name="project",
    )(tokens, early, gain)


def input_kernel(back_ref, flipped_ref, tokens_ref, resid_ref, gain_ref, *refs):
    out_ref = refs[-1]
    width = tokens_ref.shape[2]
    tokens = tokens_ref[0].astype(F32)
    scale = lax.rsqrt(jnp.sum(tokens * tokens, -1, keepdims=True) * (1.0 / width) + epsilon)
    unit = tokens * scale
    normed_back = dot(back_ref[...], flipped_ref[...], TN)
    scaled = normed_back * gain_ref[...]
    middle = jnp.sum(scaled * unit, -1, keepdims=True) * (1.0 / width)
    out_ref[0] = resid_ref[...] + scale * (scaled - unit * middle)


def input_gradient(back, flipped, tokens, resid_back, gain, first, count, filled=None):
    rows, width = tokens.shape[1:]
    tile = min(rows // 2, 512)
    first, count = first // tile, count // tile
    operands = [back, flipped, tokens, resid_back, gain]
    in_specs = [
        pl.BlockSpec((HEADS * HROWS, tile), lambda i: (0, first + i)),
        pl.BlockSpec(flipped.shape, lambda i: (0, 0), pipeline_mode=pl.Buffered(1)),
        pl.BlockSpec((1, tile, width), lambda i: (0, first + i, 0)),
        pl.BlockSpec((tile, width), lambda i: (first + i, 0)),
        pl.BlockSpec((1, width), lambda i: (0, 0)),
    ]
    aliases = {}
    if filled is not None:
        operands.append(filled)
        in_specs.append(pl.BlockSpec(memory_space=pl.ANY))
        aliases = {5: 0}
    return pl.pallas_call(
        input_kernel,
        grid=(count,),
        in_specs=in_specs,
        out_specs=pl.BlockSpec((1, tile, width), lambda i: (0, first + i, 0)),
        out_shape=jax.ShapeDtypeStruct((1, rows, width), F32),
        compiler_params=VMEM_LIMIT,
        cost_estimate=cost(4 * HEADS * HROWS * count * tile * width),
        input_output_aliases=aliases,
        name="input_gradient",
    )(*operands)


def ffn_kernel(
    padded,
    count_ref,
    tokens_ref,
    target_ref,
    mixed_ref,
    gain_ref,
    early_ref,
    late_ref,
    result_ref,
    normed_ref,
    hidden_ref,
    branch_ref,
    both_ref,
    attended_ref,
    resid_back_ref,
    mixed_back_ref,
    error_ref,
    w_out,
    w_gate,
    w_up,
    w_down,
    slope,
    active,
    sems,
):
    step = pl.program_id(0)
    tile, width = tokens_ref.shape[1:]
    copies = [
        pltpu.make_async_copy(
            early_ref.at[:, pl.ds(128 + HEADS * HROWS, width)], w_out, sems.at[0]
        )
    ] + [
        pltpu.make_async_copy(late_ref.at[:, pl.ds(k * padded, padded)], held, sems.at[k + 1])
        for k, held in enumerate((w_gate, w_up, w_down))
    ]

    @pl.when(step == 0)
    def _():
        for copy in copies:
            copy.start()
        error_ref[...] = jnp.zeros_like(error_ref)
        copies[0].wait()

    gain = gain_ref[...]
    resid = tokens_ref[0].astype(F32) + dot(mixed_ref[...], w_out[...], TN)
    scale = lax.rsqrt(jnp.sum(resid * resid, -1, keepdims=True) * (1.0 / width) + epsilon)
    unit = resid * scale
    normed = (unit * gain).astype(BF16)
    normed_ref[...] = normed.T

    @pl.when(step == 0)
    def _():
        copies[1].wait()
        copies[2].wait()

    for c in range(padded // 256):
        cols = slice(c * 256, (c + 1) * 256)
        gate = dot(normed, w_gate[:, cols], NN)
        up = dot(normed, w_up[:, cols], NN)
        sigmoid = jax.nn.sigmoid(gate)
        activated = gate * sigmoid
        hidden_ref[:, cols] = (activated * up).astype(BF16)
        active[:, cols] = activated
        slope[:, cols] = up * sigmoid * (1.0 + gate * (1.0 - sigmoid))

    @pl.when(step == 0)
    def _():
        copies[3].wait()

    full = resid + dot(hidden_ref[...], w_down[...], NT)
    result_ref[0] = full.astype(BF16)
    position = step * tile + lax.broadcasted_iota(jnp.int32, (tile, 1), 0)
    difference = jnp.where(
        position < count_ref[0], full - target_ref[0].astype(F32), 0.0
    )
    error_ref[...] += jnp.sum(difference * difference, 0, keepdims=True)
    branch = difference.astype(BF16)
    branch_ref[...] = branch.T
    for c in range(padded // 256):
        cols = slice(c * 256, (c + 1) * 256)
        hidden_back = dot(branch, w_down[:, cols], NN).astype(BF16).astype(F32)
        both_ref[:, cols] = (hidden_back * slope[:, cols]).astype(BF16)
        both_ref[:, padded + c * 256 : padded + (c + 1) * 256] = (
            hidden_back * active[:, cols]
        ).astype(BF16)
    ffn_back = dot(both_ref[:, :padded], w_gate[...], NT) + dot(
        both_ref[:, padded:], w_up[...], NT
    )
    scaled = ffn_back * gain
    middle = jnp.sum(scaled * unit, -1, keepdims=True) * (1.0 / width)
    resid_back = difference + scale * (scaled - unit * middle)
    resid_back_ref[...] = resid_back
    attended = resid_back.astype(BF16)
    attended_ref[...] = attended
    mixed_back_ref[...] = dot(w_out[...], attended, NT).astype(BF16)


def feed_forward(count, tokens, targets, mixed, gain, early, late, padded):
    rows, width = tokens.shape[1:]
    tile = min(rows, 256)
    token_spec = pl.BlockSpec((1, tile, width), lambda i, c: (0, i, 0))

    def flat(cols):
        return pl.BlockSpec((tile, cols), lambda i, c: (i, 0))

    tall = pl.BlockSpec((width, tile), lambda i, c: (0, i))
    line = pl.BlockSpec((1, width), lambda i, c: (0, 0))
    return pl.pallas_call(
        functools.partial(ffn_kernel, padded),
        grid_spec=pltpu.PrefetchScalarGridSpec(
            num_scalar_prefetch=1,
            grid=(rows // tile,),
            in_specs=[
                token_spec,
                token_spec,
                tall,
                line,
                pl.BlockSpec(memory_space=pl.ANY),
                pl.BlockSpec(memory_space=pl.ANY),
            ],
            out_specs=[
                token_spec,
                tall,
                flat(padded),
                tall,
                flat(2 * padded),
                flat(width),
                flat(width),
                tall,
                line,
            ],
            scratch_shapes=[
                pltpu.VMEM((width, width), BF16),
                pltpu.VMEM((width, padded), BF16),
                pltpu.VMEM((width, padded), BF16),
                pltpu.VMEM((width, padded), BF16),
                pltpu.VMEM((tile, padded), F32),
                pltpu.VMEM((tile, padded), F32),
                pltpu.SemaphoreType.DMA((4,)),
            ],
        ),
        out_shape=[
            jax.ShapeDtypeStruct((1, rows, width), BF16),
            jax.ShapeDtypeStruct((width, rows), BF16),
            jax.ShapeDtypeStruct((rows, padded), BF16),
            jax.ShapeDtypeStruct((width, rows), BF16),
            jax.ShapeDtypeStruct((rows, 2 * padded), BF16),
            jax.ShapeDtypeStruct((rows, width), BF16),
            jax.ShapeDtypeStruct((rows, width), F32),
            jax.ShapeDtypeStruct((width, rows), BF16),
            jax.ShapeDtypeStruct((1, width), F32),
        ],
        compiler_params=pltpu.CompilerParams(vmem_limit_bytes=60 * 1024 * 1024),
        cost_estimate=cost(4 * rows * width * (width + 3 * padded)),
        name="feed_forward",
    )(count, tokens, targets, mixed, gain, early, late)


def weight_grad_kernel(form, pick_ref, left_ref, right_ref, *refs):
    total = dot(left_ref[...], right_ref[...], form)
    if len(refs) > 1:
        total = total + refs[0][...].astype(F32)
    refs[-1][...] = total.astype(BF16)


def weight_grad(left, right, pick, cols, tile, extra=None, form=NN):
    rows, depth = left.shape
    step = min(rows, 512)
    each = cols // tile
    left_spec = pl.BlockSpec((step, depth), lambda j, i, p: (i, 0))
    if form is NT:
        right_spec = pl.BlockSpec((tile, depth), lambda j, i, p: (p[0] * each + j, 0))
    else:
        right_spec = pl.BlockSpec((depth, tile), lambda j, i, p: (0, p[0] * each + j))
    out_spec = pl.BlockSpec((step, tile), lambda j, i, p: (i, j))
    in_specs = [left_spec, right_spec]
    operands = [left, right]
    if extra is not None:
        in_specs.append(out_spec)
        operands.append(extra)
    return pl.pallas_call(
        functools.partial(weight_grad_kernel, form),
        grid_spec=pltpu.PrefetchScalarGridSpec(
            num_scalar_prefetch=1,
            grid=(each, rows // step),
            in_specs=in_specs,
            out_specs=out_spec,
        ),
        out_shape=jax.ShapeDtypeStruct((rows, cols), BF16),
        compiler_params=VMEM_LIMIT,
        cost_estimate=cost(2 * rows * cols * depth),
        name="weight_grad",
    )(pick, *operands)


def swap_core(array):
    return lax.ppermute(array, "core", [(i, 1 - i) for i in range(2)])


def sum_over(pieces, axis, dim):
    parts = lax.axis_size(axis)
    index = lax.axis_index(axis)
    total = lax.dynamic_index_in_dim(pieces, index, dim, keepdims=False).astype(F32)
    for shift in range(1, parts):
        sent = lax.dynamic_index_in_dim(
            pieces, lax.rem(index + shift, parts), dim, keepdims=False
        )
        pairs = [(i, (i + shift) % parts) for i in range(parts)]
        total = total + lax.ppermute(sent, axis, pairs).astype(F32)
    return total.astype(BF16)


def as_pieces(block):
    seq_parts, z_parts = lax.axis_size("seq"), lax.axis_size("z")
    return block.reshape(seq_parts, z_parts, 2, -1, block.shape[1])


def whole_rows(own, core):
    kept = lax.dynamic_index_in_dim(own, core, 0, keepdims=False)
    other = swap_core(lax.dynamic_index_in_dim(own, 1 - core, 0, keepdims=False))
    first = jnp.where(core == 0, kept, other)
    second = jnp.where(core == 0, other, kept)
    return first, second


def shifted_sum(array, parts, sign):
    total = jnp.zeros_like(array)
    for shift in range(1, parts):
        if sign > 0:
            pairs = [(i, i + shift) for i in range(parts - shift)]
        else:
            pairs = [(i + shift, i) for i in range(parts - shift)]
        total = total + lax.ppermute(array, "seq", pairs)
    return total


def body(
    inputs,
    targets,
    valid_count,
    gain_mix,
    w_query,
    w_key,
    w_value,
    w_out,
    gain_ffn,
    w_gate,
    w_up,
    w_down,
):
    everyone = ("seq", "z", "y", "core")
    seq_parts = lax.axis_size("seq")
    devices = lax.axis_size(everyone)
    seq_index = lax.axis_index("seq")
    batch_index = lax.axis_index(("z", "y", "core"))
    core = lax.axis_index("core")
    rows, width = inputs.shape[1:]
    hidden_units = w_gate.shape[1]
    padded = -(-hidden_units // 256) * 256
    owners = jnp.arange(valid_count.shape[0])
    count = jnp.sum(jnp.where(owners == batch_index, valid_count, 0))
    total_valid = jnp.sum(valid_count).astype(F32)
    valid_here = jnp.reshape(count - seq_index * rows, (1,))
    gains = jnp.pad(jnp.stack([gain_mix, gain_ffn], 1), ((0, 0), (0, 126)))
    early = gather_rows(jnp.concatenate([gains, w_query, w_key, w_value, w_out], 1))
    fill = ((0, 0), (0, padded - hidden_units))
    late = jnp.concatenate(
        [jnp.pad(w_gate, fill), jnp.pad(w_up, fill), jnp.pad(w_down, fill)], 1
    )
    late = lax.all_gather(late, everyone, axis=0, tiled=True)
    gain_one = early[:, 0].astype(F32)[None]
    gain_two = early[:, 1].astype(F32)[None]
    lead = HEADS * FEAT
    qkv, normed, flipped = project(inputs, early, gain_one)
    tie = lax.optimization_barrier
    upper = HEADS // 2
    lower_state = local_state(qkv, 0, upper)
    lower_init = shifted_sum(lower_state, seq_parts, 1)
    qkv, lower_state = tie((qkv, lower_state))
    upper_init = shifted_sum(local_state(qkv, upper, upper), seq_parts, 1)
    filled = attention_forward(qkv, lower_init, 0, upper)
    mixed, rest, den, saved = attention_forward(qkv, upper_init, upper, upper, filled)
    (
        result,
        normed_ffn,
        hidden,
        branch_back,
        both_back,
        attended_back,
        resid_back,
        mixed_back,
        squares,
    ) = feed_forward(valid_here, inputs, targets, mixed, gain_two, early, late, padded)
    local_error = 0.5 * jnp.sum(squares)
    mine, others = jnp.reshape(core, (1,)), jnp.reshape(1 - core, (1,))
    half, out_half, qkv_cols = padded // 2, width // 2, HEADS * HROWS // 2
    part = HEADS // 4

    high = lax.reduce_precision(local_error, 8, 7)
    middle = lax.reduce_precision(local_error - high, 8, 7)
    low = lax.reduce_precision(local_error - high - middle, 8, 7)
    column = lax.broadcasted_iota(jnp.int32, (width, -(-3 * devices // 128) * 128), 1)
    place = 3 * lax.axis_index(everyone)
    side = jnp.where(column == place, high, 0.0)
    side = jnp.where(column == place + 1, middle, side)
    side = jnp.where(column == place + 2, low, side).astype(BF16)
    side = (side.astype(F32) + swap_core(side).astype(F32)).astype(BF16)

    nb, back = local_back_state(qkv, mixed_back, mixed, rest, den)
    later = shifted_sum(back, seq_parts, -1)
    normed_ffn, nb = tie((normed_ffn, nb))
    gate_up_sent = weight_grad(normed_ffn, both_back, others, padded, half)
    gate_up_come = swap_core(gate_up_sent)
    branch_back, gate_up_sent = tie((branch_back, gate_up_sent))
    down_sent = weight_grad(branch_back, hidden, others, half, half)
    normed_ffn, down_sent = tie((normed_ffn, down_sent))
    gate_up = weight_grad(normed_ffn, both_back, mine, padded, half, gate_up_come)
    down_come = swap_core(down_sent)
    a_one = sum_over(as_pieces(gate_up[:, :half]), "seq", 0)
    a_two = sum_over(as_pieces(gate_up[:, half:]), "y", 2)
    mixed, gate_up = tie((mixed, gate_up))
    out_sent = weight_grad(mixed, attended_back, others, out_half, out_half)
    out_come = swap_core(out_sent)
    branch_back, out_sent = tie((branch_back, out_sent))
    down = weight_grad(branch_back, hidden, mine, half, half, down_come)
    mixed, down = tie((mixed, down))
    outer = weight_grad(mixed, attended_back, mine, out_half, out_half, out_come)
    cut = 128 * ((half + out_half + side.shape[1]) // 256)
    b_one = down[:, :cut]
    b_two = jnp.concatenate([down[:, cut:], outer, side], 1)
    nb, b_one, b_two = tie((nb, b_one, b_two))
    qkv_back = attention_backward(qkv, nb, saved, later, 0, part)
    nb, a_one, a_two, b_one, b_two = tie((nb, a_one, a_two, b_one, b_two))
    a_one = sum_over(a_one, "y", 1)
    a_two = sum_over(a_two, "seq", 0)
    b_one = sum_over(as_pieces(b_one), "seq", 0)
    b_two = sum_over(as_pieces(b_two), "y", 2)
    qkv_back = attention_backward(qkv, nb, saved, later, part, part, qkv_back)
    qkv_back = attention_backward(qkv, nb, saved, later, 2 * part, part, qkv_back)
    nb, a_one, a_two, b_one, b_two = tie((nb, a_one, a_two, b_one, b_two))
    a_own = sum_over(jnp.concatenate([a_one, a_two], 2), "z", 0)
    b_one = sum_over(b_one, "y", 1)
    b_two = sum_over(b_two, "seq", 0)
    qkv_back = attention_backward(qkv, nb, saved, later, 3 * part, part, qkv_back)
    qkv_back, b_one, b_two = tie((qkv_back, b_one, b_two))
    b_own = sum_over(jnp.concatenate([b_one, b_two], 2), "z", 0)
    qkv_sent = weight_grad(normed, qkv_back, others, qkv_cols, qkv_cols, None, NT)
    qkv_come = swap_core(qkv_sent)
    c_all = weight_grad(normed, qkv_back, mine, qkv_cols, qkv_cols, qkv_come, NT)
    c_cut = 128 * (qkv_cols // 256)
    c_one = sum_over(as_pieces(c_all[:, :c_cut]), "seq", 0)
    c_two = sum_over(as_pieces(c_all[:, c_cut:]), "y", 2)
    qkv_back, c_all = tie((qkv_back, c_all))
    split = rows // 2
    early_part = input_gradient(qkv_back, flipped, inputs, resid_back, gain_one, 0, split)
    early_part, c_one, c_two = tie((early_part, c_one, c_two))
    c_one = sum_over(c_one, "y", 1)
    c_two = sum_over(c_two, "seq", 0)
    input_back = input_gradient(
        qkv_back, flipped, inputs, resid_back, gain_one, split, split, early_part
    )
    input_back, c_one, c_two = tie((input_back, c_one, c_two))
    c_own = sum_over(jnp.concatenate([c_one, c_two], 2), "z", 0)
    own = w_query.shape[0]
    gate_sum, up_sum = whole_rows(a_own.reshape(2, own, -1), core)
    pair = whole_rows(b_own.reshape(2, own, -1), core)
    down_sum = jnp.concatenate([pair[0][:, :half], pair[1][:, :half]], 1)
    out_sum = jnp.concatenate(
        [pair[0][:, half : half + out_half], pair[1][:, half : half + out_half]], 1
    )
    errors = pair[0][0, half + out_half : half + out_half + 3 * devices].astype(F32)
    loss = 2.0 * jnp.sum(errors) / (width * total_valid)
    first, second = whole_rows(c_own.reshape(2, own, -1), core)
    qkv_sum = jnp.concatenate([first, second], 1).astype(F32).reshape(own, HEADS, HROWS)
    grad_query = qkv_sum[:, :, :FEAT].reshape(own, lead)
    grad_key = qkv_sum[:, :, FEAT : 2 * FEAT].reshape(own, lead)
    grad_value = qkv_sum[:, :, 2 * FEAT :].reshape(own, HEADS * HEAD_DIM)
    grad_gate = gate_sum[:, :hidden_units].astype(F32)
    grad_up = up_sum[:, :hidden_units].astype(F32)

    def gain_grad(gain, *pairs):
        total = sum(jnp.sum(w.astype(F32) * grad, 1) for w, grad in pairs)
        return total / gain.astype(F32)

    return (
        result,
        loss,
        input_back,
        gain_grad(gain_mix, (w_query, grad_query), (w_key, grad_key), (w_value, grad_value)),
        grad_query,
        grad_key,
        grad_value,
        out_sum.astype(F32),
        gain_grad(gain_ffn, (w_gate, grad_gate), (w_up, grad_up)),
        grad_gate,
        grad_up,
        down_sum[:, :hidden_units].astype(F32),
    )


def solution(mesh):
    seq_parts, fsdp_parts = mesh.shape["seq"], mesh.shape["fsdp"]
    fine = jax.sharding.Mesh(
        mesh.devices.reshape(seq_parts, fsdp_parts // 4, 2, 2), ("seq", "z", "y", "core")
    )
    both = P(("seq", "z", "y", "core"))
    rows = P(("seq", "z", "y", "core"), None)
    tokens = P(("z", "y", "core"), "seq", None)
    return jax.shard_map(
        body,
        mesh=fine,
        in_specs=(tokens, tokens, P(), both, rows, rows, rows, rows, both, rows, rows, rows),
        out_specs=(tokens, P(), tokens, both, rows, rows, rows, rows, both, rows, rows, rows),
        check_vma=False,
    )
```

```python
import functools
import math

import jax
import jax.numpy as jnp
import numpy as np
from jax import lax
from jax.experimental import pallas as pl
from jax.experimental.pallas import tpu as pltpu
from jax.sharding import PartitionSpec as P

HEADS = 16
FEAT = 16
HEAD_DIM = 64
HROWS = 2 * FEAT + HEAD_DIM
CUT = 256
GROUPS = 11
FROWS = GROUPS * FEAT
VROWS = HEAD_DIM + 16
PAIR = 2 * VROWS
SENT = HEAD_DIM + 8
HG = 4
FIRST_BACK, SECOND_BACK = 4, 2

epsilon = 1e-05
F32 = jnp.float32
BF16 = jnp.bfloat16
NN = (((1,), (0,)), ((), ()))
NT = (((1,), (1,)), ((), ()))
TN = (((0,), (0,)), ((), ()))


def dot(left, right, dims):
    return lax.dot_general(left, right, dims, preferred_element_type=F32)


def first_row(rows, cols, count=1):
    return (lax.broadcasted_iota(jnp.int32, (rows, cols), 0) < count).astype(F32)


def rolled(u, shift):
    return pltpu.roll(u, (FEAT - shift) % FEAT, 0)


def phi_rows(u, const):
    groups = [u * u]
    for d in range(1, 9):
        groups.append(u * rolled(u, d))
    groups.append(u)
    groups.append(const)
    return jnp.concatenate([g.astype(BF16) for g in groups], 0)


def phi_pull(grad, u):
    total = grad[9 * FEAT : 10 * FEAT] + 2.0 * grad[0:FEAT] * u
    for d in range(1, 9):
        g = grad[d * FEAT : (d + 1) * FEAT]
        total = total + g * rolled(u, d) + rolled(g * u, FEAT - d)
    return total


def lane_scale():
    group = lax.broadcasted_iota(jnp.int32, (1, FROWS), 1) // FEAT
    scale = jnp.where((group == 0) | (group == 8), 1.0 / 32.0, 1.0 / 16.0)
    scale = jnp.where(group == 9, 0.25, scale)
    return jnp.where(group == 10, 1.0, scale)


def causal_mask():
    s = lax.broadcasted_iota(jnp.int32, (CUT, CUT), 0)
    t = lax.broadcasted_iota(jnp.int32, (CUT, CUT), 1)
    return s <= t


def split_pair(wide):
    high = wide.astype(BF16)
    return jnp.concatenate([high, (wide - high.astype(F32)).astype(BF16)], 0)


def twice(rows):
    return jnp.concatenate([rows, rows], 0)


def pack_states(sums, out_ref):
    fill = jnp.zeros((SENT, 2 * 128 - 2 * (FROWS - 128) - 128), F32)
    for i in range(len(sums) // 2):
        a, b = sums[2 * i][:SENT], sums[2 * i + 1][:SENT]
        out_ref[i, 0] = a[:, :128]
        out_ref[i, 1] = b[:, :128]
        out_ref[i, 2] = jnp.concatenate([a[:, 128:], b[:, 128:], fill], 1)


def unpack_states(packed_ref, state):
    side = FROWS - 128
    state[...] = jnp.zeros_like(state)
    for i in range(state.shape[0] // 2):
        for j in range(2):
            state[2 * i + j, :SENT, :128] = packed_ref[i, j]
            state[2 * i + j, :SENT, 128:] = packed_ref[i, 2][:, j * side : (j + 1) * side]


def state_kernel(blocks, qkv_ref, out_ref):
    ones2 = first_row(16, CUT, 2).astype(BF16)
    const = first_row(FEAT, CUT)

    def step(b, sums):
        cols = pl.ds(pl.multiple_of(b * CUT, CUT), CUT)
        fresh = []
        for h in range(HG):
            base = h * HROWS
            k = qkv_ref[base + FEAT : base + 2 * FEAT, cols].astype(F32)
            v = qkv_ref[base + 2 * FEAT : base + HROWS, cols]
            v_aug = jnp.concatenate([v, ones2], 0)
            fresh.append(sums[h] + dot(v_aug, phi_rows(k, const), NT))
        return tuple(fresh)

    zero = jnp.zeros((VROWS, FROWS), F32)
    sums = lax.fori_loop(0, blocks, step, (zero,) * HG)
    pack_states(sums, out_ref)


def forward_kernel(blocks, qkv_ref, init_ref, *refs):
    ones2 = first_row(16, CUT, 2).astype(BF16)
    const = first_row(FEAT, CUT)
    one_low = const.astype(BF16)
    mixed_ref, den_ref, saved_ref, state = refs[-4:]
    scale = 2.0 * lane_scale()
    mask = causal_mask()
    unpack_states(init_ref, state)

    def step(b, carry):
        cols = pl.ds(pl.multiple_of(b * CUT, CUT), CUT)
        for h in range(HG):
            base = h * HROWS
            q = qkv_ref[base : base + FEAT, cols]
            k = qkv_ref[base + FEAT : base + 2 * FEAT, cols]
            v = qkv_ref[base + 2 * FEAT : base + HROWS, cols]
            v_aug = jnp.concatenate([v, ones2], 0)
            k_aug = jnp.concatenate([k, one_low], 0)
            q_aug = jnp.concatenate([q * 0.25, one_low], 0)
            u = dot(k_aug, q_aug, TN)
            weight = jnp.where(mask, u * u + 1.0, 0.0).astype(BF16)
            low = split_pair(state[h] * scale)
            saved_ref[h, b] = low
            earlier = dot(low, phi_rows(q.astype(F32), const), NN)
            numer = dot(v_aug, weight, NN) + (earlier[:VROWS] + earlier[VROWS:])
            den = numer[HEAD_DIM : HEAD_DIM + 1]
            rows = slice(h * HEAD_DIM, (h + 1) * HEAD_DIM)
            mixed_ref[rows, cols] = (numer[:HEAD_DIM] * (1.0 / den)).astype(BF16)
            den_ref[0, h : h + 1, cols] = 0.5 * den
            state[h] += dot(v_aug, phi_rows(k.astype(F32), const), NT)
        return carry

    lax.fori_loop(0, blocks, step, 0)


def back_state_kernel(blocks, qkv_ref, grad_ref, mixed_ref, den_ref, nb_ref, out_ref):
    const = first_row(FEAT, CUT)
    row = lax.broadcasted_iota(jnp.int32, (16, CUT), 0)

    def step(b, sums):
        cols = pl.ds(pl.multiple_of(b * CUT, CUT), CUT)
        fresh = []
        for h in range(HG):
            base = h * HROWS
            q = qkv_ref[base : base + FEAT, cols].astype(F32)
            rows = slice(h * HEAD_DIM, (h + 1) * HEAD_DIM)
            g = grad_ref[rows, cols].astype(F32)
            inverse = 1.0 / den_ref[0, h : h + 1, cols]
            db = -inverse * jnp.sum(
                g * mixed_ref[rows, cols].astype(F32), axis=0, keepdims=True
            )
            nb = (g * inverse).astype(BF16)
            high = db.astype(BF16).astype(F32)
            tail = jnp.where(row == 0, high, jnp.where(row == 1, db - high, 0.0)).astype(BF16)
            nb_aug = jnp.concatenate([nb, tail], 0)
            nb_ref[h, :, cols] = nb_aug
            fresh.append(sums[h] + dot(nb_aug, phi_rows(q, const), NT))
        return tuple(fresh)

    zero = jnp.zeros((VROWS, FROWS), F32)
    sums = lax.fori_loop(0, blocks, step, (zero,) * HG)
    pack_states(sums, out_ref)


def backward_kernel(
    sizes,
    blocks,
    qkv_ref,
    nb_ref,
    saved_ref,
    init_ref,
    one_ref,
    two_ref,
    block_ref,
    out_ref,
    pair_out,
    part_out,
    state,
    *refs,
):
    ones2 = first_row(16, CUT, 2).astype(BF16)
    const = first_row(FEAT, CUT)
    one_low = const.astype(BF16)
    scale = lane_scale()
    mask = causal_mask()
    halves = pl.num_programs(1)
    at = pl.program_id(0) * halves + pl.program_id(1)
    last = pl.num_programs(0) * halves - 1
    each = blocks // halves
    by_seq, by_z, by_y, by_core = neighbours(sizes)
    count = 6 + 8
    first = RowSums(sizes, (one_ref, two_ref), refs[:count], pair_out, summed=True)
    refs = refs[count:]
    second = RowSums(sizes, block_ref, refs[:6] + (part_out,) + refs[6:])

    @pl.when(at == 0)
    def _():
        greet(by_seq + by_z + [by_y, by_core])
        first.second()
        second.start()

    @pl.when(pl.program_id(1) == 0)
    def _():
        unpack_states(init_ref, state)

    def step(i, carry):
        b = blocks - 1 - (pl.program_id(1) * each + i)
        cols = pl.ds(pl.multiple_of(b * CUT, CUT), CUT)
        for h in range(HG):
            base = h * HROWS
            q = qkv_ref[base : base + FEAT, cols]
            k = qkv_ref[base + FEAT : base + 2 * FEAT, cols]
            v = qkv_ref[base + 2 * FEAT : base + HROWS, cols]
            qf = q.astype(F32)
            kf = k.astype(F32)
            q4 = q * 0.25
            nb = nb_ref[h, :, cols]
            v_aug = jnp.concatenate([v, ones2], 0)
            k_aug = jnp.concatenate([k, one_low], 0)
            q_aug = jnp.concatenate([q4, one_low], 0)
            u = dot(k_aug, q_aug, TN)
            weight = jnp.where(mask, u * u + 1.0, 0.0).astype(BF16)
            wb = dot(v_aug, nb, TN)
            sb = jnp.where(mask, wb * u, 0.0).astype(BF16)
            q_feat_back = dot(saved_ref[h, b], twice(nb), TN)
            dq = 0.25 * dot(k, sb, NN) + 0.5 * phi_pull(q_feat_back, qf)
            low = split_pair(state[h] * scale)
            k_feat_back = dot(low, twice(v_aug), TN)
            later = dot(low, phi_rows(kf, const), NN)
            dk = dot(q4, sb, NT) + phi_pull(k_feat_back, kf)
            dv = 0.5 * dot(nb[:HEAD_DIM], weight, NT) + (
                later[:HEAD_DIM] + later[VROWS : VROWS + HEAD_DIM]
            )
            out_ref[base : base + FEAT, cols] = dq.astype(BF16)
            out_ref[base + FEAT : base + 2 * FEAT, cols] = dk.astype(BF16)
            out_ref[base + 2 * FEAT : base + HROWS, cols] = dv.astype(BF16)
            state[h] += dot(nb, phi_rows(qf, const), NT)
        return carry

    lax.fori_loop(0, each, step, 0)

    @pl.when(at == last - FIRST_BACK)
    def _():
        first.third()

    @pl.when(at == last - SECOND_BACK)
    def _():
        second.second()

    @pl.when(at == last)
    def _():
        second.third()
        first.fourth()
        second.finish()
        first.finish()


def cost(flops):
    return pl.CostEstimate(flops=int(flops * 0.02), bytes_accessed=0, transcendentals=0)


def head_spec(rows, cols):
    return pl.BlockSpec((HG * rows, cols), lambda g: (g, 0))


def lead_spec(*tail):
    return pl.BlockSpec((HG,) + tail, lambda g: (g,) + (0,) * len(tail))


VMEM_LIMIT = pltpu.CompilerParams(vmem_limit_bytes=56 * 1024 * 1024)


def packed_shape(heads):
    return jax.ShapeDtypeStruct((heads // 2, 3, SENT, 128), F32)


def packed_spec():
    return pl.BlockSpec((HG // 2, 3, SENT, 128), lambda g: (g, 0, 0, 0))


def local_state(qkv, start, count):
    cols = qkv.shape[1]
    first = start // HG
    return pl.pallas_call(
        functools.partial(state_kernel, cols // CUT),
        grid=(count // HG,),
        in_specs=[pl.BlockSpec((HG * HROWS, cols), lambda g: (first + g, 0))],
        out_specs=packed_spec(),
        out_shape=packed_shape(count),
        compiler_params=VMEM_LIMIT,
        cost_estimate=cost(11e9 * cols / 2048 * count / HEADS),
        name="key_state",
    )(qkv)


def attention_forward(qkv, init, start, count, filled=()):
    cols = qkv.shape[1]
    blocks = cols // CUT
    first = start // HG

    def head_rows(rows):
        return pl.BlockSpec((HG * rows, cols), lambda g: (first + g, 0))

    def lead(*tail):
        return pl.BlockSpec((HG,) + tail, lambda g: (first + g,) + (0,) * len(tail))

    return pl.pallas_call(
        functools.partial(forward_kernel, blocks),
        grid=(count // HG,),
        in_specs=[head_rows(HROWS), packed_spec()]
        + [pl.BlockSpec(memory_space=pl.ANY)] * len(filled),
        out_specs=[
            head_rows(HEAD_DIM),
            pl.BlockSpec((1, HG, cols), lambda g: (first + g, 0, 0)),
            lead(blocks, PAIR, FROWS),
        ],
        out_shape=[
            jax.ShapeDtypeStruct((HEADS * HEAD_DIM, cols), BF16),
            jax.ShapeDtypeStruct((HEADS // HG, HG, cols), F32),
            jax.ShapeDtypeStruct((HEADS, blocks, PAIR, FROWS), BF16),
        ],
        scratch_shapes=[pltpu.VMEM((HG, VROWS, FROWS), F32)],
        compiler_params=VMEM_LIMIT,
        cost_estimate=cost(36e9 * cols / 2048 * count / HEADS),
        input_output_aliases={2 + i: i for i in range(len(filled))},
        name="attend",
    )(qkv, init, *filled)


def local_back_state(qkv, grad, mixed, den):
    cols = qkv.shape[1]
    return pl.pallas_call(
        functools.partial(back_state_kernel, cols // CUT),
        grid=(HEADS // HG,),
        in_specs=[
            head_spec(HROWS, cols),
            head_spec(HEAD_DIM, cols),
            head_spec(HEAD_DIM, cols),
            pl.BlockSpec((1, HG, cols), lambda g: (g, 0, 0)),
        ],
        out_specs=[lead_spec(VROWS, cols), packed_spec()],
        out_shape=[
            jax.ShapeDtypeStruct((HEADS, VROWS, cols), BF16),
            packed_shape(HEADS),
        ],
        compiler_params=VMEM_LIMIT,
        cost_estimate=cost(13e9 * cols / 2048),
        name="query_state",
    )(qkv, grad, mixed, den)


def attention_backward(qkv, nb, saved, init, one, two, block, own):
    cols = qkv.shape[1]
    blocks = cols // CUT
    sizes = lax.axis_size("seq"), lax.axis_size("z")
    width = block.shape[-1]
    cut = 128 * (width // 256)
    wide = one.shape[-1] + two.shape[-1]
    first_buffers, first_sems = row_sum_scratch(
        sizes, own, one.shape[-1], two.shape[-1], summed=True
    )
    second_buffers, second_sems = row_sum_scratch(
        sizes, own, cut, width - cut, ends=False, keep=False
    )

    def head_rows(rows):
        return pl.BlockSpec((HG * rows, cols), lambda g, p: (g, 0))

    def lead(*tail):
        return pl.BlockSpec((HG,) + tail, lambda g, p: (g,) + (0,) * len(tail))

    here = pl.BlockSpec(memory_space=pltpu.VMEM)
    return pl.pallas_call(
        functools.partial(backward_kernel, sizes, blocks),
        grid=(HEADS // HG, 2),
        in_specs=[
            head_rows(HROWS),
            lead(VROWS, cols),
            lead(blocks, PAIR, FROWS),
            pl.BlockSpec((HG // 2, 3, SENT, 128), lambda g, p: (g, 0, 0, 0)),
            here,
            here,
            here,
        ],
        out_specs=[head_rows(HROWS), here, here],
        out_shape=[
            jax.ShapeDtypeStruct((HEADS * HROWS, cols), BF16),
            jax.ShapeDtypeStruct((2, own, wide), BF16),
            jax.ShapeDtypeStruct((sizes[1], 2, own, width), BF16),
        ],
        scratch_shapes=[pltpu.VMEM((HG, VROWS, FROWS), F32)]
        + first_buffers
        + first_sems
        + second_buffers
        + second_sems,
        compiler_params=pltpu.CompilerParams(
            collective_id=2, has_side_effects=True, vmem_limit_bytes=58 * 1024 * 1024
        ),
        cost_estimate=cost(53e9 * cols / 2048),
        name="attend_back",
    )(qkv, nb, saved, init, one, two, block.reshape(sizes + (2, 2, own, width)))


MESH = pl.DeviceIdType.MESH


def gather_kernel(shape, split, shard_ref, out_ref, local_sem, *sems):
    seq_parts, z_parts = shape
    s, z = lax.axis_index("seq"), lax.axis_index("z")
    y, c = lax.axis_index("y"), lax.axis_index("core")
    cols = shard_ref.shape[1]
    left, right = pl.ds(0, split), pl.ds(split, cols - split)
    every = slice(None)

    def peer(ds=0, dz=0, dy=0, dc=0):
        return (
            lax.rem(s + ds, seq_parts),
            lax.rem(z + dz, z_parts),
            lax.rem(y + dy, 2),
            lax.rem(c + dc, 2),
        )

    def send(kind, slot, src, dst, device):
        return pltpu.make_async_remote_copy(
            src_ref=src,
            dst_ref=dst,
            send_sem=sems[2 * kind].at[slot],
            recv_sem=sems[2 * kind + 1].at[slot],
            device_id=device,
            device_id_type=MESH,
        )

    barrier = pltpu.get_barrier_semaphore()
    peers = [peer(ds=j) for j in range(1, seq_parts)]
    peers += [peer(dz=k) for k in range(1, z_parts)]
    peers += [peer(dy=1), peer(dc=1)]
    for device in peers:
        pl.semaphore_signal(barrier, inc=1, device_id=device, device_id_type=MESH)
    own = pltpu.make_async_copy(shard_ref, out_ref.at[s, z, y, c], local_sem)
    own.start()
    pl.semaphore_wait(barrier, len(peers))

    order = [0] + sorted(range(1, z_parts), key=lambda k: min(k, z_parts - k))
    slab = {k: lax.rem(z + z_parts - k, z_parts) for k in order}
    along = {
        k: send(0, k, shard_ref, out_ref.at[s, z, y, c], peer(dz=k)) for k in order[1:]
    }
    for k in order[1:]:
        along[k].start()
    own.wait()
    first_y, first_x = {}, {}
    for k in order:
        if k:
            along[k].wait_recv()
        at = out_ref.at[s, slab[k], y, c, :, left]
        first_y[k] = send(1, k, at, at, peer(dy=1))
        first_y[k].start()
        at = out_ref.at[s, slab[k], y, c, :, right]
        first_x[k] = [
            send(2, k * seq_parts + j, at, at, peer(ds=j)) for j in range(1, seq_parts)
        ]
        for copy in first_x[k]:
            copy.start()
    then_x, then_y, across = {}, {}, {}
    for k in order:
        first_y[k].wait_recv()
        at = out_ref.at[s, slab[k], :, c, :, left]
        then_x[k] = [
            send(3, k * seq_parts + j, at, at, peer(ds=j)) for j in range(1, seq_parts)
        ]
        for copy in then_x[k]:
            copy.start()
        for copy in first_x[k]:
            copy.wait_recv()
        at = out_ref.at[:, slab[k], y, c, :, right]
        then_y[k] = send(4, k, at, at, peer(dy=1))
        then_y[k].start()
    for k in order:
        for copy in then_x[k]:
            copy.wait_recv()
        then_y[k].wait_recv()
        at = out_ref.at[:, slab[k], :, c]
        across[k] = send(5, k, at, at, peer(dc=1))
        across[k].start()
    for k in order:
        across[k].wait_recv()
    for k in order:
        if k:
            along[k].wait_send()
        first_y[k].wait_send()
        then_y[k].wait_send()
        across[k].wait_send()
        for copy in first_x[k] + then_x[k]:
            copy.wait_send()


def gather_rows(shard):
    own, cols = shard.shape
    seq_parts, z_parts = lax.axis_size("seq"), lax.axis_size("z")
    split = cols // 256 * 128
    counts = (z_parts, z_parts, z_parts * seq_parts, z_parts * seq_parts, z_parts, z_parts)
    out = pl.pallas_call(
        functools.partial(gather_kernel, (seq_parts, z_parts), split),
        in_specs=[pl.BlockSpec(memory_space=pl.ANY)],
        out_specs=pl.BlockSpec(memory_space=pl.ANY),
        out_shape=jax.ShapeDtypeStruct((seq_parts, z_parts, 2, 2, own, cols), BF16),
        scratch_shapes=[pltpu.SemaphoreType.DMA]
        + [pltpu.SemaphoreType.DMA((n,)) for n in counts for _ in range(2)],
        compiler_params=pltpu.CompilerParams(collective_id=0, has_side_effects=True),
        cost_estimate=cost(25e9),
        name="gather_rows",
    )(shard)
    return out.reshape(-1, cols)


def project_kernel(tokens_ref, weight_ref, qkv_ref, normed_ref, flipped_ref, gain_ref):
    width = tokens_ref.shape[2]
    lead = HEADS * FEAT

    @pl.when(pl.program_id(0) == 0)
    def _():
        gain_ref[...] = weight_ref[:, :128].astype(F32).T[:8]
        for c in range(HEADS * HROWS // 128):
            piece = weight_ref[:, 128 * (c + 1) : 128 * (c + 2)].T
            start = 128 * c
            if start < 2 * lead:
                each, first = FEAT, FEAT * (start // lead)
                head = (start % lead) // FEAT
            else:
                each, first = HEAD_DIM, 2 * FEAT
                head = (start - 2 * lead) // HEAD_DIM
            for j in range(128 // each):
                at = (head + j) * HROWS + first
                flipped_ref[at : at + each, :] = piece[j * each : (j + 1) * each]

    tokens = tokens_ref[0].astype(F32)
    scale = lax.rsqrt(jnp.sum(tokens * tokens, -1, keepdims=True) * (1.0 / width) + epsilon)
    normed = (tokens * scale * gain_ref[0:1]).astype(BF16)
    normed_ref[...] = normed.T
    qkv_ref[...] = dot(flipped_ref[...], normed, NT).astype(BF16)


def project(tokens, early):
    rows, width = tokens.shape[1:]
    tile = min(rows, 512)
    return pl.pallas_call(
        project_kernel,
        grid=(rows // tile,),
        in_specs=[
            pl.BlockSpec((1, tile, width), lambda i: (0, i, 0)),
            pl.BlockSpec(
                (width, 128 + HEADS * HROWS), lambda i: (0, 0), pipeline_mode=pl.Buffered(1)
            ),
        ],
        out_specs=[
            pl.BlockSpec((HEADS * HROWS, tile), lambda i: (0, i)),
            pl.BlockSpec((width, tile), lambda i: (0, i)),
            pl.BlockSpec((HEADS * HROWS, width), lambda i: (0, 0)),
            pl.BlockSpec((8, width), lambda i: (0, 0)),
        ],
        out_shape=[
            jax.ShapeDtypeStruct((HEADS * HROWS, rows), BF16),
            jax.ShapeDtypeStruct((width, rows), BF16),
            jax.ShapeDtypeStruct((HEADS * HROWS, width), BF16),
            jax.ShapeDtypeStruct((8, width), F32),
        ],
        compiler_params=VMEM_LIMIT,
        cost_estimate=cost(2 * HEADS * HROWS * rows * width),
        name="project",
    )(tokens, early)


def remote(src, dst, sems, slot, device):
    return pltpu.make_async_remote_copy(
        src_ref=src,
        dst_ref=dst,
        send_sem=sems[0].at[slot],
        recv_sem=sems[1].at[slot],
        device_id=device,
        device_id_type=MESH,
    )


def positions():
    return tuple(lax.axis_index(name) for name in ("seq", "z", "y", "core"))


def neighbours(sizes):
    seq_parts, z_parts = sizes
    s, z, y, c = positions()
    by_seq = [(lax.rem(s + j, seq_parts), z, y, c) for j in range(1, seq_parts)]
    by_z = [(s, lax.rem(z + k, z_parts), y, c) for k in range(1, z_parts)]
    return by_seq, by_z, (s, z, 1 - y, c), (s, z, y, 1 - c)


def greet(devices):
    barrier = pltpu.get_barrier_semaphore()
    for device in devices:
        pl.semaphore_signal(barrier, inc=1, device_id=device, device_id_type=MESH)
    pl.semaphore_wait(barrier, len(devices))


class RowSums:
    def __init__(self, sizes, source, refs, out_ref=None, summed=False):
        seq_parts, z_parts = self.sizes = sizes
        s, z, y, c = self.place = positions()
        by_seq, by_z, by_y, by_core = neighbours(sizes)
        self.source, self.summed, self.out_ref = source, summed, out_ref
        refs = list(refs)
        if summed:
            self.x_sum, self.y_sum = source
        else:
            self.x_in, self.x_sum, self.y_in, self.y_sum = refs[:4]
            del refs[:4]
        self.then_y_in, self.then_x_in, self.row_sum = refs[:3]
        del refs[:3]
        self.cut = self.x_sum.shape[-1]
        rest = self.y_sum.shape[-1]
        if out_ref is not None:
            self.z_in, self.own_sum, self.swapped = refs[:3]
            del refs[:3]
        pairs = [refs[2 * i : 2 * i + 2] for i in range(len(refs) // 2)]
        others = range(1, seq_parts)
        self.first = []
        if not summed:
            left, right = pl.ds(0, self.cut), pl.ds(self.cut, rest)
            self.first_x = [
                remote(
                    source.at[lax.rem(s + j, seq_parts), :, :, :, :, left],
                    self.x_in.at[j - 1],
                    pairs[2],
                    j - 1,
                    by_seq[j - 1],
                )
                for j in others
            ]
            self.first_y = remote(
                source.at[:, :, 1 - y, :, :, right], self.y_in, pairs[3], 0, by_y
            )
            self.first = self.first_x + [self.first_y]
        self.then_y = remote(self.x_sum.at[:, 1 - y], self.then_y_in, pairs[0], 0, by_y)
        self.then_x = [
            remote(
                self.y_sum.at[lax.rem(s + j, seq_parts)],
                self.then_x_in.at[j - 1],
                pairs[1],
                j - 1,
                by_seq[j - 1],
            )
            for j in others
        ]
        if out_ref is not None:
            self.along = along_z(sizes, self.row_sum, self.z_in, pairs[-2])
            self.across = remote(self.own_sum.at[1 - c], self.swapped, pairs[-1], 0, by_core)

    def start(self):
        for copy in self.first:
            copy.start()

    def second(self):
        s, z, y, c = self.place
        if not self.summed:
            for copy in self.first_x:
                copy.wait_recv()
            total = self.source[s, :, :, :, :, : self.cut].astype(F32)
            for j in range(self.sizes[0] - 1):
                total = total + self.x_in[j].astype(F32)
            self.x_sum[...] = total.astype(BF16)
        self.then_y.start()
        if not self.summed:
            self.first_y.wait_recv()
            total = self.source[:, :, y, :, :, self.cut :].astype(F32)
            self.y_sum[...] = (total + self.y_in[...].astype(F32)).astype(BF16)
        for copy in self.then_x:
            copy.start()

    def third(self):
        s, z, y, c = self.place
        self.then_y.wait_recv()
        total = self.x_sum[:, y].astype(F32) + self.then_y_in[...].astype(F32)
        self.row_sum[:, :, :, : self.cut] = total.astype(BF16)
        for copy in self.then_x:
            copy.wait_recv()
        total = self.y_sum[s].astype(F32)
        for j in range(self.sizes[0] - 1):
            total = total + self.then_x_in[j].astype(F32)
        self.row_sum[:, :, :, self.cut :] = total.astype(BF16)
        if self.out_ref is not None:
            for copy in self.along:
                copy.start()

    def fourth(self):
        sum_z(self.along, self.row_sum, self.z_in, self.own_sum)
        self.across.start()
        c = self.place[3]
        self.out_ref[c] = self.own_sum[c]

    def finish(self):
        for copy in self.first + [self.then_y] + self.then_x:
            copy.wait_send()
        if self.out_ref is not None:
            self.across.wait_recv()
            self.out_ref[1 - self.place[3]] = self.swapped[...]
            self.across.wait_send()
            for copy in self.along:
                copy.wait_send()


def along_z(sizes, source, z_in, sems):
    z_parts = sizes[1]
    z = positions()[1]
    by_z = neighbours(sizes)[1]
    return [
        remote(source.at[lax.rem(z + k, z_parts)], z_in.at[k - 1], sems, k - 1, by_z[k - 1])
        for k in range(1, z_parts)
    ]


def sum_z(copies, source, z_in, own_sum):
    for copy in copies:
        copy.wait_recv()
    total = source[positions()[1]].astype(F32)
    for k in range(len(copies)):
        total = total + z_in[k].astype(F32)
    own_sum[...] = total.astype(BF16)


def row_sum_scratch(sizes, own, cut, rest, summed=False, ends=True, keep=True):
    seq_parts, z_parts = sizes
    cols = cut + rest

    def low(*shape):
        return pltpu.VMEM(shape, BF16)

    first = [
        low(seq_parts - 1, z_parts, 2, 2, own, cut),
        low(z_parts, 2, 2, own, cut),
        low(seq_parts, z_parts, 2, own, rest),
        low(seq_parts, z_parts, 2, own, rest),
    ]
    buffers = [] if summed else first
    buffers += [low(z_parts, 2, own, cut), low(seq_parts - 1, z_parts, 2, own, rest)]
    if keep:
        buffers += [low(z_parts, 2, own, cols)]
    counts = [1, seq_parts - 1]
    if not summed:
        counts += [seq_parts - 1, 1]
    if ends:
        buffers += [low(z_parts - 1, 2, own, cols), low(2, own, cols), low(own, cols)]
        counts += [z_parts - 1, 1]
    return buffers, [pltpu.SemaphoreType.DMA((n,)) for n in counts for _ in range(2)]


def input_kernel(
    sizes,
    back_ref,
    flipped_ref,
    tokens_ref,
    resid_ref,
    gain_ref,
    block_ref,
    part_ref,
    out_ref,
    block_out,
    part_out,
    part_z_in,
    part_sum,
    part_swapped,
    z_send,
    z_recv,
    core_send,
    core_recv,
    *refs,
):
    step = pl.program_id(0)
    last = pl.num_programs(0) - 1
    c = positions()[3]
    by_seq, by_z, by_y, by_core = neighbours(sizes)
    sums = RowSums(sizes, block_ref, refs, block_out)
    part_along = along_z(sizes, part_ref, part_z_in, (z_send, z_recv))
    part_across = remote(
        part_sum.at[1 - c], part_swapped, (core_send, core_recv), 0, by_core
    )

    @pl.when(step == 0)
    def _():
        greet(by_seq + by_z + [by_y, by_core])
        for copy in part_along:
            copy.start()
        sums.start()

    width = tokens_ref.shape[2]
    tokens = tokens_ref[0].astype(F32)
    scale = lax.rsqrt(jnp.sum(tokens * tokens, -1, keepdims=True) * (1.0 / width) + epsilon)
    unit = tokens * scale
    normed_back = dot(back_ref[...], flipped_ref[...], TN)
    scaled = normed_back * gain_ref[0:1]
    middle = jnp.sum(scaled * unit, -1, keepdims=True) * (1.0 / width)
    out_ref[0] = resid_ref[...] + scale * (scaled - unit * middle)

    @pl.when(step == last - 2)
    def _():
        sums.second()

    @pl.when(step == last - 1)
    def _():
        sums.third()

    @pl.when(step == last)
    def _():
        sum_z(part_along, part_ref, part_z_in, part_sum)
        part_across.start()
        part_out[c] = part_sum[c]
        sums.fourth()
        part_across.wait_recv()
        part_out[1 - c] = part_swapped[...]
        sums.finish()
        for copy in part_along:
            copy.wait_send()
        part_across.wait_send()


def input_gradient(back, flipped, tokens, resid_back, gain, block, part, own):
    rows, width = tokens.shape[1:]
    tile = min(rows // 4, 512)
    sizes = lax.axis_size("seq"), lax.axis_size("z")
    cols, part_cols = block.shape[-1], part.shape[-1]
    cut = 128 * (cols // 256)
    buffers, sems = row_sum_scratch(sizes, own, cut, cols - cut)
    return pl.pallas_call(
        functools.partial(input_kernel, sizes),
        grid=(rows // tile,),
        in_specs=[
            pl.BlockSpec((HEADS * HROWS, tile), lambda i: (0, i)),
            pl.BlockSpec(flipped.shape, lambda i: (0, 0), pipeline_mode=pl.Buffered(1)),
            pl.BlockSpec((1, tile, width), lambda i: (0, i, 0)),
            pl.BlockSpec((tile, width), lambda i: (i, 0)),
            pl.BlockSpec((8, width), lambda i: (0, 0)),
            pl.BlockSpec(memory_space=pltpu.VMEM),
            pl.BlockSpec(memory_space=pltpu.VMEM),
        ],
        out_specs=[
            pl.BlockSpec((1, tile, width), lambda i: (0, i, 0)),
            pl.BlockSpec(memory_space=pltpu.VMEM),
            pl.BlockSpec(memory_space=pltpu.VMEM),
        ],
        out_shape=[
            jax.ShapeDtypeStruct((1, rows, width), F32),
            jax.ShapeDtypeStruct((2, own, cols), BF16),
            jax.ShapeDtypeStruct((2, own, part_cols), BF16),
        ],
        scratch_shapes=[
            pltpu.VMEM((sizes[1] - 1, 2, own, part_cols), BF16),
            pltpu.VMEM((2, own, part_cols), BF16),
            pltpu.VMEM((own, part_cols), BF16),
            pltpu.SemaphoreType.DMA((sizes[1] - 1,)),
            pltpu.SemaphoreType.DMA((sizes[1] - 1,)),
            pltpu.SemaphoreType.DMA((1,)),
            pltpu.SemaphoreType.DMA((1,)),
        ]
        + buffers
        + sems,
        compiler_params=pltpu.CompilerParams(
            collective_id=1, has_side_effects=True, vmem_limit_bytes=56 * 1024 * 1024
        ),
        cost_estimate=cost(4 * HEADS * HROWS * rows * width),
        name="input_gradient",
    )(
        back,
        flipped,
        tokens,
        resid_back,
        gain,
        block.reshape(sizes + (2, 2, own, cols)),
        part,
    )


def ffn_kernel(
    padded,
    count_ref,
    tokens_ref,
    target_ref,
    mixed_ref,
    gain_ref,
    late_ref,
    result_ref,
    normed_ref,
    hidden_ref,
    branch_ref,
    both_ref,
    attended_ref,
    resid_back_ref,
    mixed_back_ref,
    error_ref,
    w_out,
    w_gate,
    w_up,
    w_down,
    slope,
    active,
    sems,
):
    step = pl.program_id(0)
    tile, width = tokens_ref.shape[1:]
    starts = (0, width, width + padded, width + 2 * padded)
    copies = [
        pltpu.make_async_copy(
            late_ref.at[:, pl.ds(start, held.shape[1])], held, sems.at[k]
        )
        for k, (start, held) in enumerate(zip(starts, (w_out, w_gate, w_up, w_down)))
    ]

    @pl.when(step == 0)
    def _():
        for copy in copies:
            copy.start()
        error_ref[...] = jnp.zeros_like(error_ref)
        copies[0].wait()

    gain = gain_ref[1:2]
    resid = tokens_ref[0].astype(F32) + dot(mixed_ref[...], w_out[...], TN)
    scale = lax.rsqrt(jnp.sum(resid * resid, -1, keepdims=True) * (1.0 / width) + epsilon)
    unit = resid * scale
    normed = (unit * gain).astype(BF16)
    normed_ref[...] = normed.T

    @pl.when(step == 0)
    def _():
        copies[1].wait()
        copies[2].wait()

    for c in range(padded // 256):
        cols = slice(c * 256, (c + 1) * 256)
        gate = dot(normed, w_gate[:, cols], NN)
        up = dot(normed, w_up[:, cols], NN)
        sigmoid = jax.nn.sigmoid(gate)
        activated = gate * sigmoid
        hidden_ref[:, cols] = (activated * up).astype(BF16)
        active[:, cols] = activated
        slope[:, cols] = up * sigmoid * (1.0 + gate * (1.0 - sigmoid))

    @pl.when(step == 0)
    def _():
        copies[3].wait()

    full = resid + dot(hidden_ref[...], w_down[...], NT)
    result_ref[0] = full.astype(BF16)
    position = step * tile + lax.broadcasted_iota(jnp.int32, (tile, 1), 0)
    difference = jnp.where(
        position < count_ref[0], full - target_ref[0].astype(F32), 0.0
    )
    error_ref[...] += jnp.sum(difference * difference, 0, keepdims=True)
    branch = difference.astype(BF16)
    branch_ref[...] = branch.T
    for c in range(padded // 256):
        cols = slice(c * 256, (c + 1) * 256)
        hidden_back = dot(branch, w_down[:, cols], NN).astype(BF16).astype(F32)
        both_ref[:, cols] = (hidden_back * slope[:, cols]).astype(BF16)
        both_ref[:, padded + c * 256 : padded + (c + 1) * 256] = (
            hidden_back * active[:, cols]
        ).astype(BF16)
    ffn_back = dot(both_ref[:, :padded], w_gate[...], NT) + dot(
        both_ref[:, padded:], w_up[...], NT
    )
    scaled = ffn_back * gain
    middle = jnp.sum(scaled * unit, -1, keepdims=True) * (1.0 / width)
    resid_back = difference + scale * (scaled - unit * middle)
    resid_back_ref[...] = resid_back
    attended = resid_back.astype(BF16)
    attended_ref[...] = attended
    mixed_back_ref[...] = dot(w_out[...], attended, NT).astype(BF16)


def feed_forward(count, tokens, targets, mixed, gain, late, padded):
    rows, width = tokens.shape[1:]
    tile = min(rows, 256)
    token_spec = pl.BlockSpec((1, tile, width), lambda i, c: (0, i, 0))

    def flat(cols):
        return pl.BlockSpec((tile, cols), lambda i, c: (i, 0))

    tall = pl.BlockSpec((width, tile), lambda i, c: (0, i))
    line = pl.BlockSpec((1, width), lambda i, c: (0, 0))
    return pl.pallas_call(
        functools.partial(ffn_kernel, padded),
        grid_spec=pltpu.PrefetchScalarGridSpec(
            num_scalar_prefetch=1,
            grid=(rows // tile,),
            in_specs=[
                token_spec,
                token_spec,
                tall,
                pl.BlockSpec((8, width), lambda i, c: (0, 0)),
                pl.BlockSpec(memory_space=pl.ANY),
            ],
            out_specs=[
                token_spec,
                tall,
                flat(padded),
                tall,
                flat(2 * padded),
                flat(width),
                flat(width),
                tall,
                line,
            ],
            scratch_shapes=[
                pltpu.VMEM((width, width), BF16),
                pltpu.VMEM((width, padded), BF16),
                pltpu.VMEM((width, padded), BF16),
                pltpu.VMEM((width, padded), BF16),
                pltpu.VMEM((tile, padded), F32),
                pltpu.VMEM((tile, padded), F32),
                pltpu.SemaphoreType.DMA((4,)),
            ],
        ),
        out_shape=[
            jax.ShapeDtypeStruct((1, rows, width), BF16),
            jax.ShapeDtypeStruct((width, rows), BF16),
            jax.ShapeDtypeStruct((rows, padded), BF16),
            jax.ShapeDtypeStruct((width, rows), BF16),
            jax.ShapeDtypeStruct((rows, 2 * padded), BF16),
            jax.ShapeDtypeStruct((rows, width), BF16),
            jax.ShapeDtypeStruct((rows, width), F32),
            jax.ShapeDtypeStruct((width, rows), BF16),
            jax.ShapeDtypeStruct((1, width), F32),
        ],
        compiler_params=pltpu.CompilerParams(vmem_limit_bytes=60 * 1024 * 1024),
        cost_estimate=cost(4 * rows * width * (width + 3 * padded)),
        name="feed_forward",
    )(count, tokens, targets, mixed, gain, late)


def weight_grad_kernel(form, pick_ref, left_ref, right_ref, *refs):
    total = dot(left_ref[...], right_ref[...], form)
    if len(refs) > 1:
        total = total + refs[0][...].astype(F32)
    refs[-1][...] = total.astype(BF16)


def weight_grad(left, right, pick, cols, tile, extra=None, form=NN):
    rows, depth = left.shape
    step = min(rows, 512)
    each = cols // tile
    left_spec = pl.BlockSpec((step, depth), lambda j, i, p: (i, 0))
    if form is NT:
        right_spec = pl.BlockSpec((tile, depth), lambda j, i, p: (p[0] * each + j, 0))
    else:
        right_spec = pl.BlockSpec((depth, tile), lambda j, i, p: (0, p[0] * each + j))
    out_spec = pl.BlockSpec((step, tile), lambda j, i, p: (i, j))
    in_specs = [left_spec, right_spec]
    operands = [left, right]
    if extra is not None:
        in_specs.append(out_spec)
        operands.append(extra)
    return pl.pallas_call(
        functools.partial(weight_grad_kernel, form),
        grid_spec=pltpu.PrefetchScalarGridSpec(
            num_scalar_prefetch=1,
            grid=(each, rows // step),
            in_specs=in_specs,
            out_specs=out_spec,
        ),
        out_shape=jax.ShapeDtypeStruct((rows, cols), BF16),
        compiler_params=VMEM_LIMIT,
        cost_estimate=cost(2 * rows * cols * depth),
        name="weight_grad",
    )(pick, *operands)


def swap_core(array):
    return lax.ppermute(array, "core", [(i, 1 - i) for i in range(2)])


def to_send(pieces, axis, dim):
    parts = lax.axis_size(axis)
    index = lax.axis_index(axis)
    return [
        lax.dynamic_index_in_dim(pieces, lax.rem(index + shift, parts), dim, keepdims=False)
        for shift in range(parts)
    ]


def send(pieces, axis):
    parts = lax.axis_size(axis)
    return pieces[:1] + [
        lax.ppermute(piece, axis, [(i, (i + shift) % parts) for i in range(parts)])
        for shift, piece in enumerate(pieces)
        if shift
    ]


def total(pieces):
    return sum(piece.astype(F32) for piece in pieces).astype(BF16)


def as_pieces(block):
    seq_parts, z_parts = lax.axis_size("seq"), lax.axis_size("z")
    return block.reshape(seq_parts, z_parts, 2, -1, block.shape[1])


def whole_rows(own, core):
    kept = lax.dynamic_index_in_dim(own, core, 0, keepdims=False)
    other = swap_core(lax.dynamic_index_in_dim(own, 1 - core, 0, keepdims=False))
    first = jnp.where(core == 0, kept, other)
    second = jnp.where(core == 0, other, kept)
    return first, second


def shifted_sum(array, parts, sign):
    total = jnp.zeros_like(array)
    for shift in range(1, parts):
        if sign > 0:
            pairs = [(i, i + shift) for i in range(parts - shift)]
        else:
            pairs = [(i + shift, i) for i in range(parts - shift)]
        total = total + lax.ppermute(array, "seq", pairs)
    return total


def body(
    inputs,
    targets,
    valid_count,
    gain_mix,
    w_query,
    w_key,
    w_value,
    w_out,
    gain_ffn,
    w_gate,
    w_up,
    w_down,
):
    everyone = ("seq", "z", "y", "core")
    seq_parts = lax.axis_size("seq")
    devices = lax.axis_size(everyone)
    seq_index = lax.axis_index("seq")
    batch_index = lax.axis_index(("z", "y", "core"))
    core = lax.axis_index("core")
    rows, width = inputs.shape[1:]
    hidden_units = w_gate.shape[1]
    padded = -(-hidden_units // 256) * 256
    owners = jnp.arange(valid_count.shape[0])
    count = jnp.sum(jnp.where(owners == batch_index, valid_count, 0))
    total_valid = jnp.sum(valid_count).astype(F32)
    valid_here = jnp.reshape(count - seq_index * rows, (1,))
    gains = jnp.pad(jnp.stack([gain_mix, gain_ffn], 1), ((0, 0), (0, 126)))
    early = gather_rows(jnp.concatenate([gains, w_query, w_key, w_value], 1))
    fill = ((0, 0), (0, padded - hidden_units))
    late = jnp.concatenate(
        [w_out, jnp.pad(w_gate, fill), jnp.pad(w_up, fill), jnp.pad(w_down, fill)], 1
    )
    late = lax.all_gather(late, everyone, axis=0, tiled=True)
    lead = HEADS * FEAT
    qkv, normed, flipped, gain_rows = project(inputs, early)
    tie = lax.optimization_barrier
    upper = HEADS // 2
    lower_state = local_state(qkv, 0, upper)
    lower_init = shifted_sum(lower_state, seq_parts, 1)
    qkv, lower_state = tie((qkv, lower_state))
    upper_init = shifted_sum(local_state(qkv, upper, upper), seq_parts, 1)
    filled = attention_forward(qkv, lower_init, 0, upper)
    mixed, den, saved = attention_forward(qkv, upper_init, upper, upper, filled)
    (
        result,
        normed_ffn,
        hidden,
        branch_back,
        both_back,
        attended_back,
        resid_back,
        mixed_back,
        squares,
    ) = feed_forward(valid_here, inputs, targets, mixed, gain_rows, late, padded)
    local_error = 0.5 * jnp.sum(squares)
    mine, others = jnp.reshape(core, (1,)), jnp.reshape(1 - core, (1,))
    half, out_half, qkv_cols = padded // 2, width // 2, HEADS * HROWS // 2

    high = lax.reduce_precision(local_error, 8, 7)
    middle = lax.reduce_precision(local_error - high, 8, 7)
    low = lax.reduce_precision(local_error - high - middle, 8, 7)
    column = lax.broadcasted_iota(jnp.int32, (width, -(-3 * devices // 128) * 128), 1)
    place = 3 * lax.axis_index(everyone)
    side = jnp.where(column == place, high, 0.0)
    side = jnp.where(column == place + 1, middle, side)
    side = jnp.where(column == place + 2, low, side).astype(BF16)

    nb, back = local_back_state(qkv, mixed_back, mixed, den)
    later = shifted_sum(back, seq_parts, -1)
    normed_ffn, nb = tie((normed_ffn, nb))
    gate_up_sent = weight_grad(normed_ffn, both_back, others, padded, half)
    gate_up_come = swap_core(gate_up_sent)
    branch_back, gate_up_sent = tie((branch_back, gate_up_sent))
    down_sent = weight_grad(branch_back, hidden, others, half, half)
    normed_ffn, down_sent = tie((normed_ffn, down_sent))
    gate_up = weight_grad(normed_ffn, both_back, mine, padded, half, gate_up_come)
    down_come = swap_core(down_sent)
    a_one = to_send(as_pieces(gate_up[:, :half]), "seq", 0)
    a_two = to_send(as_pieces(gate_up[:, half:]), "y", 2)
    mixed, a_one, a_two, later = tie((mixed, a_one, a_two, later))
    a_one, a_two = send(a_one, "seq"), send(a_two, "y")
    out_sent = weight_grad(mixed, attended_back, others, out_half, out_half)
    out_come = swap_core(out_sent)
    branch_back, out_sent = tie((branch_back, out_sent))
    down = weight_grad(branch_back, hidden, mine, half, half, down_come)
    mixed, down = tie((mixed, down))
    outer = weight_grad(mixed, attended_back, mine, out_half, out_half, out_come)
    block = jnp.concatenate([down, outer, side], 1)
    block, a_one, a_two = tie((block, a_one, a_two))
    own = w_query.shape[0]
    z_parts = lax.axis_size("z")
    one = total(a_one).reshape(z_parts, 2, 2, own, half)
    two = total(a_two).reshape(seq_parts, z_parts, 2, own, half)
    qkv_back, gate_up_pair, part = attention_backward(
        qkv, nb, saved, later, one, two, block, own
    )
    qkv_sent = weight_grad(normed, qkv_back, others, qkv_cols, qkv_cols, None, NT)
    qkv_come = swap_core(qkv_sent)
    c_all = weight_grad(normed, qkv_back, mine, qkv_cols, qkv_cols, qkv_come, NT)
    gate_sum, up_sum = gate_up_pair[0], gate_up_pair[1]
    input_back, first_pair, pair = input_gradient(
        qkv_back, flipped, inputs, resid_back, gain_rows, c_all, part, own
    )
    down_sum = jnp.concatenate([pair[0, :, :half], pair[1, :, :half]], 1)
    out_sum = jnp.concatenate(
        [pair[0, :, half : half + out_half], pair[1, :, half : half + out_half]], 1
    )
    errors = pair[:, 0, half + out_half : half + out_half + 3 * devices].astype(F32)
    loss = 2.0 * jnp.sum(errors) / (width * total_valid)
    first, second = first_pair[0], first_pair[1]
    qkv_sum = jnp.concatenate([first, second], 1).astype(F32).reshape(own, HEADS, HROWS)
    grad_query = qkv_sum[:, :, :FEAT].reshape(own, lead)
    grad_key = qkv_sum[:, :, FEAT : 2 * FEAT].reshape(own, lead)
    grad_value = qkv_sum[:, :, 2 * FEAT :].reshape(own, HEADS * HEAD_DIM)
    grad_gate = gate_sum[:, :hidden_units].astype(F32)
    grad_up = up_sum[:, :hidden_units].astype(F32)

    def gain_grad(gain, *pairs):
        total = sum(jnp.sum(w.astype(F32) * grad, 1) for w, grad in pairs)
        return total / gain.astype(F32)

    return (
        result,
        loss,
        input_back,
        gain_grad(gain_mix, (w_query, grad_query), (w_key, grad_key), (w_value, grad_value)),
        grad_query,
        grad_key,
        grad_value,
        out_sum.astype(F32),
        gain_grad(gain_ffn, (w_gate, grad_gate), (w_up, grad_up)),
        grad_gate,
        grad_up,
        down_sum[:, :hidden_units].astype(F32),
    )


def solution(mesh):
    seq_parts, fsdp_parts = mesh.shape["seq"], mesh.shape["fsdp"]
    fine = jax.sharding.Mesh(
        mesh.devices.reshape(seq_parts, fsdp_parts // 4, 2, 2), ("seq", "z", "y", "core")
    )
    both = P(("seq", "z", "y", "core"))
    rows = P(("seq", "z", "y", "core"), None)
    tokens = P(("z", "y", "core"), "seq", None)
    return jax.shard_map(
        body,
        mesh=fine,
        in_specs=(tokens, tokens, P(), both, rows, rows, rows, rows, both, rows, rows, rows),
        out_specs=(tokens, P(), tokens, both, rows, rows, rows, rows, both, rows, rows, rows),
        check_vma=False,
    )
```

```python
import functools
import math

import jax
import jax.numpy as jnp
import numpy as np
from jax import lax
from jax.experimental import pallas as pl
from jax.experimental.pallas import tpu as pltpu
from jax.sharding import PartitionSpec as P

HEADS = 16
FEAT = 16
HEAD_DIM = 64
HROWS = 2 * FEAT + HEAD_DIM
CUT = 256
GROUPS = 11
FROWS = GROUPS * FEAT
VROWS = HEAD_DIM + 16
PAIR = 2 * VROWS
SENT = HEAD_DIM + 8
HG = 4
FIRST_BACK, SECOND_BACK = 4, 2

epsilon = 1e-05
F32 = jnp.float32
BF16 = jnp.bfloat16
NN = (((1,), (0,)), ((), ()))
NT = (((1,), (1,)), ((), ()))
TN = (((0,), (0,)), ((), ()))


def dot(left, right, dims):
    return lax.dot_general(left, right, dims, preferred_element_type=F32)


def first_row(rows, cols, count=1):
    return (lax.broadcasted_iota(jnp.int32, (rows, cols), 0) < count).astype(F32)


def rolled(u, shift):
    return pltpu.roll(u, (FEAT - shift) % FEAT, 0)


def phi_rows(u, const):
    groups = [u * u]
    for d in range(1, 9):
        groups.append(u * rolled(u, d))
    groups.append(u)
    groups.append(const)
    return jnp.concatenate([g.astype(BF16) for g in groups], 0)


def phi_pull(grad, u):
    total = grad[9 * FEAT : 10 * FEAT] + 2.0 * grad[0:FEAT] * u
    for d in range(1, 9):
        g = grad[d * FEAT : (d + 1) * FEAT]
        total = total + g * rolled(u, d) + rolled(g * u, FEAT - d)
    return total


def lane_scale():
    group = lax.broadcasted_iota(jnp.int32, (1, FROWS), 1) // FEAT
    scale = jnp.where((group == 0) | (group == 8), 1.0 / 32.0, 1.0 / 16.0)
    scale = jnp.where(group == 9, 0.25, scale)
    return jnp.where(group == 10, 1.0, scale)


def causal_mask():
    s = lax.broadcasted_iota(jnp.int32, (CUT, CUT), 0)
    t = lax.broadcasted_iota(jnp.int32, (CUT, CUT), 1)
    return s <= t


def split_pair(wide):
    high = wide.astype(BF16)
    return jnp.concatenate([high, (wide - high.astype(F32)).astype(BF16)], 0)


def twice(rows):
    return jnp.concatenate([rows, rows], 0)


def pack_states(sums, out_ref):
    fill = jnp.zeros((SENT, 2 * 128 - 2 * (FROWS - 128) - 128), F32)
    for i in range(len(sums) // 2):
        a, b = sums[2 * i][:SENT], sums[2 * i + 1][:SENT]
        out_ref[i, 0] = a[:, :128]
        out_ref[i, 1] = b[:, :128]
        out_ref[i, 2] = jnp.concatenate([a[:, 128:], b[:, 128:], fill], 1)


def unpack_states(packed_ref, state):
    side = FROWS - 128
    state[...] = jnp.zeros_like(state)
    for i in range(state.shape[0] // 2):
        for j in range(2):
            state[2 * i + j, :SENT, :128] = packed_ref[i, j]
            state[2 * i + j, :SENT, 128:] = packed_ref[i, 2][:, j * side : (j + 1) * side]


def state_kernel(blocks, qkv_ref, out_ref):
    ones2 = first_row(16, CUT, 2).astype(BF16)
    const = first_row(FEAT, CUT)

    def step(b, sums):
        cols = pl.ds(pl.multiple_of(b * CUT, CUT), CUT)
        fresh = []
        for h in range(HG):
            base = h * HROWS
            k = qkv_ref[base + FEAT : base + 2 * FEAT, cols].astype(F32)
            v = qkv_ref[base + 2 * FEAT : base + HROWS, cols]
            v_aug = jnp.concatenate([v, ones2], 0)
            fresh.append(sums[h] + dot(v_aug, phi_rows(k, const), NT))
        return tuple(fresh)

    zero = jnp.zeros((VROWS, FROWS), F32)
    sums = lax.fori_loop(0, blocks, step, (zero,) * HG)
    pack_states(sums, out_ref)


def forward_kernel(blocks, qkv_ref, init_ref, *refs):
    ones2 = first_row(16, CUT, 2).astype(BF16)
    const = first_row(FEAT, CUT)
    one_low = const.astype(BF16)
    mixed_ref, den_ref, saved_ref, state = refs[-4:]
    scale = 2.0 * lane_scale()
    mask = causal_mask()
    unpack_states(init_ref, state)

    def step(b, carry):
        cols = pl.ds(pl.multiple_of(b * CUT, CUT), CUT)
        for h in range(HG):
            base = h * HROWS
            q = qkv_ref[base : base + FEAT, cols]
            k = qkv_ref[base + FEAT : base + 2 * FEAT, cols]
            v = qkv_ref[base + 2 * FEAT : base + HROWS, cols]
            v_aug = jnp.concatenate([v, ones2], 0)
            k_aug = jnp.concatenate([k, one_low], 0)
            q_aug = jnp.concatenate([q * 0.25, one_low], 0)
            u = dot(k_aug, q_aug, TN)
            weight = jnp.where(mask, u * u + 1.0, 0.0).astype(BF16)
            low = split_pair(state[h] * scale)
            saved_ref[h, b] = low
            earlier = dot(low, phi_rows(q.astype(F32), const), NN)
            numer = dot(v_aug, weight, NN) + (earlier[:VROWS] + earlier[VROWS:])
            den = numer[HEAD_DIM : HEAD_DIM + 1]
            rows = slice(h * HEAD_DIM, (h + 1) * HEAD_DIM)
            mixed_ref[rows, cols] = (numer[:HEAD_DIM] * (1.0 / den)).astype(BF16)
            den_ref[0, h : h + 1, cols] = 0.5 * den
            state[h] += dot(v_aug, phi_rows(k.astype(F32), const), NT)
        return carry

    lax.fori_loop(0, blocks, step, 0)


def back_state_kernel(blocks, qkv_ref, grad_ref, mixed_ref, den_ref, nb_ref, out_ref):
    const = first_row(FEAT, CUT)
    row = lax.broadcasted_iota(jnp.int32, (16, CUT), 0)

    def step(b, sums):
        cols = pl.ds(pl.multiple_of(b * CUT, CUT), CUT)
        fresh = []
        for h in range(HG):
            base = h * HROWS
            q = qkv_ref[base : base + FEAT, cols].astype(F32)
            rows = slice(h * HEAD_DIM, (h + 1) * HEAD_DIM)
            g = grad_ref[rows, cols].astype(F32)
            inverse = 1.0 / den_ref[0, h : h + 1, cols]
            db = -inverse * jnp.sum(
                g * mixed_ref[rows, cols].astype(F32), axis=0, keepdims=True
            )
            nb = (g * inverse).astype(BF16)
            high = db.astype(BF16).astype(F32)
            tail = jnp.where(row == 0, high, jnp.where(row == 1, db - high, 0.0)).astype(BF16)
            nb_aug = jnp.concatenate([nb, tail], 0)
            nb_ref[h, :, cols] = nb_aug
            fresh.append(sums[h] + dot(nb_aug, phi_rows(q, const), NT))
        return tuple(fresh)

    zero = jnp.zeros((VROWS, FROWS), F32)
    sums = lax.fori_loop(0, blocks, step, (zero,) * HG)
    pack_states(sums, out_ref)


def backward_kernel(
    sizes,
    blocks,
    qkv_ref,
    nb_ref,
    saved_ref,
    init_ref,
    one_ref,
    two_ref,
    block_ref,
    out_ref,
    pair_out,
    part_out,
    state,
    *refs,
):
    ones2 = first_row(16, CUT, 2).astype(BF16)
    const = first_row(FEAT, CUT)
    one_low = const.astype(BF16)
    scale = lane_scale()
    mask = causal_mask()
    halves = pl.num_programs(1)
    at = pl.program_id(0) * halves + pl.program_id(1)
    last = pl.num_programs(0) * halves - 1
    each = blocks // halves
    by_seq, by_z, by_y, by_core = neighbours(sizes)
    count = 6 + 8
    first = RowSums(sizes, (one_ref, two_ref), refs[:count], pair_out, summed=True)
    refs = refs[count:]
    second = RowSums(sizes, block_ref, refs[:6] + (part_out,) + refs[6:])

    @pl.when(at == 0)
    def _():
        greet(by_seq + by_z + [by_y, by_core])
        first.second()
        second.start()

    @pl.when(pl.program_id(1) == 0)
    def _():
        unpack_states(init_ref, state)

    def step(i, carry):
        b = blocks - 1 - (pl.program_id(1) * each + i)
        cols = pl.ds(pl.multiple_of(b * CUT, CUT), CUT)
        for h in range(HG):
            base = h * HROWS
            q = qkv_ref[base : base + FEAT, cols]
            k = qkv_ref[base + FEAT : base + 2 * FEAT, cols]
            v = qkv_ref[base + 2 * FEAT : base + HROWS, cols]
            qf = q.astype(F32)
            kf = k.astype(F32)
            q4 = q * 0.25
            nb = nb_ref[h, :, cols]
            v_aug = jnp.concatenate([v, ones2], 0)
            k_aug = jnp.concatenate([k, one_low], 0)
            q_aug = jnp.concatenate([q4, one_low], 0)
            u = dot(k_aug, q_aug, TN)
            weight = jnp.where(mask, u * u + 1.0, 0.0).astype(BF16)
            wb = dot(v_aug, nb, TN)
            sb = jnp.where(mask, wb * u, 0.0).astype(BF16)
            q_feat_back = dot(saved_ref[h, b], twice(nb), TN)
            dq = 0.25 * dot(k, sb, NN) + 0.5 * phi_pull(q_feat_back, qf)
            low = split_pair(state[h] * scale)
            k_feat_back = dot(low, twice(v_aug), TN)
            later = dot(low, phi_rows(kf, const), NN)
            dk = dot(q4, sb, NT) + phi_pull(k_feat_back, kf)
            dv = 0.5 * dot(nb[:HEAD_DIM], weight, NT) + (
                later[:HEAD_DIM] + later[VROWS : VROWS + HEAD_DIM]
            )
            out_ref[base : base + FEAT, cols] = dq.astype(BF16)
            out_ref[base + FEAT : base + 2 * FEAT, cols] = dk.astype(BF16)
            out_ref[base + 2 * FEAT : base + HROWS, cols] = dv.astype(BF16)
            state[h] += dot(nb, phi_rows(qf, const), NT)
        return carry

    lax.fori_loop(0, each, step, 0)

    @pl.when(at == last - FIRST_BACK)
    def _():
        first.third()

    @pl.when(at == last - SECOND_BACK)
    def _():
        second.second()

    @pl.when(at == last)
    def _():
        second.third()
        first.fourth()
        second.finish()
        first.finish()


def cost(flops):
    return pl.CostEstimate(flops=int(flops * 0.02), bytes_accessed=0, transcendentals=0)


def head_spec(rows, cols):
    return pl.BlockSpec((HG * rows, cols), lambda g: (g, 0))


def lead_spec(*tail):
    return pl.BlockSpec((HG,) + tail, lambda g: (g,) + (0,) * len(tail))


VMEM_LIMIT = pltpu.CompilerParams(vmem_limit_bytes=56 * 1024 * 1024)


def packed_shape(heads):
    return jax.ShapeDtypeStruct((heads // 2, 3, SENT, 128), F32)


def packed_spec():
    return pl.BlockSpec((HG // 2, 3, SENT, 128), lambda g: (g, 0, 0, 0))


def local_state(qkv, start, count):
    cols = qkv.shape[1]
    first = start // HG
    return pl.pallas_call(
        functools.partial(state_kernel, cols // CUT),
        grid=(count // HG,),
        in_specs=[pl.BlockSpec((HG * HROWS, cols), lambda g: (first + g, 0))],
        out_specs=packed_spec(),
        out_shape=packed_shape(count),
        compiler_params=VMEM_LIMIT,
        cost_estimate=cost(11e9 * cols / 2048 * count / HEADS),
        name="key_state",
    )(qkv)


def attention_forward(qkv, init, start, count, filled=()):
    cols = qkv.shape[1]
    blocks = cols // CUT
    first = start // HG

    def head_rows(rows):
        return pl.BlockSpec((HG * rows, cols), lambda g: (first + g, 0))

    def lead(*tail):
        return pl.BlockSpec((HG,) + tail, lambda g: (first + g,) + (0,) * len(tail))

    return pl.pallas_call(
        functools.partial(forward_kernel, blocks),
        grid=(count // HG,),
        in_specs=[head_rows(HROWS), packed_spec()]
        + [pl.BlockSpec(memory_space=pl.ANY)] * len(filled),
        out_specs=[
            head_rows(HEAD_DIM),
            pl.BlockSpec((1, HG, cols), lambda g: (first + g, 0, 0)),
            lead(blocks, PAIR, FROWS),
        ],
        out_shape=[
            jax.ShapeDtypeStruct((HEADS * HEAD_DIM, cols), BF16),
            jax.ShapeDtypeStruct((HEADS // HG, HG, cols), F32),
            jax.ShapeDtypeStruct((HEADS, blocks, PAIR, FROWS), BF16),
        ],
        scratch_shapes=[pltpu.VMEM((HG, VROWS, FROWS), F32)],
        compiler_params=VMEM_LIMIT,
        cost_estimate=cost(36e9 * cols / 2048 * count / HEADS),
        input_output_aliases={2 + i: i for i in range(len(filled))},
        name="attend",
    )(qkv, init, *filled)


def local_back_state(qkv, grad, mixed, den):
    cols = qkv.shape[1]
    return pl.pallas_call(
        functools.partial(back_state_kernel, cols // CUT),
        grid=(HEADS // HG,),
        in_specs=[
            head_spec(HROWS, cols),
            head_spec(HEAD_DIM, cols),
            head_spec(HEAD_DIM, cols),
            pl.BlockSpec((1, HG, cols), lambda g: (g, 0, 0)),
        ],
        out_specs=[lead_spec(VROWS, cols), packed_spec()],
        out_shape=[
            jax.ShapeDtypeStruct((HEADS, VROWS, cols), BF16),
            packed_shape(HEADS),
        ],
        compiler_params=VMEM_LIMIT,
        cost_estimate=cost(13e9 * cols / 2048),
        name="query_state",
    )(qkv, grad, mixed, den)


def attention_backward(qkv, nb, saved, init, one, two, block, own):
    cols = qkv.shape[1]
    blocks = cols // CUT
    sizes = lax.axis_size("seq"), lax.axis_size("z")
    width = block.shape[-1]
    cut = 128 * (width // 256)
    wide = one.shape[-1] + two.shape[-1]
    first_buffers, first_sems = row_sum_scratch(
        sizes, own, one.shape[-1], two.shape[-1], summed=True
    )
    second_buffers, second_sems = row_sum_scratch(
        sizes, own, cut, width - cut, ends=False, keep=False
    )

    def head_rows(rows):
        return pl.BlockSpec((HG * rows, cols), lambda g, p: (g, 0))

    def lead(*tail):
        return pl.BlockSpec((HG,) + tail, lambda g, p: (g,) + (0,) * len(tail))

    here = pl.BlockSpec(memory_space=pltpu.VMEM)
    return pl.pallas_call(
        functools.partial(backward_kernel, sizes, blocks),
        grid=(HEADS // HG, 2),
        in_specs=[
            head_rows(HROWS),
            lead(VROWS, cols),
            lead(blocks, PAIR, FROWS),
            pl.BlockSpec((HG // 2, 3, SENT, 128), lambda g, p: (g, 0, 0, 0)),
            here,
            here,
            here,
        ],
        out_specs=[head_rows(HROWS), here, here],
        out_shape=[
            jax.ShapeDtypeStruct((HEADS * HROWS, cols), BF16),
            jax.ShapeDtypeStruct((2, own, wide), BF16),
            jax.ShapeDtypeStruct((sizes[1], 2, own, width), BF16),
        ],
        scratch_shapes=[pltpu.VMEM((HG, VROWS, FROWS), F32)]
        + first_buffers
        + first_sems
        + second_buffers
        + second_sems,
        compiler_params=pltpu.CompilerParams(
            collective_id=2, has_side_effects=True, vmem_limit_bytes=58 * 1024 * 1024
        ),
        cost_estimate=cost(53e9 * cols / 2048),
        name="attend_back",
    )(qkv, nb, saved, init, one, two, block.reshape(sizes + (2, 2, own, width)))


MESH = pl.DeviceIdType.MESH


def gather_kernel(shape, split, shard_ref, out_ref, local_sem, *sems):
    seq_parts, z_parts = shape
    s, z = lax.axis_index("seq"), lax.axis_index("z")
    y, c = lax.axis_index("y"), lax.axis_index("core")
    cols = shard_ref.shape[1]
    left, right = pl.ds(0, split), pl.ds(split, cols - split)
    every = slice(None)

    def peer(ds=0, dz=0, dy=0, dc=0):
        return (
            lax.rem(s + ds, seq_parts),
            lax.rem(z + dz, z_parts),
            lax.rem(y + dy, 2),
            lax.rem(c + dc, 2),
        )

    def send(kind, slot, src, dst, device):
        return pltpu.make_async_remote_copy(
            src_ref=src,
            dst_ref=dst,
            send_sem=sems[2 * kind].at[slot],
            recv_sem=sems[2 * kind + 1].at[slot],
            device_id=device,
            device_id_type=MESH,
        )

    barrier = pltpu.get_barrier_semaphore()
    peers = [peer(ds=j) for j in range(1, seq_parts)]
    peers += [peer(dz=k) for k in range(1, z_parts)]
    peers += [peer(dy=1), peer(dc=1)]
    for device in peers:
        pl.semaphore_signal(barrier, inc=1, device_id=device, device_id_type=MESH)
    own = pltpu.make_async_copy(shard_ref, out_ref.at[s, z, y, c], local_sem)
    own.start()
    pl.semaphore_wait(barrier, len(peers))

    order = [0] + sorted(range(1, z_parts), key=lambda k: min(k, z_parts - k))
    slab = {k: lax.rem(z + z_parts - k, z_parts) for k in order}
    along = {
        k: send(0, k, shard_ref, out_ref.at[s, z, y, c], peer(dz=k)) for k in order[1:]
    }
    for k in order[1:]:
        along[k].start()
    own.wait()
    first_y, first_x = {}, {}
    for k in order:
        if k:
            along[k].wait_recv()
        at = out_ref.at[s, slab[k], y, c, :, left]
        first_y[k] = send(1, k, at, at, peer(dy=1))
        first_y[k].start()
        at = out_ref.at[s, slab[k], y, c, :, right]
        first_x[k] = [
            send(2, k * seq_parts + j, at, at, peer(ds=j)) for j in range(1, seq_parts)
        ]
        for copy in first_x[k]:
            copy.start()
    then_x, then_y, across = {}, {}, {}
    for k in order:
        first_y[k].wait_recv()
        at = out_ref.at[s, slab[k], :, c, :, left]
        then_x[k] = [
            send(3, k * seq_parts + j, at, at, peer(ds=j)) for j in range(1, seq_parts)
        ]
        for copy in then_x[k]:
            copy.start()
        for copy in first_x[k]:
            copy.wait_recv()
        at = out_ref.at[:, slab[k], y, c, :, right]
        then_y[k] = send(4, k, at, at, peer(dy=1))
        then_y[k].start()
    for k in order:
        for copy in then_x[k]:
            copy.wait_recv()
        then_y[k].wait_recv()
        at = out_ref.at[:, slab[k], :, c]
        across[k] = send(5, k, at, at, peer(dc=1))
        across[k].start()
    for k in order:
        across[k].wait_recv()
    for k in order:
        if k:
            along[k].wait_send()
        first_y[k].wait_send()
        then_y[k].wait_send()
        across[k].wait_send()
        for copy in first_x[k] + then_x[k]:
            copy.wait_send()


def gather_rows(shard):
    own, cols = shard.shape
    seq_parts, z_parts = lax.axis_size("seq"), lax.axis_size("z")
    split = cols // 256 * 128
    counts = (z_parts, z_parts, z_parts * seq_parts, z_parts * seq_parts, z_parts, z_parts)
    out = pl.pallas_call(
        functools.partial(gather_kernel, (seq_parts, z_parts), split),
        in_specs=[pl.BlockSpec(memory_space=pl.ANY)],
        out_specs=pl.BlockSpec(memory_space=pl.ANY),
        out_shape=jax.ShapeDtypeStruct((seq_parts, z_parts, 2, 2, own, cols), BF16),
        scratch_shapes=[pltpu.SemaphoreType.DMA]
        + [pltpu.SemaphoreType.DMA((n,)) for n in counts for _ in range(2)],
        compiler_params=pltpu.CompilerParams(collective_id=0, has_side_effects=True),
        cost_estimate=cost(25e9),
        name="gather_rows",
    )(shard)
    return out.reshape(-1, cols)


def project_kernel(tokens_ref, weight_ref, qkv_ref, normed_ref, flipped_ref, gain_ref):
    width = tokens_ref.shape[2]
    lead = HEADS * FEAT

    @pl.when(pl.program_id(0) == 0)
    def _():
        gain_ref[...] = weight_ref[:, :128].astype(F32).T[:8]
        for c in range(HEADS * HROWS // 128):
            piece = weight_ref[:, 128 * (c + 1) : 128 * (c + 2)].T
            start = 128 * c
            if start < 2 * lead:
                each, first = FEAT, FEAT * (start // lead)
                head = (start % lead) // FEAT
            else:
                each, first = HEAD_DIM, 2 * FEAT
                head = (start - 2 * lead) // HEAD_DIM
            for j in range(128 // each):
                at = (head + j) * HROWS + first
                flipped_ref[at : at + each, :] = piece[j * each : (j + 1) * each]

    tokens = tokens_ref[0].astype(F32)
    scale = lax.rsqrt(jnp.sum(tokens * tokens, -1, keepdims=True) * (1.0 / width) + epsilon)
    normed = (tokens * scale * gain_ref[0:1]).astype(BF16)
    normed_ref[...] = normed.T
    qkv_ref[...] = dot(flipped_ref[...], normed, NT).astype(BF16)


def project(tokens, early):
    rows, width = tokens.shape[1:]
    tile = min(rows, 512)
    return pl.pallas_call(
        project_kernel,
        grid=(rows // tile,),
        in_specs=[
            pl.BlockSpec((1, tile, width), lambda i: (0, i, 0)),
            pl.BlockSpec(
                (width, 128 + HEADS * HROWS), lambda i: (0, 0), pipeline_mode=pl.Buffered(1)
            ),
        ],
        out_specs=[
            pl.BlockSpec((HEADS * HROWS, tile), lambda i: (0, i)),
            pl.BlockSpec((width, tile), lambda i: (0, i)),
            pl.BlockSpec((HEADS * HROWS, width), lambda i: (0, 0)),
            pl.BlockSpec((8, width), lambda i: (0, 0)),
        ],
        out_shape=[
            jax.ShapeDtypeStruct((HEADS * HROWS, rows), BF16),
            jax.ShapeDtypeStruct((width, rows), BF16),
            jax.ShapeDtypeStruct((HEADS * HROWS, width), BF16),
            jax.ShapeDtypeStruct((8, width), F32),
        ],
        compiler_params=VMEM_LIMIT,
        cost_estimate=cost(2 * HEADS * HROWS * rows * width),
        name="project",
    )(tokens, early)


def remote(src, dst, sems, slot, device):
    return pltpu.make_async_remote_copy(
        src_ref=src,
        dst_ref=dst,
        send_sem=sems[0].at[slot],
        recv_sem=sems[1].at[slot],
        device_id=device,
        device_id_type=MESH,
    )


def positions():
    return tuple(lax.axis_index(name) for name in ("seq", "z", "y", "core"))


def neighbours(sizes):
    seq_parts, z_parts = sizes
    s, z, y, c = positions()
    by_seq = [(lax.rem(s + j, seq_parts), z, y, c) for j in range(1, seq_parts)]
    by_z = [(s, lax.rem(z + k, z_parts), y, c) for k in range(1, z_parts)]
    return by_seq, by_z, (s, z, 1 - y, c), (s, z, y, 1 - c)


def greet(devices):
    barrier = pltpu.get_barrier_semaphore()
    for device in devices:
        pl.semaphore_signal(barrier, inc=1, device_id=device, device_id_type=MESH)
    pl.semaphore_wait(barrier, len(devices))


class RowSums:
    def __init__(self, sizes, source, refs, out_ref=None, summed=False):
        seq_parts, z_parts = self.sizes = sizes
        s, z, y, c = self.place = positions()
        by_seq, by_z, by_y, by_core = neighbours(sizes)
        self.source, self.summed, self.out_ref = source, summed, out_ref
        refs = list(refs)
        if summed:
            self.x_sum, self.y_sum = source
        else:
            self.x_in, self.x_sum, self.y_in, self.y_sum = refs[:4]
            del refs[:4]
        self.then_y_in, self.then_x_in, self.row_sum = refs[:3]
        del refs[:3]
        self.cut = self.x_sum.shape[-1]
        rest = self.y_sum.shape[-1]
        if out_ref is not None:
            self.z_in, self.own_sum, self.swapped = refs[:3]
            del refs[:3]
        pairs = [refs[2 * i : 2 * i + 2] for i in range(len(refs) // 2)]
        others = range(1, seq_parts)
        self.first = []
        if not summed:
            left, right = pl.ds(0, self.cut), pl.ds(self.cut, rest)
            self.first_x = [
                remote(
                    source.at[lax.rem(s + j, seq_parts), :, :, :, :, left],
                    self.x_in.at[j - 1],
                    pairs[2],
                    j - 1,
                    by_seq[j - 1],
                )
                for j in others
            ]
            self.first_y = remote(
                source.at[:, :, 1 - y, :, :, right], self.y_in, pairs[3], 0, by_y
            )
            self.first = self.first_x + [self.first_y]
        self.then_y = remote(self.x_sum.at[:, 1 - y], self.then_y_in, pairs[0], 0, by_y)
        self.then_x = [
            remote(
                self.y_sum.at[lax.rem(s + j, seq_parts)],
                self.then_x_in.at[j - 1],
                pairs[1],
                j - 1,
                by_seq[j - 1],
            )
            for j in others
        ]
        if out_ref is not None:
            self.along = along_z(sizes, self.row_sum, self.z_in, pairs[-2])
            self.across = remote(self.own_sum.at[1 - c], self.swapped, pairs[-1], 0, by_core)

    def start(self):
        for copy in self.first:
            copy.start()

    def second(self):
        s, z, y, c = self.place
        if not self.summed:
            for copy in self.first_x:
                copy.wait_recv()
            total = self.source[s, :, :, :, :, : self.cut].astype(F32)
            for j in range(self.sizes[0] - 1):
                total = total + self.x_in[j].astype(F32)
            self.x_sum[...] = total.astype(BF16)
        self.then_y.start()
        if not self.summed:
            self.first_y.wait_recv()
            total = self.source[:, :, y, :, :, self.cut :].astype(F32)
            self.y_sum[...] = (total + self.y_in[...].astype(F32)).astype(BF16)
        for copy in self.then_x:
            copy.start()

    def third(self):
        s, z, y, c = self.place
        self.then_y.wait_recv()
        total = self.x_sum[:, y].astype(F32) + self.then_y_in[...].astype(F32)
        self.row_sum[:, :, :, : self.cut] = total.astype(BF16)
        for copy in self.then_x:
            copy.wait_recv()
        total = self.y_sum[s].astype(F32)
        for j in range(self.sizes[0] - 1):
            total = total + self.then_x_in[j].astype(F32)
        self.row_sum[:, :, :, self.cut :] = total.astype(BF16)
        if self.out_ref is not None:
            for copy in self.along:
                copy.start()

    def fourth(self):
        sum_z(self.along, self.row_sum, self.z_in, self.own_sum)
        self.across.start()
        c = self.place[3]
        self.out_ref[c] = self.own_sum[c]

    def finish(self):
        for copy in self.first + [self.then_y] + self.then_x:
            copy.wait_send()
        if self.out_ref is not None:
            self.across.wait_recv()
            self.out_ref[1 - self.place[3]] = self.swapped[...]
            self.across.wait_send()
            for copy in self.along:
                copy.wait_send()


def along_z(sizes, source, z_in, sems):
    z_parts = sizes[1]
    z = positions()[1]
    by_z = neighbours(sizes)[1]
    return [
        remote(source.at[lax.rem(z + k, z_parts)], z_in.at[k - 1], sems, k - 1, by_z[k - 1])
        for k in range(1, z_parts)
    ]


def sum_z(copies, source, z_in, own_sum):
    for copy in copies:
        copy.wait_recv()
    total = source[positions()[1]].astype(F32)
    for k in range(len(copies)):
        total = total + z_in[k].astype(F32)
    own_sum[...] = total.astype(BF16)


def row_sum_scratch(sizes, own, cut, rest, summed=False, ends=True, keep=True):
    seq_parts, z_parts = sizes
    cols = cut + rest

    def low(*shape):
        return pltpu.VMEM(shape, BF16)

    first = [
        low(seq_parts - 1, z_parts, 2, 2, own, cut),
        low(z_parts, 2, 2, own, cut),
        low(seq_parts, z_parts, 2, own, rest),
        low(seq_parts, z_parts, 2, own, rest),
    ]
    buffers = [] if summed else first
    buffers += [low(z_parts, 2, own, cut), low(seq_parts - 1, z_parts, 2, own, rest)]
    if keep:
        buffers += [low(z_parts, 2, own, cols)]
    counts = [1, seq_parts - 1]
    if not summed:
        counts += [seq_parts - 1, 1]
    if ends:
        buffers += [low(z_parts - 1, 2, own, cols), low(2, own, cols), low(own, cols)]
        counts += [z_parts - 1, 1]
    return buffers, [pltpu.SemaphoreType.DMA((n,)) for n in counts for _ in range(2)]


def input_kernel(
    sizes,
    back_ref,
    flipped_ref,
    tokens_ref,
    resid_ref,
    gain_ref,
    block_ref,
    part_ref,
    out_ref,
    block_out,
    part_out,
    part_z_in,
    part_sum,
    part_swapped,
    z_send,
    z_recv,
    core_send,
    core_recv,
    *refs,
):
    step = pl.program_id(0)
    last = pl.num_programs(0) - 1
    c = positions()[3]
    by_seq, by_z, by_y, by_core = neighbours(sizes)
    sums = RowSums(sizes, block_ref, refs, block_out)
    part_along = along_z(sizes, part_ref, part_z_in, (z_send, z_recv))
    part_across = remote(
        part_sum.at[1 - c], part_swapped, (core_send, core_recv), 0, by_core
    )

    @pl.when(step == 0)
    def _():
        greet(by_seq + by_z + [by_y, by_core])
        for copy in part_along:
            copy.start()
        sums.start()

    width = tokens_ref.shape[2]
    tokens = tokens_ref[0].astype(F32)
    scale = lax.rsqrt(jnp.sum(tokens * tokens, -1, keepdims=True) * (1.0 / width) + epsilon)
    unit = tokens * scale
    normed_back = dot(back_ref[...], flipped_ref[...], TN)
    scaled = normed_back * gain_ref[0:1]
    middle = jnp.sum(scaled * unit, -1, keepdims=True) * (1.0 / width)
    out_ref[0] = resid_ref[...] + scale * (scaled - unit * middle)

    @pl.when(step == last - 2)
    def _():
        sums.second()

    @pl.when(step == last - 1)
    def _():
        sums.third()

    @pl.when(step == last)
    def _():
        sum_z(part_along, part_ref, part_z_in, part_sum)
        part_across.start()
        part_out[c] = part_sum[c]
        sums.fourth()
        part_across.wait_recv()
        part_out[1 - c] = part_swapped[...]
        sums.finish()
        for copy in part_along:
            copy.wait_send()
        part_across.wait_send()


def input_gradient(back, flipped, tokens, resid_back, gain, block, part, own):
    rows, width = tokens.shape[1:]
    tile = min(rows // 4, 512)
    sizes = lax.axis_size("seq"), lax.axis_size("z")
    cols, part_cols = block.shape[-1], part.shape[-1]
    cut = 128 * (cols // 256)
    buffers, sems = row_sum_scratch(sizes, own, cut, cols - cut)
    return pl.pallas_call(
        functools.partial(input_kernel, sizes),
        grid=(rows // tile,),
        in_specs=[
            pl.BlockSpec((HEADS * HROWS, tile), lambda i: (0, i)),
            pl.BlockSpec(flipped.shape, lambda i: (0, 0), pipeline_mode=pl.Buffered(1)),
            pl.BlockSpec((1, tile, width), lambda i: (0, i, 0)),
            pl.BlockSpec((tile, width), lambda i: (i, 0)),
            pl.BlockSpec((8, width), lambda i: (0, 0)),
            pl.BlockSpec(memory_space=pltpu.VMEM),
            pl.BlockSpec(memory_space=pltpu.VMEM),
        ],
        out_specs=[
            pl.BlockSpec((1, tile, width), lambda i: (0, i, 0)),
            pl.BlockSpec(memory_space=pltpu.VMEM),
            pl.BlockSpec(memory_space=pltpu.VMEM),
        ],
        out_shape=[
            jax.ShapeDtypeStruct((1, rows, width), F32),
            jax.ShapeDtypeStruct((2, own, cols), BF16),
            jax.ShapeDtypeStruct((2, own, part_cols), BF16),
        ],
        scratch_shapes=[
            pltpu.VMEM((sizes[1] - 1, 2, own, part_cols), BF16),
            pltpu.VMEM((2, own, part_cols), BF16),
            pltpu.VMEM((own, part_cols), BF16),
            pltpu.SemaphoreType.DMA((sizes[1] - 1,)),
            pltpu.SemaphoreType.DMA((sizes[1] - 1,)),
            pltpu.SemaphoreType.DMA((1,)),
            pltpu.SemaphoreType.DMA((1,)),
        ]
        + buffers
        + sems,
        compiler_params=pltpu.CompilerParams(
            collective_id=1, has_side_effects=True, vmem_limit_bytes=56 * 1024 * 1024
        ),
        cost_estimate=cost(4 * HEADS * HROWS * rows * width),
        name="input_gradient",
    )(
        back,
        flipped,
        tokens,
        resid_back,
        gain,
        block.reshape(sizes + (2, 2, own, cols)),
        part,
    )


def last_kernel(
    sizes,
    normed_ref,
    back_ref,
    flipped_ref,
    tokens_ref,
    resid_ref,
    gain_ref,
    part_ref,
    out_ref,
    block_out,
    part_out,
    sent,
    come,
    block,
    part_z_in,
    part_sum,
    part_swapped,
    half_send,
    half_recv,
    z_send,
    z_recv,
    core_send,
    core_recv,
    *refs,
):
    step = pl.program_id(0)
    c = positions()[3]
    by_seq, by_z, by_y, by_core = neighbours(sizes)
    sums = RowSums(sizes, block, refs, block_out)
    part_along = along_z(sizes, part_ref, part_z_in, (z_send, z_recv))
    part_across = remote(
        part_sum.at[1 - c], part_swapped, (core_send, core_recv), 0, by_core
    )
    half = remote(sent, come, (half_send, half_recv), 0, by_core)
    cols = sent.shape[1]
    each = sent.shape[0] // sizes[0]
    tile, width = tokens_ref.shape[1:]

    def gradient(s, which):
        rows = pl.ds(pl.multiple_of(which * cols, 16), cols)
        return dot(normed_ref[s * each : (s + 1) * each, :], back_ref[rows, :], NT)

    @pl.when(step == 0)
    def _():
        greet(by_seq + by_z + [by_y, by_core])
        for copy in part_along:
            copy.start()
        for s in range(sizes[0]):
            sent[s * each : (s + 1) * each, :] = gradient(s, 1 - c).astype(BF16)
        half.start()

    @pl.when(step == 2)
    def _():
        half.wait_recv()
        for s in range(sizes[0]):
            total = gradient(s, c) + come[s * each : (s + 1) * each, :].astype(F32)
            block[s] = total.astype(BF16).reshape(block.shape[1:])
        sums.start()

    @pl.when((step == 1) | (step > 2))
    def _():
        at = pl.multiple_of(step // 3 * (step - 2) * tile, 128)
        tokens = tokens_ref[0].astype(F32)
        scale = lax.rsqrt(
            jnp.sum(tokens * tokens, -1, keepdims=True) * (1.0 / width) + epsilon
        )
        unit = tokens * scale
        normed_back = dot(back_ref[:, pl.ds(at, tile)], flipped_ref[...], TN)
        scaled = normed_back * gain_ref[0:1]
        middle = jnp.sum(scaled * unit, -1, keepdims=True) * (1.0 / width)
        out_ref[0] = resid_ref[...] + scale * (scaled - unit * middle)

    @pl.when(step == 4)
    def _():
        sums.second()

    @pl.when(step == 5)
    def _():
        sums.third()
        sum_z(part_along, part_ref, part_z_in, part_sum)
        part_across.start()
        part_out[c] = part_sum[c]
        sums.fourth()
        part_across.wait_recv()
        part_out[1 - c] = part_swapped[...]
        sums.finish()
        for copy in part_along:
            copy.wait_send()
        part_across.wait_send()
        half.wait_send()


def last_gradients(normed, back, flipped, tokens, resid_back, gain, part, own):
    rows, width = tokens.shape[1:]
    tile = rows // 4
    sizes = lax.axis_size("seq"), lax.axis_size("z")
    cols, part_cols = HEADS * HROWS // 2, part.shape[-1]
    cut = 128 * (cols // 256)
    buffers, sems = row_sum_scratch(sizes, own, cut, cols - cut)
    here = pl.BlockSpec(memory_space=pltpu.VMEM)

    def place(i):
        return i // 3 * (i - 2)

    def low(*shape):
        return pltpu.VMEM(shape, BF16)

    one, many = pltpu.SemaphoreType.DMA((1,)), pltpu.SemaphoreType.DMA((sizes[1] - 1,))
    return pl.pallas_call(
        functools.partial(last_kernel, sizes),
        grid=(6,),
        in_specs=[
            here,
            here,
            here,
            pl.BlockSpec((1, tile, width), lambda i: (0, place(i), 0)),
            pl.BlockSpec((tile, width), lambda i: (place(i), 0)),
            pl.BlockSpec((8, width), lambda i: (0, 0)),
            here,
        ],
        out_specs=[pl.BlockSpec((1, tile, width), lambda i: (0, place(i), 0)), here, here],
        out_shape=[
            jax.ShapeDtypeStruct((1, rows, width), F32),
            jax.ShapeDtypeStruct((2, own, cols), BF16),
            jax.ShapeDtypeStruct((2, own, part_cols), BF16),
        ],
        scratch_shapes=[
            low(width, cols),
            low(width, cols),
            low(*sizes, 2, 2, own, cols),
            low(sizes[1] - 1, 2, own, part_cols),
            low(2, own, part_cols),
            low(own, part_cols),
            one,
            one,
            many,
            many,
            one,
            one,
        ]
        + buffers
        + sems,
        compiler_params=pltpu.CompilerParams(
            collective_id=3, has_side_effects=True, vmem_limit_bytes=56 * 1024 * 1024
        ),
        cost_estimate=cost(8 * HEADS * HROWS * rows * width),
        name="last_gradients",
    )(normed, back, flipped, tokens, resid_back, gain, part)


def ffn_kernel(
    padded,
    count_ref,
    tokens_ref,
    target_ref,
    mixed_ref,
    gain_ref,
    late_ref,
    result_ref,
    normed_ref,
    hidden_ref,
    branch_ref,
    both_ref,
    attended_ref,
    resid_back_ref,
    mixed_back_ref,
    error_ref,
    w_out,
    w_gate,
    w_up,
    w_down,
    slope,
    active,
    sems,
):
    step = pl.program_id(0)
    tile, width = tokens_ref.shape[1:]
    starts = (0, width, width + padded, width + 2 * padded)
    copies = [
        pltpu.make_async_copy(
            late_ref.at[:, pl.ds(start, held.shape[1])], held, sems.at[k]
        )
        for k, (start, held) in enumerate(zip(starts, (w_out, w_gate, w_up, w_down)))
    ]

    @pl.when(step == 0)
    def _():
        for copy in copies:
            copy.start()
        error_ref[...] = jnp.zeros_like(error_ref)
        copies[0].wait()

    gain = gain_ref[1:2]
    resid = tokens_ref[0].astype(F32) + dot(mixed_ref[...], w_out[...], TN)
    scale = lax.rsqrt(jnp.sum(resid * resid, -1, keepdims=True) * (1.0 / width) + epsilon)
    unit = resid * scale
    normed = (unit * gain).astype(BF16)
    normed_ref[...] = normed.T

    @pl.when(step == 0)
    def _():
        copies[1].wait()
        copies[2].wait()

    for c in range(padded // 256):
        cols = slice(c * 256, (c + 1) * 256)
        gate = dot(normed, w_gate[:, cols], NN)
        up = dot(normed, w_up[:, cols], NN)
        sigmoid = jax.nn.sigmoid(gate)
        activated = gate * sigmoid
        hidden_ref[:, cols] = (activated * up).astype(BF16)
        active[:, cols] = activated
        slope[:, cols] = up * sigmoid * (1.0 + gate * (1.0 - sigmoid))

    @pl.when(step == 0)
    def _():
        copies[3].wait()

    full = resid + dot(hidden_ref[...], w_down[...], NT)
    result_ref[0] = full.astype(BF16)
    position = step * tile + lax.broadcasted_iota(jnp.int32, (tile, 1), 0)
    difference = jnp.where(
        position < count_ref[0], full - target_ref[0].astype(F32), 0.0
    )
    error_ref[...] += jnp.sum(difference * difference, 0, keepdims=True)
    branch = difference.astype(BF16)
    branch_ref[...] = branch.T
    for c in range(padded // 256):
        cols = slice(c * 256, (c + 1) * 256)
        hidden_back = dot(branch, w_down[:, cols], NN).astype(BF16).astype(F32)
        both_ref[:, cols] = (hidden_back * slope[:, cols]).astype(BF16)
        both_ref[:, padded + c * 256 : padded + (c + 1) * 256] = (
            hidden_back * active[:, cols]
        ).astype(BF16)
    ffn_back = dot(both_ref[:, :padded], w_gate[...], NT) + dot(
        both_ref[:, padded:], w_up[...], NT
    )
    scaled = ffn_back * gain
    middle = jnp.sum(scaled * unit, -1, keepdims=True) * (1.0 / width)
    resid_back = difference + scale * (scaled - unit * middle)
    resid_back_ref[...] = resid_back
    attended = resid_back.astype(BF16)
    attended_ref[...] = attended
    mixed_back_ref[...] = dot(w_out[...], attended, NT).astype(BF16)


def feed_forward(count, tokens, targets, mixed, gain, late, padded):
    rows, width = tokens.shape[1:]
    tile = min(rows, 256)
    token_spec = pl.BlockSpec((1, tile, width), lambda i, c: (0, i, 0))

    def flat(cols):
        return pl.BlockSpec((tile, cols), lambda i, c: (i, 0))

    tall = pl.BlockSpec((width, tile), lambda i, c: (0, i))
    line = pl.BlockSpec((1, width), lambda i, c: (0, 0))
    return pl.pallas_call(
        functools.partial(ffn_kernel, padded),
        grid_spec=pltpu.PrefetchScalarGridSpec(
            num_scalar_prefetch=1,
            grid=(rows // tile,),
            in_specs=[
                token_spec,
                token_spec,
                tall,
                pl.BlockSpec((8, width), lambda i, c: (0, 0)),
                pl.BlockSpec(memory_space=pl.ANY),
            ],
            out_specs=[
                token_spec,
                tall,
                flat(padded),
                tall,
                flat(2 * padded),
                flat(width),
                flat(width),
                tall,
                line,
            ],
            scratch_shapes=[
                pltpu.VMEM((width, width), BF16),
                pltpu.VMEM((width, padded), BF16),
                pltpu.VMEM((width, padded), BF16),
                pltpu.VMEM((width, padded), BF16),
                pltpu.VMEM((tile, padded), F32),
                pltpu.VMEM((tile, padded), F32),
                pltpu.SemaphoreType.DMA((4,)),
            ],
        ),
        out_shape=[
            jax.ShapeDtypeStruct((1, rows, width), BF16),
            jax.ShapeDtypeStruct((width, rows), BF16),
            jax.ShapeDtypeStruct((rows, padded), BF16),
            jax.ShapeDtypeStruct((width, rows), BF16),
            jax.ShapeDtypeStruct((rows, 2 * padded), BF16),
            jax.ShapeDtypeStruct((rows, width), BF16),
            jax.ShapeDtypeStruct((rows, width), F32),
            jax.ShapeDtypeStruct((width, rows), BF16),
            jax.ShapeDtypeStruct((1, width), F32),
        ],
        compiler_params=pltpu.CompilerParams(vmem_limit_bytes=60 * 1024 * 1024),
        cost_estimate=cost(4 * rows * width * (width + 3 * padded)),
        name="feed_forward",
    )(count, tokens, targets, mixed, gain, late)


def weight_grad_kernel(form, pick_ref, left_ref, right_ref, *refs):
    total = dot(left_ref[...], right_ref[...], form)
    if len(refs) > 1:
        total = total + refs[0][...].astype(F32)
    refs[-1][...] = total.astype(BF16)


def weight_grad(left, right, pick, cols, tile, extra=None, form=NN):
    rows, depth = left.shape
    step = min(rows, 512)
    each = cols // tile
    left_spec = pl.BlockSpec((step, depth), lambda j, i, p: (i, 0))
    if form is NT:
        right_spec = pl.BlockSpec((tile, depth), lambda j, i, p: (p[0] * each + j, 0))
    else:
        right_spec = pl.BlockSpec((depth, tile), lambda j, i, p: (0, p[0] * each + j))
    out_spec = pl.BlockSpec((step, tile), lambda j, i, p: (i, j))
    in_specs = [left_spec, right_spec]
    operands = [left, right]
    if extra is not None:
        in_specs.append(out_spec)
        operands.append(extra)
    return pl.pallas_call(
        functools.partial(weight_grad_kernel, form),
        grid_spec=pltpu.PrefetchScalarGridSpec(
            num_scalar_prefetch=1,
            grid=(each, rows // step),
            in_specs=in_specs,
            out_specs=out_spec,
        ),
        out_shape=jax.ShapeDtypeStruct((rows, cols), BF16),
        compiler_params=VMEM_LIMIT,
        cost_estimate=cost(2 * rows * cols * depth),
        name="weight_grad",
    )(pick, *operands)


def swap_core(array):
    return lax.ppermute(array, "core", [(i, 1 - i) for i in range(2)])


def to_send(pieces, axis, dim):
    parts = lax.axis_size(axis)
    index = lax.axis_index(axis)
    return [
        lax.dynamic_index_in_dim(pieces, lax.rem(index + shift, parts), dim, keepdims=False)
        for shift in range(parts)
    ]


def send(pieces, axis):
    parts = lax.axis_size(axis)
    return pieces[:1] + [
        lax.ppermute(piece, axis, [(i, (i + shift) % parts) for i in range(parts)])
        for shift, piece in enumerate(pieces)
        if shift
    ]


def total(pieces):
    return sum(piece.astype(F32) for piece in pieces).astype(BF16)


def as_pieces(block):
    seq_parts, z_parts = lax.axis_size("seq"), lax.axis_size("z")
    return block.reshape(seq_parts, z_parts, 2, -1, block.shape[1])


def whole_rows(own, core):
    kept = lax.dynamic_index_in_dim(own, core, 0, keepdims=False)
    other = swap_core(lax.dynamic_index_in_dim(own, 1 - core, 0, keepdims=False))
    first = jnp.where(core == 0, kept, other)
    second = jnp.where(core == 0, other, kept)
    return first, second


def shifted_sum(array, parts, sign):
    total = jnp.zeros_like(array)
    for shift in range(1, parts):
        if sign > 0:
            pairs = [(i, i + shift) for i in range(parts - shift)]
        else:
            pairs = [(i + shift, i) for i in range(parts - shift)]
        total = total + lax.ppermute(array, "seq", pairs)
    return total


def body(
    inputs,
    targets,
    valid_count,
    gain_mix,
    w_query,
    w_key,
    w_value,
    w_out,
    gain_ffn,
    w_gate,
    w_up,
    w_down,
):
    everyone = ("seq", "z", "y", "core")
    seq_parts = lax.axis_size("seq")
    devices = lax.axis_size(everyone)
    seq_index = lax.axis_index("seq")
    batch_index = lax.axis_index(("z", "y", "core"))
    core = lax.axis_index("core")
    rows, width = inputs.shape[1:]
    hidden_units = w_gate.shape[1]
    padded = -(-hidden_units // 256) * 256
    owners = jnp.arange(valid_count.shape[0])
    count = jnp.sum(jnp.where(owners == batch_index, valid_count, 0))
    total_valid = jnp.sum(valid_count).astype(F32)
    valid_here = jnp.reshape(count - seq_index * rows, (1,))
    gains = jnp.pad(jnp.stack([gain_mix, gain_ffn], 1), ((0, 0), (0, 126)))
    early = gather_rows(jnp.concatenate([gains, w_query, w_key, w_value], 1))
    fill = ((0, 0), (0, padded - hidden_units))
    late = jnp.concatenate(
        [w_out, jnp.pad(w_gate, fill), jnp.pad(w_up, fill), jnp.pad(w_down, fill)], 1
    )
    late = lax.all_gather(late, everyone, axis=0, tiled=True)
    lead = HEADS * FEAT
    qkv, normed, flipped, gain_rows = project(inputs, early)
    tie = lax.optimization_barrier
    upper = HEADS // 2
    lower_state = local_state(qkv, 0, upper)
    lower_init = shifted_sum(lower_state, seq_parts, 1)
    qkv, lower_state = tie((qkv, lower_state))
    upper_init = shifted_sum(local_state(qkv, upper, upper), seq_parts, 1)
    filled = attention_forward(qkv, lower_init, 0, upper)
    mixed, den, saved = attention_forward(qkv, upper_init, upper, upper, filled)
    (
        result,
        normed_ffn,
        hidden,
        branch_back,
        both_back,
        attended_back,
        resid_back,
        mixed_back,
        squares,
    ) = feed_forward(valid_here, inputs, targets, mixed, gain_rows, late, padded)
    local_error = 0.5 * jnp.sum(squares)
    mine, others = jnp.reshape(core, (1,)), jnp.reshape(1 - core, (1,))
    half, out_half, qkv_cols = padded // 2, width // 2, HEADS * HROWS // 2

    high = lax.reduce_precision(local_error, 8, 7)
    middle = lax.reduce_precision(local_error - high, 8, 7)
    low = lax.reduce_precision(local_error - high - middle, 8, 7)
    column = lax.broadcasted_iota(jnp.int32, (width, -(-3 * devices // 128) * 128), 1)
    place = 3 * lax.axis_index(everyone)
    side = jnp.where(column == place, high, 0.0)
    side = jnp.where(column == place + 1, middle, side)
    side = jnp.where(column == place + 2, low, side).astype(BF16)

    nb, back = local_back_state(qkv, mixed_back, mixed, den)
    later = shifted_sum(back, seq_parts, -1)
    normed_ffn, nb = tie((normed_ffn, nb))
    gate_up_sent = weight_grad(normed_ffn, both_back, others, padded, half)
    gate_up_come = swap_core(gate_up_sent)
    branch_back, gate_up_sent = tie((branch_back, gate_up_sent))
    down_sent = weight_grad(branch_back, hidden, others, half, half)
    normed_ffn, down_sent = tie((normed_ffn, down_sent))
    gate_up = weight_grad(normed_ffn, both_back, mine, padded, half, gate_up_come)
    down_come = swap_core(down_sent)
    a_one = to_send(as_pieces(gate_up[:, :half]), "seq", 0)
    a_two = to_send(as_pieces(gate_up[:, half:]), "y", 2)
    mixed, a_one, a_two, later = tie((mixed, a_one, a_two, later))
    a_one, a_two = send(a_one, "seq"), send(a_two, "y")
    out_sent = weight_grad(mixed, attended_back, others, out_half, out_half)
    out_come = swap_core(out_sent)
    branch_back, out_sent = tie((branch_back, out_sent))
    down = weight_grad(branch_back, hidden, mine, half, half, down_come)
    mixed, down = tie((mixed, down))
    outer = weight_grad(mixed, attended_back, mine, out_half, out_half, out_come)
    block = jnp.concatenate([down, outer, side], 1)
    block, a_one, a_two = tie((block, a_one, a_two))
    own = w_query.shape[0]
    z_parts = lax.axis_size("z")
    one = total(a_one).reshape(z_parts, 2, 2, own, half)
    two = total(a_two).reshape(seq_parts, z_parts, 2, own, half)
    qkv_back, gate_up_pair, part = attention_backward(
        qkv, nb, saved, later, one, two, block, own
    )
    gate_sum, up_sum = gate_up_pair[0], gate_up_pair[1]
    if own % 16 == 0 and rows % 512 == 0:
        input_back, first_pair, pair = last_gradients(
            normed, qkv_back, flipped, inputs, resid_back, gain_rows, part, own
        )
    else:
        qkv_sent = weight_grad(normed, qkv_back, others, qkv_cols, qkv_cols, None, NT)
        qkv_come = swap_core(qkv_sent)
        c_all = weight_grad(normed, qkv_back, mine, qkv_cols, qkv_cols, qkv_come, NT)
        input_back, first_pair, pair = input_gradient(
            qkv_back, flipped, inputs, resid_back, gain_rows, c_all, part, own
        )
    down_sum = jnp.concatenate([pair[0, :, :half], pair[1, :, :half]], 1)
    out_sum = jnp.concatenate(
        [pair[0, :, half : half + out_half], pair[1, :, half : half + out_half]], 1
    )
    errors = pair[:, 0, half + out_half : half + out_half + 3 * devices].astype(F32)
    loss = 2.0 * jnp.sum(errors) / (width * total_valid)
    first, second = first_pair[0], first_pair[1]
    qkv_sum = jnp.concatenate([first, second], 1).astype(F32).reshape(own, HEADS, HROWS)
    grad_query = qkv_sum[:, :, :FEAT].reshape(own, lead)
    grad_key = qkv_sum[:, :, FEAT : 2 * FEAT].reshape(own, lead)
    grad_value = qkv_sum[:, :, 2 * FEAT :].reshape(own, HEADS * HEAD_DIM)
    grad_gate = gate_sum[:, :hidden_units].astype(F32)
    grad_up = up_sum[:, :hidden_units].astype(F32)

    def gain_grad(gain, *pairs):
        total = sum(jnp.sum(w.astype(F32) * grad, 1) for w, grad in pairs)
        return total / gain.astype(F32)

    return (
        result,
        loss,
        input_back,
        gain_grad(gain_mix, (w_query, grad_query), (w_key, grad_key), (w_value, grad_value)),
        grad_query,
        grad_key,
        grad_value,
        out_sum.astype(F32),
        gain_grad(gain_ffn, (w_gate, grad_gate), (w_up, grad_up)),
        grad_gate,
        grad_up,
        down_sum[:, :hidden_units].astype(F32),
    )


def solution(mesh):
    seq_parts, fsdp_parts = mesh.shape["seq"], mesh.shape["fsdp"]
    fine = jax.sharding.Mesh(
        mesh.devices.reshape(seq_parts, fsdp_parts // 4, 2, 2), ("seq", "z", "y", "core")
    )
    both = P(("seq", "z", "y", "core"))
    rows = P(("seq", "z", "y", "core"), None)
    tokens = P(("z", "y", "core"), "seq", None)
    return jax.shard_map(
        body,
        mesh=fine,
        in_specs=(tokens, tokens, P(), both, rows, rows, rows, rows, both, rows, rows, rows),
        out_specs=(tokens, P(), tokens, both, rows, rows, rows, rows, both, rows, rows, rows),
        check_vma=False,
    )
```

```python
import functools
import math

import jax
import jax.numpy as jnp
import numpy as np
from jax import lax
from jax.experimental import pallas as pl
from jax.experimental.pallas import tpu as pltpu
from jax.sharding import PartitionSpec as P

HEADS = 16
FEAT = 16
HEAD_DIM = 64
HROWS = 2 * FEAT + HEAD_DIM
CUT = 256
GROUPS = 11
FROWS = GROUPS * FEAT
VROWS = HEAD_DIM + 16
PAIR = 2 * VROWS
SENT = HEAD_DIM + 8
HG = 4
FIRST_BACK, SECOND_BACK = 4, 2

epsilon = 1e-05
F32 = jnp.float32
BF16 = jnp.bfloat16
NN = (((1,), (0,)), ((), ()))
NT = (((1,), (1,)), ((), ()))
TN = (((0,), (0,)), ((), ()))


def dot(left, right, dims):
    return lax.dot_general(left, right, dims, preferred_element_type=F32)


def first_row(rows, cols, count=1):
    return (lax.broadcasted_iota(jnp.int32, (rows, cols), 0) < count).astype(F32)


def rolled(u, shift):
    return pltpu.roll(u, (FEAT - shift) % FEAT, 0)


def phi_rows(u, const):
    groups = [u * u]
    for d in range(1, 9):
        groups.append(u * rolled(u, d))
    groups.append(u)
    groups.append(const)
    return jnp.concatenate([g.astype(BF16) for g in groups], 0)


def phi_pull(grad, u):
    total = grad[9 * FEAT : 10 * FEAT] + 2.0 * grad[0:FEAT] * u
    for d in range(1, 9):
        g = grad[d * FEAT : (d + 1) * FEAT]
        total = total + g * rolled(u, d) + rolled(g * u, FEAT - d)
    return total


def lane_scale():
    group = lax.broadcasted_iota(jnp.int32, (1, FROWS), 1) // FEAT
    scale = jnp.where((group == 0) | (group == 8), 1.0 / 32.0, 1.0 / 16.0)
    scale = jnp.where(group == 9, 0.25, scale)
    return jnp.where(group == 10, 1.0, scale)


def causal_mask():
    s = lax.broadcasted_iota(jnp.int32, (CUT, CUT), 0)
    t = lax.broadcasted_iota(jnp.int32, (CUT, CUT), 1)
    return s <= t


def split_pair(wide):
    high = wide.astype(BF16)
    return jnp.concatenate([high, (wide - high.astype(F32)).astype(BF16)], 0)


def twice(rows):
    return jnp.concatenate([rows, rows], 0)


def pack_states(sums, out_ref):
    fill = jnp.zeros((SENT, 2 * 128 - 2 * (FROWS - 128) - 128), F32)
    for i in range(len(sums) // 2):
        a, b = sums[2 * i][:SENT], sums[2 * i + 1][:SENT]
        out_ref[i, 0] = a[:, :128]
        out_ref[i, 1] = b[:, :128]
        out_ref[i, 2] = jnp.concatenate([a[:, 128:], b[:, 128:], fill], 1)


def unpack_states(packed_ref, state):
    side = FROWS - 128
    state[...] = jnp.zeros_like(state)
    for i in range(state.shape[0] // 2):
        for j in range(2):
            state[2 * i + j, :SENT, :128] = packed_ref[i, j]
            state[2 * i + j, :SENT, 128:] = packed_ref[i, 2][:, j * side : (j + 1) * side]


def state_kernel(blocks, qkv_ref, out_ref):
    ones2 = first_row(16, CUT, 2).astype(BF16)
    const = first_row(FEAT, CUT)

    def step(b, sums):
        cols = pl.ds(pl.multiple_of(b * CUT, CUT), CUT)
        fresh = []
        for h in range(HG):
            base = h * HROWS
            k = qkv_ref[base + FEAT : base + 2 * FEAT, cols].astype(F32)
            v = qkv_ref[base + 2 * FEAT : base + HROWS, cols]
            v_aug = jnp.concatenate([v, ones2], 0)
            fresh.append(sums[h] + dot(v_aug, phi_rows(k, const), NT))
        return tuple(fresh)

    zero = jnp.zeros((VROWS, FROWS), F32)
    sums = lax.fori_loop(0, blocks, step, (zero,) * HG)
    pack_states(sums, out_ref)


def forward_kernel(blocks, qkv_ref, init_ref, *refs):
    ones2 = first_row(16, CUT, 2).astype(BF16)
    const = first_row(FEAT, CUT)
    one_low = const.astype(BF16)
    mixed_ref, den_ref, saved_ref, state = refs[-4:]
    scale = 2.0 * lane_scale()
    mask = causal_mask()
    unpack_states(init_ref, state)

    def step(b, carry):
        cols = pl.ds(pl.multiple_of(b * CUT, CUT), CUT)
        for h in range(HG):
            base = h * HROWS
            q = qkv_ref[base : base + FEAT, cols]
            k = qkv_ref[base + FEAT : base + 2 * FEAT, cols]
            v = qkv_ref[base + 2 * FEAT : base + HROWS, cols]
            v_aug = jnp.concatenate([v, ones2], 0)
            k_aug = jnp.concatenate([k, one_low], 0)
            q_aug = jnp.concatenate([q * 0.25, one_low], 0)
            u = dot(k_aug, q_aug, TN)
            weight = jnp.where(mask, u * u + 1.0, 0.0).astype(BF16)
            low = split_pair(state[h] * scale)
            saved_ref[h, b] = low
            earlier = dot(low, phi_rows(q.astype(F32), const), NN)
            numer = dot(v_aug, weight, NN) + (earlier[:VROWS] + earlier[VROWS:])
            den = numer[HEAD_DIM : HEAD_DIM + 1]
            rows = slice(h * HEAD_DIM, (h + 1) * HEAD_DIM)
            mixed_ref[rows, cols] = (numer[:HEAD_DIM] * (1.0 / den)).astype(BF16)
            den_ref[0, h : h + 1, cols] = 0.5 * den
            state[h] += dot(v_aug, phi_rows(k.astype(F32), const), NT)
        return carry

    lax.fori_loop(0, blocks, step, 0)


def back_state_kernel(blocks, qkv_ref, grad_ref, mixed_ref, den_ref, nb_ref, out_ref):
    const = first_row(FEAT, CUT)
    row = lax.broadcasted_iota(jnp.int32, (16, CUT), 0)

    def step(b, sums):
        cols = pl.ds(pl.multiple_of(b * CUT, CUT), CUT)
        fresh = []
        for h in range(HG):
            base = h * HROWS
            q = qkv_ref[base : base + FEAT, cols].astype(F32)
            rows = slice(h * HEAD_DIM, (h + 1) * HEAD_DIM)
            g = grad_ref[rows, cols].astype(F32)
            inverse = 1.0 / den_ref[0, h : h + 1, cols]
            db = -inverse * jnp.sum(
                g * mixed_ref[rows, cols].astype(F32), axis=0, keepdims=True
            )
            nb = (g * inverse).astype(BF16)
            high = db.astype(BF16).astype(F32)
            tail = jnp.where(row == 0, high, jnp.where(row == 1, db - high, 0.0)).astype(BF16)
            nb_aug = jnp.concatenate([nb, tail], 0)
            nb_ref[h, :, cols] = nb_aug
            fresh.append(sums[h] + dot(nb_aug, phi_rows(q, const), NT))
        return tuple(fresh)

    zero = jnp.zeros((VROWS, FROWS), F32)
    sums = lax.fori_loop(0, blocks, step, (zero,) * HG)
    pack_states(sums, out_ref)


def backward_kernel(
    sizes,
    blocks,
    qkv_ref,
    nb_ref,
    saved_ref,
    init_ref,
    wide_ref,
    one_ref,
    two_ref,
    block_ref,
    out_ref,
    pair_out,
    part_out,
    state,
    *refs,
):
    ones2 = first_row(16, CUT, 2).astype(BF16)
    const = first_row(FEAT, CUT)
    one_low = const.astype(BF16)
    scale = lane_scale()
    mask = causal_mask()
    halves = pl.num_programs(1)
    at = pl.program_id(0) * halves + pl.program_id(1)
    last = pl.num_programs(0) * halves - 1
    each = blocks // halves
    by_seq, by_z, by_y, by_core = neighbours(sizes)
    count = 8 + 8
    first = RowSums(sizes, wide_ref, refs[:count], pair_out, (one_ref, two_ref))
    refs = refs[count:]
    second = RowSums(sizes, block_ref, refs[:6] + (part_out,) + refs[6:])

    @pl.when(at == 0)
    def _():
        greet(by_seq + by_z + [by_y, by_core])
        first.second()
        second.start()

    @pl.when(pl.program_id(1) == 0)
    def _():
        unpack_states(init_ref, state)

    def step(i, carry):
        b = blocks - 1 - (pl.program_id(1) * each + i)
        cols = pl.ds(pl.multiple_of(b * CUT, CUT), CUT)
        for h in range(HG):
            base = h * HROWS
            q = qkv_ref[base : base + FEAT, cols]
            k = qkv_ref[base + FEAT : base + 2 * FEAT, cols]
            v = qkv_ref[base + 2 * FEAT : base + HROWS, cols]
            qf = q.astype(F32)
            kf = k.astype(F32)
            q4 = q * 0.25
            nb = nb_ref[h, :, cols]
            v_aug = jnp.concatenate([v, ones2], 0)
            k_aug = jnp.concatenate([k, one_low], 0)
            q_aug = jnp.concatenate([q4, one_low], 0)
            u = dot(k_aug, q_aug, TN)
            weight = jnp.where(mask, u * u + 1.0, 0.0).astype(BF16)
            wb = dot(v_aug, nb, TN)
            sb = jnp.where(mask, wb * u, 0.0).astype(BF16)
            q_feat_back = dot(saved_ref[h, b], twice(nb), TN)
            dq = 0.25 * dot(k, sb, NN) + 0.5 * phi_pull(q_feat_back, qf)
            low = split_pair(state[h] * scale)
            k_feat_back = dot(low, twice(v_aug), TN)
            later = dot(low, phi_rows(kf, const), NN)
            dk = dot(q4, sb, NT) + phi_pull(k_feat_back, kf)
            dv = 0.5 * dot(nb[:HEAD_DIM], weight, NT) + (
                later[:HEAD_DIM] + later[VROWS : VROWS + HEAD_DIM]
            )
            out_ref[base : base + FEAT, cols] = dq.astype(BF16)
            out_ref[base + FEAT : base + 2 * FEAT, cols] = dk.astype(BF16)
            out_ref[base + 2 * FEAT : base + HROWS, cols] = dv.astype(BF16)
            state[h] += dot(nb, phi_rows(qf, const), NT)
        return carry

    lax.fori_loop(0, each, step, 0)

    @pl.when(at == last - FIRST_BACK)
    def _():
        first.third()

    @pl.when(at == last - SECOND_BACK)
    def _():
        second.second()

    @pl.when(at == last)
    def _():
        second.third()
        first.fourth()
        second.finish()
        first.finish()


def cost(flops):
    return pl.CostEstimate(flops=int(flops * 0.02), bytes_accessed=0, transcendentals=0)


def head_spec(rows, cols):
    return pl.BlockSpec((HG * rows, cols), lambda g: (g, 0))


def lead_spec(*tail):
    return pl.BlockSpec((HG,) + tail, lambda g: (g,) + (0,) * len(tail))


VMEM_LIMIT = pltpu.CompilerParams(vmem_limit_bytes=56 * 1024 * 1024)


def packed_shape(heads):
    return jax.ShapeDtypeStruct((heads // 2, 3, SENT, 128), F32)


def packed_spec():
    return pl.BlockSpec((HG // 2, 3, SENT, 128), lambda g: (g, 0, 0, 0))


def local_state(qkv, start, count):
    cols = qkv.shape[1]
    first = start // HG
    return pl.pallas_call(
        functools.partial(state_kernel, cols // CUT),
        grid=(count // HG,),
        in_specs=[pl.BlockSpec((HG * HROWS, cols), lambda g: (first + g, 0))],
        out_specs=packed_spec(),
        out_shape=packed_shape(count),
        compiler_params=VMEM_LIMIT,
        cost_estimate=cost(11e9 * cols / 2048 * count / HEADS),
        name="key_state",
    )(qkv)


def attention_forward(qkv, init, start, count, filled=()):
    cols = qkv.shape[1]
    blocks = cols // CUT
    first = start // HG

    def head_rows(rows):
        return pl.BlockSpec((HG * rows, cols), lambda g: (first + g, 0))

    def lead(*tail):
        return pl.BlockSpec((HG,) + tail, lambda g: (first + g,) + (0,) * len(tail))

    return pl.pallas_call(
        functools.partial(forward_kernel, blocks),
        grid=(count // HG,),
        in_specs=[head_rows(HROWS), packed_spec()]
        + [pl.BlockSpec(memory_space=pl.ANY)] * len(filled),
        out_specs=[
            head_rows(HEAD_DIM),
            pl.BlockSpec((1, HG, cols), lambda g: (first + g, 0, 0)),
            lead(blocks, PAIR, FROWS),
        ],
        out_shape=[
            jax.ShapeDtypeStruct((HEADS * HEAD_DIM, cols), BF16),
            jax.ShapeDtypeStruct((HEADS // HG, HG, cols), F32),
            jax.ShapeDtypeStruct((HEADS, blocks, PAIR, FROWS), BF16),
        ],
        scratch_shapes=[pltpu.VMEM((HG, VROWS, FROWS), F32)],
        compiler_params=VMEM_LIMIT,
        cost_estimate=cost(36e9 * cols / 2048 * count / HEADS),
        input_output_aliases={2 + i: i for i in range(len(filled))},
        name="attend",
    )(qkv, init, *filled)


def local_back_state(qkv, grad, mixed, den):
    cols = qkv.shape[1]
    return pl.pallas_call(
        functools.partial(back_state_kernel, cols // CUT),
        grid=(HEADS // HG,),
        in_specs=[
            head_spec(HROWS, cols),
            head_spec(HEAD_DIM, cols),
            head_spec(HEAD_DIM, cols),
            pl.BlockSpec((1, HG, cols), lambda g: (g, 0, 0)),
        ],
        out_specs=[lead_spec(VROWS, cols), packed_spec()],
        out_shape=[
            jax.ShapeDtypeStruct((HEADS, VROWS, cols), BF16),
            packed_shape(HEADS),
        ],
        compiler_params=VMEM_LIMIT,
        cost_estimate=cost(13e9 * cols / 2048),
        name="query_state",
    )(qkv, grad, mixed, den)


def attention_backward(qkv, nb, saved, init, wide, one, two, block, own):
    cols = qkv.shape[1]
    blocks = cols // CUT
    sizes = lax.axis_size("seq"), lax.axis_size("z")
    width = block.shape[-1]
    cut = 128 * (width // 256)
    first_buffers, first_sems = row_sum_scratch(
        sizes, own, one.shape[-1], two.shape[-1], summed=True
    )
    second_buffers, second_sems = row_sum_scratch(
        sizes, own, cut, width - cut, ends=False, keep=False
    )

    def head_rows(rows):
        return pl.BlockSpec((HG * rows, cols), lambda g, p: (g, 0))

    def lead(*tail):
        return pl.BlockSpec((HG,) + tail, lambda g, p: (g,) + (0,) * len(tail))

    here = pl.BlockSpec(memory_space=pltpu.VMEM)
    return pl.pallas_call(
        functools.partial(backward_kernel, sizes, blocks),
        grid=(HEADS // HG, 2),
        in_specs=[
            head_rows(HROWS),
            lead(VROWS, cols),
            lead(blocks, PAIR, FROWS),
            pl.BlockSpec((HG // 2, 3, SENT, 128), lambda g, p: (g, 0, 0, 0)),
            here,
            here,
            here,
            here,
        ],
        out_specs=[head_rows(HROWS), here, here],
        out_shape=[
            jax.ShapeDtypeStruct((HEADS * HROWS, cols), BF16),
            jax.ShapeDtypeStruct((2, own, wide.shape[-1]), BF16),
            jax.ShapeDtypeStruct((sizes[1], 2, own, width), BF16),
        ],
        scratch_shapes=[pltpu.VMEM((HG, VROWS, FROWS), F32)]
        + first_buffers
        + first_sems
        + second_buffers
        + second_sems,
        compiler_params=pltpu.CompilerParams(
            collective_id=2, has_side_effects=True, vmem_limit_bytes=58 * 1024 * 1024
        ),
        cost_estimate=cost(53e9 * cols / 2048),
        name="attend_back",
    )(
        qkv,
        nb,
        saved,
        init,
        wide.reshape(sizes + (2, 2, own, wide.shape[-1])),
        one,
        two,
        block.reshape(sizes + (2, 2, own, width)),
    )


MESH = pl.DeviceIdType.MESH


def gather_kernel(shape, split, shard_ref, out_ref, local_sem, *sems):
    seq_parts, z_parts = shape
    s, z = lax.axis_index("seq"), lax.axis_index("z")
    y, c = lax.axis_index("y"), lax.axis_index("core")
    cols = shard_ref.shape[1]
    left, right = pl.ds(0, split), pl.ds(split, cols - split)
    every = slice(None)

    def peer(ds=0, dz=0, dy=0, dc=0):
        return (
            lax.rem(s + ds, seq_parts),
            lax.rem(z + dz, z_parts),
            lax.rem(y + dy, 2),
            lax.rem(c + dc, 2),
        )

    def send(kind, slot, src, dst, device):
        return pltpu.make_async_remote_copy(
            src_ref=src,
            dst_ref=dst,
            send_sem=sems[2 * kind].at[slot],
            recv_sem=sems[2 * kind + 1].at[slot],
            device_id=device,
            device_id_type=MESH,
        )

    barrier = pltpu.get_barrier_semaphore()
    peers = [peer(ds=j) for j in range(1, seq_parts)]
    peers += [peer(dz=k) for k in range(1, z_parts)]
    peers += [peer(dy=1), peer(dc=1)]
    for device in peers:
        pl.semaphore_signal(barrier, inc=1, device_id=device, device_id_type=MESH)
    own = pltpu.make_async_copy(shard_ref, out_ref.at[s, z, y, c], local_sem)
    own.start()
    pl.semaphore_wait(barrier, len(peers))

    order = [0] + sorted(range(1, z_parts), key=lambda k: min(k, z_parts - k))
    slab = {k: lax.rem(z + z_parts - k, z_parts) for k in order}
    along = {
        k: send(0, k, shard_ref, out_ref.at[s, z, y, c], peer(dz=k)) for k in order[1:]
    }
    for k in order[1:]:
        along[k].start()
    own.wait()
    first_y, first_x = {}, {}
    for k in order:
        if k:
            along[k].wait_recv()
        at = out_ref.at[s, slab[k], y, c, :, left]
        first_y[k] = send(1, k, at, at, peer(dy=1))
        first_y[k].start()
        at = out_ref.at[s, slab[k], y, c, :, right]
        first_x[k] = [
            send(2, k * seq_parts + j, at, at, peer(ds=j)) for j in range(1, seq_parts)
        ]
        for copy in first_x[k]:
            copy.start()
    then_x, then_y, across = {}, {}, {}
    for k in order:
        first_y[k].wait_recv()
        at = out_ref.at[s, slab[k], :, c, :, left]
        then_x[k] = [
            send(3, k * seq_parts + j, at, at, peer(ds=j)) for j in range(1, seq_parts)
        ]
        for copy in then_x[k]:
            copy.start()
        for copy in first_x[k]:
            copy.wait_recv()
        at = out_ref.at[:, slab[k], y, c, :, right]
        then_y[k] = send(4, k, at, at, peer(dy=1))
        then_y[k].start()
    for k in order:
        for copy in then_x[k]:
            copy.wait_recv()
        then_y[k].wait_recv()
        at = out_ref.at[:, slab[k], :, c]
        across[k] = send(5, k, at, at, peer(dc=1))
        across[k].start()
    for k in order:
        across[k].wait_recv()
    for k in order:
        if k:
            along[k].wait_send()
        first_y[k].wait_send()
        then_y[k].wait_send()
        across[k].wait_send()
        for copy in first_x[k] + then_x[k]:
            copy.wait_send()


def gather_rows(shard):
    own, cols = shard.shape
    seq_parts, z_parts = lax.axis_size("seq"), lax.axis_size("z")
    split = cols // 256 * 128
    counts = (z_parts, z_parts, z_parts * seq_parts, z_parts * seq_parts, z_parts, z_parts)
    out = pl.pallas_call(
        functools.partial(gather_kernel, (seq_parts, z_parts), split),
        in_specs=[pl.BlockSpec(memory_space=pl.ANY)],
        out_specs=pl.BlockSpec(memory_space=pl.ANY),
        out_shape=jax.ShapeDtypeStruct((seq_parts, z_parts, 2, 2, own, cols), BF16),
        scratch_shapes=[pltpu.SemaphoreType.DMA]
        + [pltpu.SemaphoreType.DMA((n,)) for n in counts for _ in range(2)],
        compiler_params=pltpu.CompilerParams(collective_id=0, has_side_effects=True),
        cost_estimate=cost(25e9),
        name="gather_rows",
    )(shard)
    return out.reshape(-1, cols)


def project_kernel(tokens_ref, weight_ref, qkv_ref, normed_ref, flipped_ref, gain_ref):
    width = tokens_ref.shape[2]
    lead = HEADS * FEAT

    @pl.when(pl.program_id(0) == 0)
    def _():
        gain_ref[...] = weight_ref[:, :128].astype(F32).T[:8]
        for c in range(HEADS * HROWS // 128):
            piece = weight_ref[:, 128 * (c + 1) : 128 * (c + 2)].T
            start = 128 * c
            if start < 2 * lead:
                each, first = FEAT, FEAT * (start // lead)
                head = (start % lead) // FEAT
            else:
                each, first = HEAD_DIM, 2 * FEAT
                head = (start - 2 * lead) // HEAD_DIM
            for j in range(128 // each):
                at = (head + j) * HROWS + first
                flipped_ref[at : at + each, :] = piece[j * each : (j + 1) * each]

    tokens = tokens_ref[0].astype(F32)
    scale = lax.rsqrt(jnp.sum(tokens * tokens, -1, keepdims=True) * (1.0 / width) + epsilon)
    normed = (tokens * scale * gain_ref[0:1]).astype(BF16)
    normed_ref[...] = normed.T
    qkv_ref[...] = dot(flipped_ref[...], normed, NT).astype(BF16)


def project(tokens, early):
    rows, width = tokens.shape[1:]
    tile = min(rows, 512)
    return pl.pallas_call(
        project_kernel,
        grid=(rows // tile,),
        in_specs=[
            pl.BlockSpec((1, tile, width), lambda i: (0, i, 0)),
            pl.BlockSpec(
                (width, 128 + HEADS * HROWS), lambda i: (0, 0), pipeline_mode=pl.Buffered(1)
            ),
        ],
        out_specs=[
            pl.BlockSpec((HEADS * HROWS, tile), lambda i: (0, i)),
            pl.BlockSpec((width, tile), lambda i: (0, i)),
            pl.BlockSpec((HEADS * HROWS, width), lambda i: (0, 0)),
            pl.BlockSpec((8, width), lambda i: (0, 0)),
        ],
        out_shape=[
            jax.ShapeDtypeStruct((HEADS * HROWS, rows), BF16),
            jax.ShapeDtypeStruct((width, rows), BF16),
            jax.ShapeDtypeStruct((HEADS * HROWS, width), BF16),
            jax.ShapeDtypeStruct((8, width), F32),
        ],
        compiler_params=VMEM_LIMIT,
        cost_estimate=cost(2 * HEADS * HROWS * rows * width),
        name="project",
    )(tokens, early)


def remote(src, dst, sems, slot, device):
    return pltpu.make_async_remote_copy(
        src_ref=src,
        dst_ref=dst,
        send_sem=sems[0].at[slot],
        recv_sem=sems[1].at[slot],
        device_id=device,
        device_id_type=MESH,
    )


def positions():
    return tuple(lax.axis_index(name) for name in ("seq", "z", "y", "core"))


def neighbours(sizes):
    seq_parts, z_parts = sizes
    s, z, y, c = positions()
    by_seq = [(lax.rem(s + j, seq_parts), z, y, c) for j in range(1, seq_parts)]
    by_z = [(s, lax.rem(z + k, z_parts), y, c) for k in range(1, z_parts)]
    return by_seq, by_z, (s, z, 1 - y, c), (s, z, y, 1 - c)


def greet(devices):
    barrier = pltpu.get_barrier_semaphore()
    for device in devices:
        pl.semaphore_signal(barrier, inc=1, device_id=device, device_id_type=MESH)
    pl.semaphore_wait(barrier, len(devices))


class RowSums:
    def __init__(self, sizes, source, refs, out_ref=None, arrived=None):
        seq_parts, z_parts = self.sizes = sizes
        s, z, y, c = self.place = positions()
        by_seq, by_z, by_y, by_core = neighbours(sizes)
        self.source, self.summed, self.out_ref = source, arrived is not None, out_ref
        refs = list(refs)
        self.x_sum, self.y_sum = refs[:2]
        del refs[:2]
        if arrived is None:
            arrived = refs[:2]
            del refs[:2]
        self.x_in, self.y_in = arrived
        self.then_y_in, self.then_x_in, self.row_sum = refs[:3]
        del refs[:3]
        self.cut = self.x_sum.shape[-1]
        rest = self.y_sum.shape[-1]
        if out_ref is not None:
            self.z_in, self.own_sum, self.swapped = refs[:3]
            del refs[:3]
        pairs = [refs[2 * i : 2 * i + 2] for i in range(len(refs) // 2)]
        others = range(1, seq_parts)
        self.first = []
        if not self.summed:
            left, right = pl.ds(0, self.cut), pl.ds(self.cut, rest)
            self.first_x = [
                remote(
                    source.at[lax.rem(s + j, seq_parts), :, :, :, :, left],
                    self.x_in.at[j - 1],
                    pairs[2],
                    j - 1,
                    by_seq[j - 1],
                )
                for j in others
            ]
            self.first_y = remote(
                source.at[:, :, 1 - y, :, :, right], self.y_in, pairs[3], 0, by_y
            )
            self.first = self.first_x + [self.first_y]
        self.then_y = remote(self.x_sum.at[:, 1 - y], self.then_y_in, pairs[0], 0, by_y)
        self.then_x = [
            remote(
                self.y_sum.at[lax.rem(s + j, seq_parts)],
                self.then_x_in.at[j - 1],
                pairs[1],
                j - 1,
                by_seq[j - 1],
            )
            for j in others
        ]
        if out_ref is not None:
            self.along = along_z(sizes, self.row_sum, self.z_in, pairs[-2])
            self.across = remote(self.own_sum.at[1 - c], self.swapped, pairs[-1], 0, by_core)

    def start(self):
        for copy in self.first:
            copy.start()

    def second(self):
        s, z, y, c = self.place
        if not self.summed:
            for copy in self.first_x:
                copy.wait_recv()
        total = self.source[s, :, :, :, :, : self.cut].astype(F32)
        for j in range(self.sizes[0] - 1):
            total = total + self.x_in[j].astype(F32)
        self.x_sum[...] = total.astype(BF16)
        self.then_y.start()
        if not self.summed:
            self.first_y.wait_recv()
        total = self.source[:, :, y, :, :, self.cut :].astype(F32)
        self.y_sum[...] = (total + self.y_in[...].astype(F32)).astype(BF16)
        for copy in self.then_x:
            copy.start()

    def third(self):
        s, z, y, c = self.place
        self.then_y.wait_recv()
        total = self.x_sum[:, y].astype(F32) + self.then_y_in[...].astype(F32)
        self.row_sum[:, :, :, : self.cut] = total.astype(BF16)
        for copy in self.then_x:
            copy.wait_recv()
        total = self.y_sum[s].astype(F32)
        for j in range(self.sizes[0] - 1):
            total = total + self.then_x_in[j].astype(F32)
        self.row_sum[:, :, :, self.cut :] = total.astype(BF16)
        if self.out_ref is not None:
            for copy in self.along:
                copy.start()

    def fourth(self):
        sum_z(self.along, self.row_sum, self.z_in, self.own_sum)
        self.across.start()
        c = self.place[3]
        self.out_ref[c] = self.own_sum[c]

    def finish(self):
        for copy in self.first + [self.then_y] + self.then_x:
            copy.wait_send()
        if self.out_ref is not None:
            self.across.wait_recv()
            self.out_ref[1 - self.place[3]] = self.swapped[...]
            self.across.wait_send()
            for copy in self.along:
                copy.wait_send()


def along_z(sizes, source, z_in, sems):
    z_parts = sizes[1]
    z = positions()[1]
    by_z = neighbours(sizes)[1]
    return [
        remote(source.at[lax.rem(z + k, z_parts)], z_in.at[k - 1], sems, k - 1, by_z[k - 1])
        for k in range(1, z_parts)
    ]


def sum_z(copies, source, z_in, own_sum):
    for copy in copies:
        copy.wait_recv()
    total = source[positions()[1]].astype(F32)
    for k in range(len(copies)):
        total = total + z_in[k].astype(F32)
    own_sum[...] = total.astype(BF16)


def row_sum_scratch(sizes, own, cut, rest, summed=False, ends=True, keep=True):
    seq_parts, z_parts = sizes
    cols = cut + rest

    def low(*shape):
        return pltpu.VMEM(shape, BF16)

    buffers = [low(z_parts, 2, 2, own, cut), low(seq_parts, z_parts, 2, own, rest)]
    if not summed:
        buffers += [
            low(seq_parts - 1, z_parts, 2, 2, own, cut),
            low(seq_parts, z_parts, 2, own, rest),
        ]
    buffers += [low(z_parts, 2, own, cut), low(seq_parts - 1, z_parts, 2, own, rest)]
    if keep:
        buffers += [low(z_parts, 2, own, cols)]
    counts = [1, seq_parts - 1]
    if not summed:
        counts += [seq_parts - 1, 1]
    if ends:
        buffers += [low(z_parts - 1, 2, own, cols), low(2, own, cols), low(own, cols)]
        counts += [z_parts - 1, 1]
    return buffers, [pltpu.SemaphoreType.DMA((n,)) for n in counts for _ in range(2)]


def input_kernel(
    sizes,
    back_ref,
    flipped_ref,
    tokens_ref,
    resid_ref,
    gain_ref,
    block_ref,
    part_ref,
    out_ref,
    block_out,
    part_out,
    part_z_in,
    part_sum,
    part_swapped,
    z_send,
    z_recv,
    core_send,
    core_recv,
    *refs,
):
    step = pl.program_id(0)
    last = pl.num_programs(0) - 1
    c = positions()[3]
    by_seq, by_z, by_y, by_core = neighbours(sizes)
    sums = RowSums(sizes, block_ref, refs, block_out)
    part_along = along_z(sizes, part_ref, part_z_in, (z_send, z_recv))
    part_across = remote(
        part_sum.at[1 - c], part_swapped, (core_send, core_recv), 0, by_core
    )

    @pl.when(step == 0)
    def _():
        greet(by_seq + by_z + [by_y, by_core])
        for copy in part_along:
            copy.start()
        sums.start()

    width = tokens_ref.shape[2]
    tokens = tokens_ref[0].astype(F32)
    scale = lax.rsqrt(jnp.sum(tokens * tokens, -1, keepdims=True) * (1.0 / width) + epsilon)
    unit = tokens * scale
    normed_back = dot(back_ref[...], flipped_ref[...], TN)
    scaled = normed_back * gain_ref[0:1]
    middle = jnp.sum(scaled * unit, -1, keepdims=True) * (1.0 / width)
    out_ref[0] = resid_ref[...] + scale * (scaled - unit * middle)

    @pl.when(step == last - 2)
    def _():
        sums.second()

    @pl.when(step == last - 1)
    def _():
        sums.third()

    @pl.when(step == last)
    def _():
        sum_z(part_along, part_ref, part_z_in, part_sum)
        part_across.start()
        part_out[c] = part_sum[c]
        sums.fourth()
        part_across.wait_recv()
        part_out[1 - c] = part_swapped[...]
        sums.finish()
        for copy in part_along:
            copy.wait_send()
        part_across.wait_send()


def input_gradient(back, flipped, tokens, resid_back, gain, block, part, own):
    rows, width = tokens.shape[1:]
    tile = min(rows // 4, 512)
    sizes = lax.axis_size("seq"), lax.axis_size("z")
    cols, part_cols = block.shape[-1], part.shape[-1]
    cut = 128 * (cols // 256)
    buffers, sems = row_sum_scratch(sizes, own, cut, cols - cut)
    return pl.pallas_call(
        functools.partial(input_kernel, sizes),
        grid=(rows // tile,),
        in_specs=[
            pl.BlockSpec((HEADS * HROWS, tile), lambda i: (0, i)),
            pl.BlockSpec(flipped.shape, lambda i: (0, 0), pipeline_mode=pl.Buffered(1)),
            pl.BlockSpec((1, tile, width), lambda i: (0, i, 0)),
            pl.BlockSpec((tile, width), lambda i: (i, 0)),
            pl.BlockSpec((8, width), lambda i: (0, 0)),
            pl.BlockSpec(memory_space=pltpu.VMEM),
            pl.BlockSpec(memory_space=pltpu.VMEM),
        ],
        out_specs=[
            pl.BlockSpec((1, tile, width), lambda i: (0, i, 0)),
            pl.BlockSpec(memory_space=pltpu.VMEM),
            pl.BlockSpec(memory_space=pltpu.VMEM),
        ],
        out_shape=[
            jax.ShapeDtypeStruct((1, rows, width), F32),
            jax.ShapeDtypeStruct((2, own, cols), BF16),
            jax.ShapeDtypeStruct((2, own, part_cols), BF16),
        ],
        scratch_shapes=[
            pltpu.VMEM((sizes[1] - 1, 2, own, part_cols), BF16),
            pltpu.VMEM((2, own, part_cols), BF16),
            pltpu.VMEM((own, part_cols), BF16),
            pltpu.SemaphoreType.DMA((sizes[1] - 1,)),
            pltpu.SemaphoreType.DMA((sizes[1] - 1,)),
            pltpu.SemaphoreType.DMA((1,)),
            pltpu.SemaphoreType.DMA((1,)),
        ]
        + buffers
        + sems,
        compiler_params=pltpu.CompilerParams(
            collective_id=1, has_side_effects=True, vmem_limit_bytes=56 * 1024 * 1024
        ),
        cost_estimate=cost(4 * HEADS * HROWS * rows * width),
        name="input_gradient",
    )(
        back,
        flipped,
        tokens,
        resid_back,
        gain,
        block.reshape(sizes + (2, 2, own, cols)),
        part,
    )


def last_kernel(
    sizes,
    normed_ref,
    back_ref,
    flipped_ref,
    tokens_ref,
    resid_ref,
    gain_ref,
    part_ref,
    out_ref,
    block_out,
    part_out,
    sent,
    come,
    block,
    part_z_in,
    part_sum,
    part_swapped,
    half_send,
    half_recv,
    z_send,
    z_recv,
    core_send,
    core_recv,
    *refs,
):
    step = pl.program_id(0)
    c = positions()[3]
    by_seq, by_z, by_y, by_core = neighbours(sizes)
    sums = RowSums(sizes, block, refs, block_out)
    part_along = along_z(sizes, part_ref, part_z_in, (z_send, z_recv))
    part_across = remote(
        part_sum.at[1 - c], part_swapped, (core_send, core_recv), 0, by_core
    )
    half = remote(sent, come, (half_send, half_recv), 0, by_core)
    cols = sent.shape[1]
    each = sent.shape[0] // sizes[0]
    tile, width = tokens_ref.shape[1:]

    def gradient(s, which):
        rows = pl.ds(pl.multiple_of(which * cols, 16), cols)
        return dot(normed_ref[s * each : (s + 1) * each, :], back_ref[rows, :], NT)

    @pl.when(step == 0)
    def _():
        greet(by_seq + by_z + [by_y, by_core])
        for copy in part_along:
            copy.start()
        for s in range(sizes[0]):
            sent[s * each : (s + 1) * each, :] = gradient(s, 1 - c).astype(BF16)
        half.start()

    @pl.when(step == 2)
    def _():
        half.wait_recv()
        for s in range(sizes[0]):
            total = gradient(s, c) + come[s * each : (s + 1) * each, :].astype(F32)
            block[s] = total.astype(BF16).reshape(block.shape[1:])
        sums.start()

    @pl.when((step == 1) | (step > 2))
    def _():
        at = pl.multiple_of(step // 3 * (step - 2) * tile, 128)
        tokens = tokens_ref[0].astype(F32)
        scale = lax.rsqrt(
            jnp.sum(tokens * tokens, -1, keepdims=True) * (1.0 / width) + epsilon
        )
        unit = tokens * scale
        normed_back = dot(back_ref[:, pl.ds(at, tile)], flipped_ref[...], TN)
        scaled = normed_back * gain_ref[0:1]
        middle = jnp.sum(scaled * unit, -1, keepdims=True) * (1.0 / width)
        out_ref[0] = resid_ref[...] + scale * (scaled - unit * middle)

    @pl.when(step == 4)
    def _():
        sums.second()

    @pl.when(step == 5)
    def _():
        sums.third()
        sum_z(part_along, part_ref, part_z_in, part_sum)
        part_across.start()
        part_out[c] = part_sum[c]
        sums.fourth()
        part_across.wait_recv()
        part_out[1 - c] = part_swapped[...]
        sums.finish()
        for copy in part_along:
            copy.wait_send()
        part_across.wait_send()
        half.wait_send()


def last_gradients(normed, back, flipped, tokens, resid_back, gain, part, own):
    rows, width = tokens.shape[1:]
    tile = rows // 4
    sizes = lax.axis_size("seq"), lax.axis_size("z")
    cols, part_cols = HEADS * HROWS // 2, part.shape[-1]
    cut = 128 * (cols // 256)
    buffers, sems = row_sum_scratch(sizes, own, cut, cols - cut)
    here = pl.BlockSpec(memory_space=pltpu.VMEM)

    def place(i):
        return i // 3 * (i - 2)

    def low(*shape):
        return pltpu.VMEM(shape, BF16)

    one, many = pltpu.SemaphoreType.DMA((1,)), pltpu.SemaphoreType.DMA((sizes[1] - 1,))
    return pl.pallas_call(
        functools.partial(last_kernel, sizes),
        grid=(6,),
        in_specs=[
            here,
            here,
            here,
            pl.BlockSpec((1, tile, width), lambda i: (0, place(i), 0)),
            pl.BlockSpec((tile, width), lambda i: (place(i), 0)),
            pl.BlockSpec((8, width), lambda i: (0, 0)),
            here,
        ],
        out_specs=[pl.BlockSpec((1, tile, width), lambda i: (0, place(i), 0)), here, here],
        out_shape=[
            jax.ShapeDtypeStruct((1, rows, width), F32),
            jax.ShapeDtypeStruct((2, own, cols), BF16),
            jax.ShapeDtypeStruct((2, own, part_cols), BF16),
        ],
        scratch_shapes=[
            low(width, cols),
            low(width, cols),
            low(*sizes, 2, 2, own, cols),
            low(sizes[1] - 1, 2, own, part_cols),
            low(2, own, part_cols),
            low(own, part_cols),
            one,
            one,
            many,
            many,
            one,
            one,
        ]
        + buffers
        + sems,
        compiler_params=pltpu.CompilerParams(
            collective_id=3, has_side_effects=True, vmem_limit_bytes=56 * 1024 * 1024
        ),
        cost_estimate=cost(8 * HEADS * HROWS * rows * width),
        name="last_gradients",
    )(normed, back, flipped, tokens, resid_back, gain, part)


def ffn_kernel(
    padded,
    count_ref,
    tokens_ref,
    target_ref,
    mixed_ref,
    gain_ref,
    late_ref,
    result_ref,
    normed_ref,
    hidden_ref,
    branch_ref,
    both_ref,
    attended_ref,
    resid_back_ref,
    mixed_back_ref,
    side_ref,
    error_ref,
    w_out,
    w_gate,
    w_up,
    w_down,
    slope,
    active,
    sems,
):
    step = pl.program_id(0)
    tile, width = tokens_ref.shape[1:]
    starts = (0, width, width + padded, width + 2 * padded)
    copies = [
        pltpu.make_async_copy(
            late_ref.at[:, pl.ds(start, held.shape[1])], held, sems.at[k]
        )
        for k, (start, held) in enumerate(zip(starts, (w_out, w_gate, w_up, w_down)))
    ]

    @pl.when(step == 0)
    def _():
        for copy in copies:
            copy.start()
        error_ref[...] = jnp.zeros_like(error_ref)
        copies[0].wait()

    gain = gain_ref[1:2]
    resid = tokens_ref[0].astype(F32) + dot(mixed_ref[...], w_out[...], TN)
    scale = lax.rsqrt(jnp.sum(resid * resid, -1, keepdims=True) * (1.0 / width) + epsilon)
    unit = resid * scale
    normed = (unit * gain).astype(BF16)
    normed_ref[...] = normed.T

    @pl.when(step == 0)
    def _():
        copies[1].wait()
        copies[2].wait()

    for c in range(padded // 256):
        cols = slice(c * 256, (c + 1) * 256)
        gate = dot(normed, w_gate[:, cols], NN)
        up = dot(normed, w_up[:, cols], NN)
        sigmoid = jax.nn.sigmoid(gate)
        activated = gate * sigmoid
        hidden_ref[:, cols] = (activated * up).astype(BF16)
        active[:, cols] = activated
        slope[:, cols] = up * sigmoid * (1.0 + gate * (1.0 - sigmoid))

    @pl.when(step == 0)
    def _():
        copies[3].wait()

    full = resid + dot(hidden_ref[...], w_down[...], NT)
    result_ref[0] = full.astype(BF16)
    position = step * tile + lax.broadcasted_iota(jnp.int32, (tile, 1), 0)
    difference = jnp.where(
        position < count_ref[0], full - target_ref[0].astype(F32), 0.0
    )
    error_ref[...] += jnp.sum(difference * difference, 0, keepdims=True)
    branch = difference.astype(BF16)
    branch_ref[...] = branch.T
    for c in range(padded // 256):
        cols = slice(c * 256, (c + 1) * 256)
        hidden_back = dot(branch, w_down[:, cols], NN).astype(BF16).astype(F32)
        both_ref[:, cols] = (hidden_back * slope[:, cols]).astype(BF16)
        both_ref[:, padded + c * 256 : padded + (c + 1) * 256] = (
            hidden_back * active[:, cols]
        ).astype(BF16)
    ffn_back = dot(both_ref[:, :padded], w_gate[...], NT) + dot(
        both_ref[:, padded:], w_up[...], NT
    )
    scaled = ffn_back * gain
    middle = jnp.sum(scaled * unit, -1, keepdims=True) * (1.0 / width)
    resid_back = difference + scale * (scaled - unit * middle)
    resid_back_ref[...] = resid_back
    attended = resid_back.astype(BF16)
    attended_ref[...] = attended
    mixed_back_ref[...] = dot(w_out[...], attended, NT).astype(BF16)

    @pl.when(step == pl.num_programs(0) - 1)
    def _():
        error = 0.5 * jnp.sum(error_ref[...], -1, keepdims=True)
        high = error.astype(BF16).astype(F32)
        middle = (error - high).astype(BF16).astype(F32)
        low = error - high - middle
        column = lax.broadcasted_iota(jnp.int32, side_ref.shape, 1) - count_ref[1]
        side = jnp.where(column == 0, high, jnp.where(column == 1, middle, 0.0))
        side_ref[...] = jnp.where(column == 2, low, side).astype(BF16)


def feed_forward(count, tokens, targets, mixed, gain, late, padded, extra):
    rows, width = tokens.shape[1:]
    tile = min(rows, 256)
    token_spec = pl.BlockSpec((1, tile, width), lambda i, c: (0, i, 0))

    def flat(cols):
        return pl.BlockSpec((tile, cols), lambda i, c: (i, 0))

    tall = pl.BlockSpec((width, tile), lambda i, c: (0, i))
    return pl.pallas_call(
        functools.partial(ffn_kernel, padded),
        grid_spec=pltpu.PrefetchScalarGridSpec(
            num_scalar_prefetch=1,
            grid=(rows // tile,),
            in_specs=[
                token_spec,
                token_spec,
                tall,
                pl.BlockSpec((8, width), lambda i, c: (0, 0)),
                pl.BlockSpec(memory_space=pl.ANY),
            ],
            out_specs=[
                token_spec,
                tall,
                flat(padded),
                tall,
                flat(2 * padded),
                flat(width),
                flat(width),
                tall,
                pl.BlockSpec((width, extra), lambda i, c: (0, 0)),
            ],
            scratch_shapes=[
                pltpu.VMEM((1, width), F32),
                pltpu.VMEM((width, width), BF16),
                pltpu.VMEM((width, padded), BF16),
                pltpu.VMEM((width, padded), BF16),
                pltpu.VMEM((width, padded), BF16),
                pltpu.VMEM((tile, padded), F32),
                pltpu.VMEM((tile, padded), F32),
                pltpu.SemaphoreType.DMA((4,)),
            ],
        ),
        out_shape=[
            jax.ShapeDtypeStruct((1, rows, width), BF16),
            jax.ShapeDtypeStruct((width, rows), BF16),
            jax.ShapeDtypeStruct((rows, padded), BF16),
            jax.ShapeDtypeStruct((width, rows), BF16),
            jax.ShapeDtypeStruct((rows, 2 * padded), BF16),
            jax.ShapeDtypeStruct((rows, width), BF16),
            jax.ShapeDtypeStruct((rows, width), F32),
            jax.ShapeDtypeStruct((width, rows), BF16),
            jax.ShapeDtypeStruct((width, extra), BF16),
        ],
        compiler_params=pltpu.CompilerParams(vmem_limit_bytes=60 * 1024 * 1024),
        cost_estimate=cost(4 * rows * width * (width + 3 * padded)),
        name="feed_forward",
    )(count, tokens, targets, mixed, gain, late)


def weight_grad_kernel(form, pick_ref, left_ref, right_ref, *refs):
    total = dot(left_ref[...], right_ref[...], form)
    if len(refs) > 1:
        total = total + refs[0][...].astype(F32)
    refs[-1][...] = total.astype(BF16)


def weight_grad(left, right, pick, cols, tile, extra=None, form=NN):
    rows, depth = left.shape
    step = min(rows, 512)
    each = cols // tile
    left_spec = pl.BlockSpec((step, depth), lambda j, i, p: (i, 0))
    if form is NT:
        right_spec = pl.BlockSpec((tile, depth), lambda j, i, p: (p[0] * each + j, 0))
    else:
        right_spec = pl.BlockSpec((depth, tile), lambda j, i, p: (0, p[0] * each + j))
    out_spec = pl.BlockSpec((step, tile), lambda j, i, p: (i, j))
    in_specs = [left_spec, right_spec]
    operands = [left, right]
    if extra is not None:
        in_specs.append(out_spec)
        operands.append(extra)
    return pl.pallas_call(
        functools.partial(weight_grad_kernel, form),
        grid_spec=pltpu.PrefetchScalarGridSpec(
            num_scalar_prefetch=1,
            grid=(each, rows // step),
            in_specs=in_specs,
            out_specs=out_spec,
        ),
        out_shape=jax.ShapeDtypeStruct((rows, cols), BF16),
        compiler_params=VMEM_LIMIT,
        cost_estimate=cost(2 * rows * cols * depth),
        name="weight_grad",
    )(pick, *operands)


def swap_core(array):
    return lax.ppermute(array, "core", [(i, 1 - i) for i in range(2)])


def to_send(pieces, axis, dim):
    parts = lax.axis_size(axis)
    index = lax.axis_index(axis)
    return [
        lax.dynamic_index_in_dim(pieces, lax.rem(index + shift, parts), dim, keepdims=False)
        for shift in range(1, parts)
    ]


def send(pieces, axis):
    parts = lax.axis_size(axis)
    return [
        lax.ppermute(piece, axis, [(i, (i + shift) % parts) for i in range(parts)])
        for shift, piece in enumerate(pieces, 1)
    ]


def as_pieces(block):
    seq_parts, z_parts = lax.axis_size("seq"), lax.axis_size("z")
    return block.reshape(seq_parts, z_parts, 2, -1, block.shape[1])


def whole_rows(own, core):
    kept = lax.dynamic_index_in_dim(own, core, 0, keepdims=False)
    other = swap_core(lax.dynamic_index_in_dim(own, 1 - core, 0, keepdims=False))
    first = jnp.where(core == 0, kept, other)
    second = jnp.where(core == 0, other, kept)
    return first, second


def shifted_sum(array, parts, sign):
    total = jnp.zeros_like(array)
    for shift in range(1, parts):
        if sign > 0:
            pairs = [(i, i + shift) for i in range(parts - shift)]
        else:
            pairs = [(i + shift, i) for i in range(parts - shift)]
        total = total + lax.ppermute(array, "seq", pairs)
    return total


def body(
    inputs,
    targets,
    valid_count,
    gain_mix,
    w_query,
    w_key,
    w_value,
    w_out,
    gain_ffn,
    w_gate,
    w_up,
    w_down,
):
    everyone = ("seq", "z", "y", "core")
    seq_parts = lax.axis_size("seq")
    devices = lax.axis_size(everyone)
    seq_index = lax.axis_index("seq")
    batch_index = lax.axis_index(("z", "y", "core"))
    core = lax.axis_index("core")
    rows, width = inputs.shape[1:]
    hidden_units = w_gate.shape[1]
    padded = -(-hidden_units // 256) * 256
    owners = jnp.arange(valid_count.shape[0])
    count = jnp.sum(jnp.where(owners == batch_index, valid_count, 0))
    total_valid = jnp.sum(valid_count).astype(F32)
    place = 3 * lax.axis_index(everyone)
    valid_here = jnp.stack([count - seq_index * rows, place]).astype(jnp.int32)
    extra = -(-3 * devices // 128) * 128
    gains = jnp.pad(jnp.stack([gain_mix, gain_ffn], 1), ((0, 0), (0, 126)))
    early = gather_rows(jnp.concatenate([gains, w_query, w_key, w_value], 1))
    fill = ((0, 0), (0, padded - hidden_units))
    late = jnp.concatenate(
        [w_out, jnp.pad(w_gate, fill), jnp.pad(w_up, fill), jnp.pad(w_down, fill)], 1
    )
    late = lax.all_gather(late, everyone, axis=0, tiled=True)
    lead = HEADS * FEAT
    qkv, normed, flipped, gain_rows = project(inputs, early)
    tie = lax.optimization_barrier
    upper = HEADS // 2
    lower_state = local_state(qkv, 0, upper)
    lower_init = shifted_sum(lower_state, seq_parts, 1)
    qkv, lower_state = tie((qkv, lower_state))
    upper_init = shifted_sum(local_state(qkv, upper, upper), seq_parts, 1)
    filled = attention_forward(qkv, lower_init, 0, upper)
    mixed, den, saved = attention_forward(qkv, upper_init, upper, upper, filled)
    (
        result,
        normed_ffn,
        hidden,
        branch_back,
        both_back,
        attended_back,
        resid_back,
        mixed_back,
        side,
    ) = feed_forward(valid_here, inputs, targets, mixed, gain_rows, late, padded, extra)
    mine, others = jnp.reshape(core, (1,)), jnp.reshape(1 - core, (1,))
    half, out_half, qkv_cols = padded // 2, width // 2, HEADS * HROWS // 2

    nb, back = local_back_state(qkv, mixed_back, mixed, den)
    later = shifted_sum(back, seq_parts, -1)
    normed_ffn, nb = tie((normed_ffn, nb))
    gate_up_sent = weight_grad(normed_ffn, both_back, others, padded, half)
    gate_up_come = swap_core(gate_up_sent)
    branch_back, gate_up_sent = tie((branch_back, gate_up_sent))
    down_sent = weight_grad(branch_back, hidden, others, half, half)
    normed_ffn, down_sent = tie((normed_ffn, down_sent))
    gate_up = weight_grad(normed_ffn, both_back, mine, padded, half, gate_up_come)
    down_come = swap_core(down_sent)
    a_one = to_send(as_pieces(gate_up[:, :half]), "seq", 0)
    a_two = to_send(as_pieces(gate_up[:, half:]), "y", 2)
    mixed, a_one, a_two, later = tie((mixed, a_one, a_two, later))
    a_one, a_two = send(a_one, "seq"), send(a_two, "y")
    out_sent = weight_grad(mixed, attended_back, others, out_half, out_half)
    out_come = swap_core(out_sent)
    branch_back, out_sent = tie((branch_back, out_sent))
    down = weight_grad(branch_back, hidden, mine, half, half, down_come)
    mixed, down = tie((mixed, down))
    outer = weight_grad(mixed, attended_back, mine, out_half, out_half, out_come)
    block = jnp.concatenate([down, outer, side], 1)
    block, a_one, a_two = tie((block, a_one, a_two))
    own = w_query.shape[0]
    z_parts = lax.axis_size("z")
    one = jnp.stack(a_one).reshape(seq_parts - 1, z_parts, 2, 2, own, half)
    two = a_two[0].reshape(seq_parts, z_parts, 2, own, half)
    qkv_back, gate_up_pair, part = attention_backward(
        qkv, nb, saved, later, gate_up, one, two, block, own
    )
    gate_sum, up_sum = gate_up_pair[0], gate_up_pair[1]
    if own % 16 == 0 and rows % 512 == 0:
        input_back, first_pair, pair = last_gradients(
            normed, qkv_back, flipped, inputs, resid_back, gain_rows, part, own
        )
    else:
        qkv_sent = weight_grad(normed, qkv_back, others, qkv_cols, qkv_cols, None, NT)
        qkv_come = swap_core(qkv_sent)
        c_all = weight_grad(normed, qkv_back, mine, qkv_cols, qkv_cols, qkv_come, NT)
        input_back, first_pair, pair = input_gradient(
            qkv_back, flipped, inputs, resid_back, gain_rows, c_all, part, own
        )
    down_sum = jnp.concatenate([pair[0, :, :half], pair[1, :, :half]], 1)
    out_sum = jnp.concatenate(
        [pair[0, :, half : half + out_half], pair[1, :, half : half + out_half]], 1
    )
    errors = pair[:, 0, half + out_half : half + out_half + 3 * devices].astype(F32)
    loss = 2.0 * jnp.sum(errors) / (width * total_valid)
    first, second = first_pair[0], first_pair[1]
    qkv_sum = jnp.concatenate([first, second], 1).astype(F32).reshape(own, HEADS, HROWS)
    grad_query = qkv_sum[:, :, :FEAT].reshape(own, lead)
    grad_key = qkv_sum[:, :, FEAT : 2 * FEAT].reshape(own, lead)
    grad_value = qkv_sum[:, :, 2 * FEAT :].reshape(own, HEADS * HEAD_DIM)
    grad_gate = gate_sum[:, :hidden_units].astype(F32)
    grad_up = up_sum[:, :hidden_units].astype(F32)

    def gain_grad(gain, *pairs):
        total = sum(jnp.sum(w.astype(F32) * grad, 1) for w, grad in pairs)
        return total / gain.astype(F32)

    return (
        result,
        loss,
        input_back,
        gain_grad(gain_mix, (w_query, grad_query), (w_key, grad_key), (w_value, grad_value)),
        grad_query,
        grad_key,
        grad_value,
        out_sum.astype(F32),
        gain_grad(gain_ffn, (w_gate, grad_gate), (w_up, grad_up)),
        grad_gate,
        grad_up,
        down_sum[:, :hidden_units].astype(F32),
    )


def solution(mesh):
    seq_parts, fsdp_parts = mesh.shape["seq"], mesh.shape["fsdp"]
    fine = jax.sharding.Mesh(
        mesh.devices.reshape(seq_parts, fsdp_parts // 4, 2, 2), ("seq", "z", "y", "core")
    )
    both = P(("seq", "z", "y", "core"))
    rows = P(("seq", "z", "y", "core"), None)
    tokens = P(("z", "y", "core"), "seq", None)
    return jax.shard_map(
        body,
        mesh=fine,
        in_specs=(tokens, tokens, P(), both, rows, rows, rows, rows, both, rows, rows, rows),
        out_specs=(tokens, P(), tokens, both, rows, rows, rows, rows, both, rows, rows, rows),
        check_vma=False,
    )
```

```python
import functools
import math

import jax
import jax.numpy as jnp
import numpy as np
from jax import lax
from jax.experimental import pallas as pl
from jax.experimental.pallas import tpu as pltpu
from jax.sharding import PartitionSpec as P

HEADS = 16
FEAT = 16
HEAD_DIM = 64
HROWS = 2 * FEAT + HEAD_DIM
CUT = 256
GROUPS = 11
FROWS = GROUPS * FEAT
VROWS = HEAD_DIM + 16
PAIR = 2 * VROWS
SENT = HEAD_DIM + 8
HG = 8
FIRST_BACK, SECOND_BACK = 2, 1

epsilon = 1e-05
F32 = jnp.float32
BF16 = jnp.bfloat16
NN = (((1,), (0,)), ((), ()))
NT = (((1,), (1,)), ((), ()))
TN = (((0,), (0,)), ((), ()))


def dot(left, right, dims):
    return lax.dot_general(left, right, dims, preferred_element_type=F32)


def first_row(rows, cols, count=1):
    return (lax.broadcasted_iota(jnp.int32, (rows, cols), 0) < count).astype(F32)


def rolled(u, shift):
    return pltpu.roll(u, (FEAT - shift) % FEAT, 0)


def phi_rows(u, const):
    groups = [u * u]
    for d in range(1, 9):
        groups.append(u * rolled(u, d))
    groups.append(u)
    groups.append(const)
    return jnp.concatenate([g.astype(BF16) for g in groups], 0)


def phi_pull(grad, u):
    total = grad[9 * FEAT : 10 * FEAT] + 2.0 * grad[0:FEAT] * u
    for d in range(1, 9):
        g = grad[d * FEAT : (d + 1) * FEAT]
        total = total + g * rolled(u, d) + rolled(g * u, FEAT - d)
    return total


def lane_scale():
    group = lax.broadcasted_iota(jnp.int32, (1, FROWS), 1) // FEAT
    scale = jnp.where((group == 0) | (group == 8), 1.0 / 32.0, 1.0 / 16.0)
    scale = jnp.where(group == 9, 0.25, scale)
    return jnp.where(group == 10, 1.0, scale)


def causal_mask():
    s = lax.broadcasted_iota(jnp.int32, (CUT, CUT), 0)
    t = lax.broadcasted_iota(jnp.int32, (CUT, CUT), 1)
    return s <= t


def split_pair(wide):
    high = wide.astype(BF16)
    return jnp.concatenate([high, (wide - high.astype(F32)).astype(BF16)], 0)


def twice(rows):
    return jnp.concatenate([rows, rows], 0)


def pack_states(sums, out_ref):
    fill = jnp.zeros((SENT, 2 * 128 - 2 * (FROWS - 128) - 128), F32)
    for i in range(len(sums) // 2):
        a, b = sums[2 * i][:SENT], sums[2 * i + 1][:SENT]
        out_ref[i, 0] = a[:, :128]
        out_ref[i, 1] = b[:, :128]
        out_ref[i, 2] = jnp.concatenate([a[:, 128:], b[:, 128:], fill], 1)


def unpack_states(packed_ref, state):
    side = FROWS - 128
    state[...] = jnp.zeros_like(state)
    for i in range(state.shape[0] // 2):
        for j in range(2):
            state[2 * i + j, :SENT, :128] = packed_ref[i, j]
            state[2 * i + j, :SENT, 128:] = packed_ref[i, 2][:, j * side : (j + 1) * side]


def state_kernel(blocks, qkv_ref, out_ref):
    ones2 = first_row(16, CUT, 2).astype(BF16)
    const = first_row(FEAT, CUT)

    def step(b, sums):
        cols = pl.ds(pl.multiple_of(b * CUT, CUT), CUT)
        fresh = []
        for h in range(HG):
            base = h * HROWS
            k = qkv_ref[base + FEAT : base + 2 * FEAT, cols].astype(F32)
            v = qkv_ref[base + 2 * FEAT : base + HROWS, cols]
            v_aug = jnp.concatenate([v, ones2], 0)
            fresh.append(sums[h] + dot(v_aug, phi_rows(k, const), NT))
        return tuple(fresh)

    zero = jnp.zeros((VROWS, FROWS), F32)
    sums = lax.fori_loop(0, blocks, step, (zero,) * HG)
    pack_states(sums, out_ref)


def forward_kernel(blocks, qkv_ref, init_ref, *refs):
    ones2 = first_row(16, CUT, 2).astype(BF16)
    const = first_row(FEAT, CUT)
    one_low = const.astype(BF16)
    mixed_ref, den_ref, saved_ref, state = refs[-4:]
    scale = 2.0 * lane_scale()
    mask = causal_mask()
    unpack_states(init_ref, state)

    def step(b, carry):
        cols = pl.ds(pl.multiple_of(b * CUT, CUT), CUT)
        for h in range(HG):
            base = h * HROWS
            q = qkv_ref[base : base + FEAT, cols]
            k = qkv_ref[base + FEAT : base + 2 * FEAT, cols]
            v = qkv_ref[base + 2 * FEAT : base + HROWS, cols]
            v_aug = jnp.concatenate([v, ones2], 0)
            k_aug = jnp.concatenate([k, one_low], 0)
            q_aug = jnp.concatenate([q * 0.25, one_low], 0)
            u = dot(k_aug, q_aug, TN)
            weight = jnp.where(mask, u * u + 1.0, 0.0).astype(BF16)
            low = split_pair(state[h] * scale)
            saved_ref[h, b] = low
            earlier = dot(low, phi_rows(q.astype(F32), const), NN)
            numer = dot(v_aug, weight, NN) + (earlier[:VROWS] + earlier[VROWS:])
            den = numer[HEAD_DIM : HEAD_DIM + 1]
            rows = slice(h * HEAD_DIM, (h + 1) * HEAD_DIM)
            mixed_ref[rows, cols] = (numer[:HEAD_DIM] * (1.0 / den)).astype(BF16)
            den_ref[0, h : h + 1, cols] = 0.5 * den
            state[h] += dot(v_aug, phi_rows(k.astype(F32), const), NT)
        return carry

    lax.fori_loop(0, blocks, step, 0)


def back_state_kernel(blocks, qkv_ref, grad_ref, mixed_ref, den_ref, nb_ref, out_ref):
    const = first_row(FEAT, CUT)
    row = lax.broadcasted_iota(jnp.int32, (16, CUT), 0)

    def step(b, sums):
        cols = pl.ds(pl.multiple_of(b * CUT, CUT), CUT)
        fresh = []
        for h in range(HG):
            base = h * HROWS
            q = qkv_ref[base : base + FEAT, cols].astype(F32)
            rows = slice(h * HEAD_DIM, (h + 1) * HEAD_DIM)
            g = grad_ref[rows, cols].astype(F32)
            inverse = 1.0 / den_ref[0, h : h + 1, cols]
            db = -inverse * jnp.sum(
                g * mixed_ref[rows, cols].astype(F32), axis=0, keepdims=True
            )
            nb = (g * inverse).astype(BF16)
            high = db.astype(BF16).astype(F32)
            tail = jnp.where(row == 0, high, jnp.where(row == 1, db - high, 0.0)).astype(BF16)
            nb_aug = jnp.concatenate([nb, tail], 0)
            nb_ref[h, :, cols] = nb_aug
            fresh.append(sums[h] + dot(nb_aug, phi_rows(q, const), NT))
        return tuple(fresh)

    zero = jnp.zeros((VROWS, FROWS), F32)
    sums = lax.fori_loop(0, blocks, step, (zero,) * HG)
    pack_states(sums, out_ref)


def backward_kernel(
    sizes,
    blocks,
    qkv_ref,
    nb_ref,
    saved_ref,
    init_ref,
    wide_ref,
    one_ref,
    two_ref,
    block_ref,
    out_ref,
    pair_out,
    part_out,
    state,
    *refs,
):
    ones2 = first_row(16, CUT, 2).astype(BF16)
    const = first_row(FEAT, CUT)
    one_low = const.astype(BF16)
    scale = lane_scale()
    mask = causal_mask()
    halves = pl.num_programs(1)
    at = pl.program_id(0) * halves + pl.program_id(1)
    last = pl.num_programs(0) * halves - 1
    each = blocks // halves
    by_seq, by_z, by_y, by_core = neighbours(sizes)
    count = 8 + 8
    first = RowSums(sizes, wide_ref, refs[:count], pair_out, (one_ref, two_ref))
    refs = refs[count:]
    second = RowSums(sizes, block_ref, refs[:6] + (part_out,) + refs[6:])

    @pl.when(at == 0)
    def _():
        greet(by_seq + by_z + [by_y, by_core])
        first.second()
        second.start()

    @pl.when(pl.program_id(1) == 0)
    def _():
        unpack_states(init_ref, state)

    def step(i, carry):
        b = blocks - 1 - (pl.program_id(1) * each + i)
        cols = pl.ds(pl.multiple_of(b * CUT, CUT), CUT)
        for h in range(HG):
            base = h * HROWS
            q = qkv_ref[base : base + FEAT, cols]
            k = qkv_ref[base + FEAT : base + 2 * FEAT, cols]
            v = qkv_ref[base + 2 * FEAT : base + HROWS, cols]
            qf = q.astype(F32)
            kf = k.astype(F32)
            q4 = q * 0.25
            nb = nb_ref[h, :, cols]
            v_aug = jnp.concatenate([v, ones2], 0)
            k_aug = jnp.concatenate([k, one_low], 0)
            q_aug = jnp.concatenate([q4, one_low], 0)
            u = dot(k_aug, q_aug, TN)
            weight = jnp.where(mask, u * u + 1.0, 0.0).astype(BF16)
            wb = dot(v_aug, nb, TN)
            sb = jnp.where(mask, wb * u, 0.0).astype(BF16)
            q_feat_back = dot(saved_ref[h, b], twice(nb), TN)
            dq = 0.25 * dot(k, sb, NN) + 0.5 * phi_pull(q_feat_back, qf)
            low = split_pair(state[h] * scale)
            k_feat_back = dot(low, twice(v_aug), TN)
            later = dot(low, phi_rows(kf, const), NN)
            dk = dot(q4, sb, NT) + phi_pull(k_feat_back, kf)
            dv = 0.5 * dot(nb[:HEAD_DIM], weight, NT) + (
                later[:HEAD_DIM] + later[VROWS : VROWS + HEAD_DIM]
            )
            out_ref[base : base + FEAT, cols] = dq.astype(BF16)
            out_ref[base + FEAT : base + 2 * FEAT, cols] = dk.astype(BF16)
            out_ref[base + 2 * FEAT : base + HROWS, cols] = dv.astype(BF16)
            state[h] += dot(nb, phi_rows(qf, const), NT)
        return carry

    lax.fori_loop(0, each, step, 0)

    @pl.when(at == last - FIRST_BACK)
    def _():
        first.third()

    @pl.when(at == last - SECOND_BACK)
    def _():
        second.second()

    @pl.when(at == last)
    def _():
        second.third()
        first.fourth()
        second.finish()
        first.finish()


def cost(flops):
    return pl.CostEstimate(flops=int(flops * 0.02), bytes_accessed=0, transcendentals=0)


def head_spec(rows, cols):
    return pl.BlockSpec((HG * rows, cols), lambda g: (g, 0))


def lead_spec(*tail):
    return pl.BlockSpec((HG,) + tail, lambda g: (g,) + (0,) * len(tail))


VMEM_LIMIT = pltpu.CompilerParams(vmem_limit_bytes=56 * 1024 * 1024)


def packed_shape(heads):
    return jax.ShapeDtypeStruct((heads // 2, 3, SENT, 128), F32)


def packed_spec():
    return pl.BlockSpec((HG // 2, 3, SENT, 128), lambda g: (g, 0, 0, 0))


def local_state(qkv, start, count):
    cols = qkv.shape[1]
    first = start // HG
    return pl.pallas_call(
        functools.partial(state_kernel, cols // CUT),
        grid=(count // HG,),
        in_specs=[pl.BlockSpec((HG * HROWS, cols), lambda g: (first + g, 0))],
        out_specs=packed_spec(),
        out_shape=packed_shape(count),
        compiler_params=VMEM_LIMIT,
        cost_estimate=cost(11e9 * cols / 2048 * count / HEADS),
        name="key_state",
    )(qkv)


def attention_forward(qkv, init, start, count, filled=()):
    cols = qkv.shape[1]
    blocks = cols // CUT
    first = start // HG

    def head_rows(rows):
        return pl.BlockSpec((HG * rows, cols), lambda g: (first + g, 0))

    def lead(*tail):
        return pl.BlockSpec((HG,) + tail, lambda g: (first + g,) + (0,) * len(tail))

    return pl.pallas_call(
        functools.partial(forward_kernel, blocks),
        grid=(count // HG,),
        in_specs=[head_rows(HROWS), packed_spec()]
        + [pl.BlockSpec(memory_space=pl.ANY)] * len(filled),
        out_specs=[
            head_rows(HEAD_DIM),
            pl.BlockSpec((1, HG, cols), lambda g: (first + g, 0, 0)),
            lead(blocks, PAIR, FROWS),
        ],
        out_shape=[
            jax.ShapeDtypeStruct((HEADS * HEAD_DIM, cols), BF16),
            jax.ShapeDtypeStruct((HEADS // HG, HG, cols), F32),
            jax.ShapeDtypeStruct((HEADS, blocks, PAIR, FROWS), BF16),
        ],
        scratch_shapes=[pltpu.VMEM((HG, VROWS, FROWS), F32)],
        compiler_params=VMEM_LIMIT,
        cost_estimate=cost(36e9 * cols / 2048 * count / HEADS),
        input_output_aliases={2 + i: i for i in range(len(filled))},
        name="attend",
    )(qkv, init, *filled)


def local_back_state(qkv, grad, mixed, den):
    cols = qkv.shape[1]
    return pl.pallas_call(
        functools.partial(back_state_kernel, cols // CUT),
        grid=(HEADS // HG,),
        in_specs=[
            head_spec(HROWS, cols),
            head_spec(HEAD_DIM, cols),
            head_spec(HEAD_DIM, cols),
            pl.BlockSpec((1, HG, cols), lambda g: (g, 0, 0)),
        ],
        out_specs=[lead_spec(VROWS, cols), packed_spec()],
        out_shape=[
            jax.ShapeDtypeStruct((HEADS, VROWS, cols), BF16),
            packed_shape(HEADS),
        ],
        compiler_params=VMEM_LIMIT,
        cost_estimate=cost(13e9 * cols / 2048),
        name="query_state",
    )(qkv, grad, mixed, den)


def attention_backward(qkv, nb, saved, init, wide, one, two, block, own):
    cols = qkv.shape[1]
    blocks = cols // CUT
    sizes = lax.axis_size("seq"), lax.axis_size("z")
    width = block.shape[-1]
    cut = 128 * (width // 256)
    first_buffers, first_sems = row_sum_scratch(
        sizes, own, one.shape[-1], two.shape[-1], summed=True
    )
    second_buffers, second_sems = row_sum_scratch(
        sizes, own, cut, width - cut, ends=False, keep=False
    )

    def head_rows(rows):
        return pl.BlockSpec((HG * rows, cols), lambda g, p: (g, 0))

    def lead(*tail):
        return pl.BlockSpec((HG,) + tail, lambda g, p: (g,) + (0,) * len(tail))

    here = pl.BlockSpec(memory_space=pltpu.VMEM)
    return pl.pallas_call(
        functools.partial(backward_kernel, sizes, blocks),
        grid=(HEADS // HG, 2),
        in_specs=[
            head_rows(HROWS),
            lead(VROWS, cols),
            lead(blocks, PAIR, FROWS),
            pl.BlockSpec((HG // 2, 3, SENT, 128), lambda g, p: (g, 0, 0, 0)),
            here,
            here,
            here,
            here,
        ],
        out_specs=[head_rows(HROWS), here, here],
        out_shape=[
            jax.ShapeDtypeStruct((HEADS * HROWS, cols), BF16),
            jax.ShapeDtypeStruct((2, own, wide.shape[-1]), BF16),
            jax.ShapeDtypeStruct((sizes[1], 2, own, width), BF16),
        ],
        scratch_shapes=[pltpu.VMEM((HG, VROWS, FROWS), F32)]
        + first_buffers
        + first_sems
        + second_buffers
        + second_sems,
        compiler_params=pltpu.CompilerParams(
            collective_id=2, has_side_effects=True, vmem_limit_bytes=58 * 1024 * 1024
        ),
        cost_estimate=cost(53e9 * cols / 2048),
        name="attend_back",
    )(
        qkv,
        nb,
        saved,
        init,
        wide.reshape(sizes + (2, 2, own, wide.shape[-1])),
        one,
        two,
        block.reshape(sizes + (2, 2, own, width)),
    )


MESH = pl.DeviceIdType.MESH


def gather_kernel(shape, split, shard_ref, out_ref, local_sem, *sems):
    seq_parts, z_parts = shape
    s, z = lax.axis_index("seq"), lax.axis_index("z")
    y, c = lax.axis_index("y"), lax.axis_index("core")
    cols = shard_ref.shape[1]
    left, right = pl.ds(0, split), pl.ds(split, cols - split)
    every = slice(None)

    def peer(ds=0, dz=0, dy=0, dc=0):
        return (
            lax.rem(s + ds, seq_parts),
            lax.rem(z + dz, z_parts),
            lax.rem(y + dy, 2),
            lax.rem(c + dc, 2),
        )

    def send(kind, slot, src, dst, device):
        return pltpu.make_async_remote_copy(
            src_ref=src,
            dst_ref=dst,
            send_sem=sems[2 * kind].at[slot],
            recv_sem=sems[2 * kind + 1].at[slot],
            device_id=device,
            device_id_type=MESH,
        )

    barrier = pltpu.get_barrier_semaphore()
    peers = [peer(ds=j) for j in range(1, seq_parts)]
    peers += [peer(dz=k) for k in range(1, z_parts)]
    peers += [peer(dy=1), peer(dc=1)]
    for device in peers:
        pl.semaphore_signal(barrier, inc=1, device_id=device, device_id_type=MESH)
    own = pltpu.make_async_copy(shard_ref, out_ref.at[s, z, y, c], local_sem)
    own.start()
    pl.semaphore_wait(barrier, len(peers))

    order = [0] + sorted(range(1, z_parts), key=lambda k: min(k, z_parts - k))
    slab = {k: lax.rem(z + z_parts - k, z_parts) for k in order}
    along = {
        k: send(0, k, shard_ref, out_ref.at[s, z, y, c], peer(dz=k)) for k in order[1:]
    }
    for k in order[1:]:
        along[k].start()
    own.wait()
    first_y, first_x = {}, {}
    for k in order:
        if k:
            along[k].wait_recv()
        at = out_ref.at[s, slab[k], y, c, :, left]
        first_y[k] = send(1, k, at, at, peer(dy=1))
        first_y[k].start()
        at = out_ref.at[s, slab[k], y, c, :, right]
        first_x[k] = [
            send(2, k * seq_parts + j, at, at, peer(ds=j)) for j in range(1, seq_parts)
        ]
        for copy in first_x[k]:
            copy.start()
    then_x, then_y, across = {}, {}, {}
    for k in order:
        first_y[k].wait_recv()
        at = out_ref.at[s, slab[k], :, c, :, left]
        then_x[k] = [
            send(3, k * seq_parts + j, at, at, peer(ds=j)) for j in range(1, seq_parts)
        ]
        for copy in then_x[k]:
            copy.start()
        for copy in first_x[k]:
            copy.wait_recv()
        at = out_ref.at[:, slab[k], y, c, :, right]
        then_y[k] = send(4, k, at, at, peer(dy=1))
        then_y[k].start()
    for k in order:
        for copy in then_x[k]:
            copy.wait_recv()
        then_y[k].wait_recv()
        at = out_ref.at[:, slab[k], :, c]
        across[k] = send(5, k, at, at, peer(dc=1))
        across[k].start()
    for k in order:
        across[k].wait_recv()
    for k in order:
        if k:
            along[k].wait_send()
        first_y[k].wait_send()
        then_y[k].wait_send()
        across[k].wait_send()
        for copy in first_x[k] + then_x[k]:
            copy.wait_send()


def gather_rows(shard):
    own, cols = shard.shape
    seq_parts, z_parts = lax.axis_size("seq"), lax.axis_size("z")
    split = cols // 256 * 128
    counts = (z_parts, z_parts, z_parts * seq_parts, z_parts * seq_parts, z_parts, z_parts)
    out = pl.pallas_call(
        functools.partial(gather_kernel, (seq_parts, z_parts), split),
        in_specs=[pl.BlockSpec(memory_space=pl.ANY)],
        out_specs=pl.BlockSpec(memory_space=pl.ANY),
        out_shape=jax.ShapeDtypeStruct((seq_parts, z_parts, 2, 2, own, cols), BF16),
        scratch_shapes=[pltpu.SemaphoreType.DMA]
        + [pltpu.SemaphoreType.DMA((n,)) for n in counts for _ in range(2)],
        compiler_params=pltpu.CompilerParams(collective_id=0, has_side_effects=True),
        cost_estimate=cost(25e9),
        name="gather_rows",
    )(shard)
    return out.reshape(-1, cols)


def project_kernel(tokens_ref, weight_ref, qkv_ref, normed_ref, flipped_ref, gain_ref):
    width = tokens_ref.shape[2]
    lead = HEADS * FEAT

    @pl.when(pl.program_id(0) == 0)
    def _():
        gain_ref[...] = weight_ref[:, :128].astype(F32).T[:8]
        for c in range(HEADS * HROWS // 128):
            piece = weight_ref[:, 128 * (c + 1) : 128 * (c + 2)].T
            start = 128 * c
            if start < 2 * lead:
                each, first = FEAT, FEAT * (start // lead)
                head = (start % lead) // FEAT
            else:
                each, first = HEAD_DIM, 2 * FEAT
                head = (start - 2 * lead) // HEAD_DIM
            for j in range(128 // each):
                at = (head + j) * HROWS + first
                flipped_ref[at : at + each, :] = piece[j * each : (j + 1) * each]

    tokens = tokens_ref[0].astype(F32)
    scale = lax.rsqrt(jnp.sum(tokens * tokens, -1, keepdims=True) * (1.0 / width) + epsilon)
    normed = (tokens * scale * gain_ref[0:1]).astype(BF16)
    normed_ref[...] = normed.T
    qkv_ref[...] = dot(flipped_ref[...], normed, NT).astype(BF16)


def project(tokens, early):
    rows, width = tokens.shape[1:]
    tile = min(rows, 512)
    return pl.pallas_call(
        project_kernel,
        grid=(rows // tile,),
        in_specs=[
            pl.BlockSpec((1, tile, width), lambda i: (0, i, 0)),
            pl.BlockSpec(
                (width, 128 + HEADS * HROWS), lambda i: (0, 0), pipeline_mode=pl.Buffered(1)
            ),
        ],
        out_specs=[
            pl.BlockSpec((HEADS * HROWS, tile), lambda i: (0, i)),
            pl.BlockSpec((width, tile), lambda i: (0, i)),
            pl.BlockSpec((HEADS * HROWS, width), lambda i: (0, 0)),
            pl.BlockSpec((8, width), lambda i: (0, 0)),
        ],
        out_shape=[
            jax.ShapeDtypeStruct((HEADS * HROWS, rows), BF16),
            jax.ShapeDtypeStruct((width, rows), BF16),
            jax.ShapeDtypeStruct((HEADS * HROWS, width), BF16),
            jax.ShapeDtypeStruct((8, width), F32),
        ],
        compiler_params=VMEM_LIMIT,
        cost_estimate=cost(2 * HEADS * HROWS * rows * width),
        name="project",
    )(tokens, early)


def remote(src, dst, sems, slot, device):
    return pltpu.make_async_remote_copy(
        src_ref=src,
        dst_ref=dst,
        send_sem=sems[0].at[slot],
        recv_sem=sems[1].at[slot],
        device_id=device,
        device_id_type=MESH,
    )


def positions():
    return tuple(lax.axis_index(name) for name in ("seq", "z", "y", "core"))


def neighbours(sizes):
    seq_parts, z_parts = sizes
    s, z, y, c = positions()
    by_seq = [(lax.rem(s + j, seq_parts), z, y, c) for j in range(1, seq_parts)]
    by_z = [(s, lax.rem(z + k, z_parts), y, c) for k in range(1, z_parts)]
    return by_seq, by_z, (s, z, 1 - y, c), (s, z, y, 1 - c)


def greet(devices):
    barrier = pltpu.get_barrier_semaphore()
    for device in devices:
        pl.semaphore_signal(barrier, inc=1, device_id=device, device_id_type=MESH)
    pl.semaphore_wait(barrier, len(devices))


class RowSums:
    def __init__(self, sizes, source, refs, out_ref=None, arrived=None):
        seq_parts, z_parts = self.sizes = sizes
        s, z, y, c = self.place = positions()
        by_seq, by_z, by_y, by_core = neighbours(sizes)
        self.source, self.summed, self.out_ref = source, arrived is not None, out_ref
        refs = list(refs)
        self.x_sum, self.y_sum = refs[:2]
        del refs[:2]
        if arrived is None:
            arrived = refs[:2]
            del refs[:2]
        self.x_in, self.y_in = arrived
        self.then_y_in, self.then_x_in, self.row_sum = refs[:3]
        del refs[:3]
        self.cut = self.x_sum.shape[-1]
        rest = self.y_sum.shape[-1]
        if out_ref is not None:
            self.z_in, self.own_sum, self.swapped = refs[:3]
            del refs[:3]
        pairs = [refs[2 * i : 2 * i + 2] for i in range(len(refs) // 2)]
        others = range(1, seq_parts)
        self.first = []
        if not self.summed:
            left, right = pl.ds(0, self.cut), pl.ds(self.cut, rest)
            self.first_x = [
                remote(
                    source.at[lax.rem(s + j, seq_parts), :, :, :, :, left],
                    self.x_in.at[j - 1],
                    pairs[2],
                    j - 1,
                    by_seq[j - 1],
                )
                for j in others
            ]
            self.first_y = remote(
                source.at[:, :, 1 - y, :, :, right], self.y_in, pairs[3], 0, by_y
            )
            self.first = self.first_x + [self.first_y]
        self.then_y = remote(self.x_sum.at[:, 1 - y], self.then_y_in, pairs[0], 0, by_y)
        self.then_x = [
            remote(
                self.y_sum.at[lax.rem(s + j, seq_parts)],
                self.then_x_in.at[j - 1],
                pairs[1],
                j - 1,
                by_seq[j - 1],
            )
            for j in others
        ]
        if out_ref is not None:
            self.along = along_z(sizes, self.row_sum, self.z_in, pairs[-2])
            self.across = remote(self.own_sum.at[1 - c], self.swapped, pairs[-1], 0, by_core)

    def start(self):
        for copy in self.first:
            copy.start()

    def second(self):
        s, z, y, c = self.place
        if not self.summed:
            for copy in self.first_x:
                copy.wait_recv()
        total = self.source[s, :, :, :, :, : self.cut].astype(F32)
        for j in range(self.sizes[0] - 1):
            total = total + self.x_in[j].astype(F32)
        self.x_sum[...] = total.astype(BF16)
        self.then_y.start()
        if not self.summed:
            self.first_y.wait_recv()
        total = self.source[:, :, y, :, :, self.cut :].astype(F32)
        self.y_sum[...] = (total + self.y_in[...].astype(F32)).astype(BF16)
        for copy in self.then_x:
            copy.start()

    def third(self):
        s, z, y, c = self.place
        self.then_y.wait_recv()
        total = self.x_sum[:, y].astype(F32) + self.then_y_in[...].astype(F32)
        self.row_sum[:, :, :, : self.cut] = total.astype(BF16)
        for copy in self.then_x:
            copy.wait_recv()
        total = self.y_sum[s].astype(F32)
        for j in range(self.sizes[0] - 1):
            total = total + self.then_x_in[j].astype(F32)
        self.row_sum[:, :, :, self.cut :] = total.astype(BF16)
        if self.out_ref is not None:
            for copy in self.along:
                copy.start()

    def fourth(self):
        sum_z(self.along, self.row_sum, self.z_in, self.own_sum)
        self.across.start()
        c = self.place[3]
        self.out_ref[c] = self.own_sum[c]

    def finish(self):
        for copy in self.first + [self.then_y] + self.then_x:
            copy.wait_send()
        if self.out_ref is not None:
            self.across.wait_recv()
            self.out_ref[1 - self.place[3]] = self.swapped[...]
            self.across.wait_send()
            for copy in self.along:
                copy.wait_send()


def along_z(sizes, source, z_in, sems):
    z_parts = sizes[1]
    z = positions()[1]
    by_z = neighbours(sizes)[1]
    return [
        remote(source.at[lax.rem(z + k, z_parts)], z_in.at[k - 1], sems, k - 1, by_z[k - 1])
        for k in range(1, z_parts)
    ]


def sum_z(copies, source, z_in, own_sum):
    for copy in copies:
        copy.wait_recv()
    total = source[positions()[1]].astype(F32)
    for k in range(len(copies)):
        total = total + z_in[k].astype(F32)
    own_sum[...] = total.astype(BF16)


def row_sum_scratch(sizes, own, cut, rest, summed=False, ends=True, keep=True):
    seq_parts, z_parts = sizes
    cols = cut + rest

    def low(*shape):
        return pltpu.VMEM(shape, BF16)

    buffers = [low(z_parts, 2, 2, own, cut), low(seq_parts, z_parts, 2, own, rest)]
    if not summed:
        buffers += [
            low(seq_parts - 1, z_parts, 2, 2, own, cut),
            low(seq_parts, z_parts, 2, own, rest),
        ]
    buffers += [low(z_parts, 2, own, cut), low(seq_parts - 1, z_parts, 2, own, rest)]
    if keep:
        buffers += [low(z_parts, 2, own, cols)]
    counts = [1, seq_parts - 1]
    if not summed:
        counts += [seq_parts - 1, 1]
    if ends:
        buffers += [low(z_parts - 1, 2, own, cols), low(2, own, cols), low(own, cols)]
        counts += [z_parts - 1, 1]
    return buffers, [pltpu.SemaphoreType.DMA((n,)) for n in counts for _ in range(2)]


def input_kernel(
    sizes,
    back_ref,
    flipped_ref,
    tokens_ref,
    resid_ref,
    gain_ref,
    block_ref,
    part_ref,
    out_ref,
    block_out,
    part_out,
    part_z_in,
    part_sum,
    part_swapped,
    z_send,
    z_recv,
    core_send,
    core_recv,
    *refs,
):
    step = pl.program_id(0)
    last = pl.num_programs(0) - 1
    c = positions()[3]
    by_seq, by_z, by_y, by_core = neighbours(sizes)
    sums = RowSums(sizes, block_ref, refs, block_out)
    part_along = along_z(sizes, part_ref, part_z_in, (z_send, z_recv))
    part_across = remote(
        part_sum.at[1 - c], part_swapped, (core_send, core_recv), 0, by_core
    )

    @pl.when(step == 0)
    def _():
        greet(by_seq + by_z + [by_y, by_core])
        for copy in part_along:
            copy.start()
        sums.start()

    width = tokens_ref.shape[2]
    tokens = tokens_ref[0].astype(F32)
    scale = lax.rsqrt(jnp.sum(tokens * tokens, -1, keepdims=True) * (1.0 / width) + epsilon)
    unit = tokens * scale
    normed_back = dot(back_ref[...], flipped_ref[...], TN)
    scaled = normed_back * gain_ref[0:1]
    middle = jnp.sum(scaled * unit, -1, keepdims=True) * (1.0 / width)
    out_ref[0] = resid_ref[...] + scale * (scaled - unit * middle)

    @pl.when(step == last - 2)
    def _():
        sums.second()

    @pl.when(step == last - 1)
    def _():
        sums.third()

    @pl.when(step == last)
    def _():
        sum_z(part_along, part_ref, part_z_in, part_sum)
        part_across.start()
        part_out[c] = part_sum[c]
        sums.fourth()
        part_across.wait_recv()
        part_out[1 - c] = part_swapped[...]
        sums.finish()
        for copy in part_along:
            copy.wait_send()
        part_across.wait_send()


def input_gradient(back, flipped, tokens, resid_back, gain, block, part, own):
    rows, width = tokens.shape[1:]
    tile = min(rows // 4, 512)
    sizes = lax.axis_size("seq"), lax.axis_size("z")
    cols, part_cols = block.shape[-1], part.shape[-1]
    cut = 128 * (cols // 256)
    buffers, sems = row_sum_scratch(sizes, own, cut, cols - cut)
    return pl.pallas_call(
        functools.partial(input_kernel, sizes),
        grid=(rows // tile,),
        in_specs=[
            pl.BlockSpec((HEADS * HROWS, tile), lambda i: (0, i)),
            pl.BlockSpec(flipped.shape, lambda i: (0, 0), pipeline_mode=pl.Buffered(1)),
            pl.BlockSpec((1, tile, width), lambda i: (0, i, 0)),
            pl.BlockSpec((tile, width), lambda i: (i, 0)),
            pl.BlockSpec((8, width), lambda i: (0, 0)),
            pl.BlockSpec(memory_space=pltpu.VMEM),
            pl.BlockSpec(memory_space=pltpu.VMEM),
        ],
        out_specs=[
            pl.BlockSpec((1, tile, width), lambda i: (0, i, 0)),
            pl.BlockSpec(memory_space=pltpu.VMEM),
            pl.BlockSpec(memory_space=pltpu.VMEM),
        ],
        out_shape=[
            jax.ShapeDtypeStruct((1, rows, width), F32),
            jax.ShapeDtypeStruct((2, own, cols), BF16),
            jax.ShapeDtypeStruct((2, own, part_cols), BF16),
        ],
        scratch_shapes=[
            pltpu.VMEM((sizes[1] - 1, 2, own, part_cols), BF16),
            pltpu.VMEM((2, own, part_cols), BF16),
            pltpu.VMEM((own, part_cols), BF16),
            pltpu.SemaphoreType.DMA((sizes[1] - 1,)),
            pltpu.SemaphoreType.DMA((sizes[1] - 1,)),
            pltpu.SemaphoreType.DMA((1,)),
            pltpu.SemaphoreType.DMA((1,)),
        ]
        + buffers
        + sems,
        compiler_params=pltpu.CompilerParams(
            collective_id=1, has_side_effects=True, vmem_limit_bytes=56 * 1024 * 1024
        ),
        cost_estimate=cost(4 * HEADS * HROWS * rows * width),
        name="input_gradient",
    )(
        back,
        flipped,
        tokens,
        resid_back,
        gain,
        block.reshape(sizes + (2, 2, own, cols)),
        part,
    )


def last_kernel(
    sizes,
    normed_ref,
    back_ref,
    flipped_ref,
    tokens_ref,
    resid_ref,
    gain_ref,
    part_ref,
    out_ref,
    block_out,
    part_out,
    sent,
    come,
    block,
    part_z_in,
    part_sum,
    part_swapped,
    half_send,
    half_recv,
    z_send,
    z_recv,
    core_send,
    core_recv,
    *refs,
):
    step = pl.program_id(0)
    c = positions()[3]
    by_seq, by_z, by_y, by_core = neighbours(sizes)
    sums = RowSums(sizes, block, refs, block_out)
    part_along = along_z(sizes, part_ref, part_z_in, (z_send, z_recv))
    part_across = remote(
        part_sum.at[1 - c], part_swapped, (core_send, core_recv), 0, by_core
    )
    half = remote(sent, come, (half_send, half_recv), 0, by_core)
    cols = sent.shape[1]
    each = sent.shape[0] // sizes[0]
    tile, width = tokens_ref.shape[1:]

    def gradient(s, which):
        rows = pl.ds(pl.multiple_of(which * cols, 16), cols)
        return dot(normed_ref[s * each : (s + 1) * each, :], back_ref[rows, :], NT)

    @pl.when(step == 0)
    def _():
        greet(by_seq + by_z + [by_y, by_core])
        for copy in part_along:
            copy.start()
        for s in range(sizes[0]):
            sent[s * each : (s + 1) * each, :] = gradient(s, 1 - c).astype(BF16)
        half.start()

    @pl.when(step == 2)
    def _():
        half.wait_recv()
        for s in range(sizes[0]):
            total = gradient(s, c) + come[s * each : (s + 1) * each, :].astype(F32)
            block[s] = total.astype(BF16).reshape(block.shape[1:])
        sums.start()

    @pl.when((step == 1) | (step > 2))
    def _():
        at = pl.multiple_of(step // 3 * (step - 2) * tile, 128)
        tokens = tokens_ref[0].astype(F32)
        scale = lax.rsqrt(
            jnp.sum(tokens * tokens, -1, keepdims=True) * (1.0 / width) + epsilon
        )
        unit = tokens * scale
        normed_back = dot(back_ref[:, pl.ds(at, tile)], flipped_ref[...], TN)
        scaled = normed_back * gain_ref[0:1]
        middle = jnp.sum(scaled * unit, -1, keepdims=True) * (1.0 / width)
        out_ref[0] = resid_ref[...] + scale * (scaled - unit * middle)

    @pl.when(step == 4)
    def _():
        sums.second()

    @pl.when(step == 5)
    def _():
        sums.third()
        sum_z(part_along, part_ref, part_z_in, part_sum)
        part_across.start()
        part_out[c] = part_sum[c]
        sums.fourth()
        part_across.wait_recv()
        part_out[1 - c] = part_swapped[...]
        sums.finish()
        for copy in part_along:
            copy.wait_send()
        part_across.wait_send()
        half.wait_send()


def last_gradients(normed, back, flipped, tokens, resid_back, gain, part, own):
    rows, width = tokens.shape[1:]
    tile = rows // 4
    sizes = lax.axis_size("seq"), lax.axis_size("z")
    cols, part_cols = HEADS * HROWS // 2, part.shape[-1]
    cut = 128 * (cols // 256)
    buffers, sems = row_sum_scratch(sizes, own, cut, cols - cut)
    here = pl.BlockSpec(memory_space=pltpu.VMEM)

    def place(i):
        return i // 3 * (i - 2)

    def low(*shape):
        return pltpu.VMEM(shape, BF16)

    one, many = pltpu.SemaphoreType.DMA((1,)), pltpu.SemaphoreType.DMA((sizes[1] - 1,))
    return pl.pallas_call(
        functools.partial(last_kernel, sizes),
        grid=(6,),
        in_specs=[
            here,
            here,
            here,
            pl.BlockSpec((1, tile, width), lambda i: (0, place(i), 0)),
            pl.BlockSpec((tile, width), lambda i: (place(i), 0)),
            pl.BlockSpec((8, width), lambda i: (0, 0)),
            here,
        ],
        out_specs=[pl.BlockSpec((1, tile, width), lambda i: (0, place(i), 0)), here, here],
        out_shape=[
            jax.ShapeDtypeStruct((1, rows, width), F32),
            jax.ShapeDtypeStruct((2, own, cols), BF16),
            jax.ShapeDtypeStruct((2, own, part_cols), BF16),
        ],
        scratch_shapes=[
            low(width, cols),
            low(width, cols),
            low(*sizes, 2, 2, own, cols),
            low(sizes[1] - 1, 2, own, part_cols),
            low(2, own, part_cols),
            low(own, part_cols),
            one,
            one,
            many,
            many,
            one,
            one,
        ]
        + buffers
        + sems,
        compiler_params=pltpu.CompilerParams(
            collective_id=3, has_side_effects=True, vmem_limit_bytes=56 * 1024 * 1024
        ),
        cost_estimate=cost(8 * HEADS * HROWS * rows * width),
        name="last_gradients",
    )(normed, back, flipped, tokens, resid_back, gain, part)


def ffn_kernel(
    padded,
    count_ref,
    tokens_ref,
    target_ref,
    mixed_ref,
    gain_ref,
    late_ref,
    result_ref,
    normed_ref,
    hidden_ref,
    branch_ref,
    both_ref,
    attended_ref,
    resid_back_ref,
    mixed_back_ref,
    side_ref,
    error_ref,
    w_out,
    w_gate,
    w_up,
    w_down,
    slope,
    active,
    sems,
):
    step = pl.program_id(0)
    tile, width = tokens_ref.shape[1:]
    starts = (0, width, width + padded, width + 2 * padded)
    copies = [
        pltpu.make_async_copy(
            late_ref.at[:, pl.ds(start, held.shape[1])], held, sems.at[k]
        )
        for k, (start, held) in enumerate(zip(starts, (w_out, w_gate, w_up, w_down)))
    ]

    @pl.when(step == 0)
    def _():
        for copy in copies:
            copy.start()
        error_ref[...] = jnp.zeros_like(error_ref)
        copies[0].wait()

    gain = gain_ref[1:2]
    resid = tokens_ref[0].astype(F32) + dot(mixed_ref[...], w_out[...], TN)
    scale = lax.rsqrt(jnp.sum(resid * resid, -1, keepdims=True) * (1.0 / width) + epsilon)
    unit = resid * scale
    normed = (unit * gain).astype(BF16)
    normed_ref[...] = normed.T

    @pl.when(step == 0)
    def _():
        copies[1].wait()
        copies[2].wait()

    for c in range(padded // 256):
        cols = slice(c * 256, (c + 1) * 256)
        gate = dot(normed, w_gate[:, cols], NN)
        up = dot(normed, w_up[:, cols], NN)
        sigmoid = jax.nn.sigmoid(gate)
        activated = gate * sigmoid
        hidden_ref[:, cols] = (activated * up).astype(BF16)
        active[:, cols] = activated
        slope[:, cols] = up * sigmoid * (1.0 + gate * (1.0 - sigmoid))

    @pl.when(step == 0)
    def _():
        copies[3].wait()

    full = resid + dot(hidden_ref[...], w_down[...], NT)
    result_ref[0] = full.astype(BF16)
    position = step * tile + lax.broadcasted_iota(jnp.int32, (tile, 1), 0)
    difference = jnp.where(
        position < count_ref[0], full - target_ref[0].astype(F32), 0.0
    )
    error_ref[...] += jnp.sum(difference * difference, 0, keepdims=True)
    branch = difference.astype(BF16)
    branch_ref[...] = branch.T
    for c in range(padded // 256):
        cols = slice(c * 256, (c + 1) * 256)
        hidden_back = dot(branch, w_down[:, cols], NN).astype(BF16).astype(F32)
        both_ref[:, cols] = (hidden_back * slope[:, cols]).astype(BF16)
        both_ref[:, padded + c * 256 : padded + (c + 1) * 256] = (
            hidden_back * active[:, cols]
        ).astype(BF16)
    ffn_back = dot(both_ref[:, :padded], w_gate[...], NT) + dot(
        both_ref[:, padded:], w_up[...], NT
    )
    scaled = ffn_back * gain
    middle = jnp.sum(scaled * unit, -1, keepdims=True) * (1.0 / width)
    resid_back = difference + scale * (scaled - unit * middle)
    resid_back_ref[...] = resid_back
    attended = resid_back.astype(BF16)
    attended_ref[...] = attended
    mixed_back_ref[...] = dot(w_out[...], attended, NT).astype(BF16)

    @pl.when(step == pl.num_programs(0) - 1)
    def _():
        error = 0.5 * jnp.sum(error_ref[...], -1, keepdims=True)
        high = error.astype(BF16).astype(F32)
        middle = (error - high).astype(BF16).astype(F32)
        low = error - high - middle
        column = lax.broadcasted_iota(jnp.int32, side_ref.shape, 1) - count_ref[1]
        side = jnp.where(column == 0, high, jnp.where(column == 1, middle, 0.0))
        side_ref[...] = jnp.where(column == 2, low, side).astype(BF16)


def feed_forward(count, tokens, targets, mixed, gain, late, padded, extra):
    rows, width = tokens.shape[1:]
    tile = min(rows, 256)
    token_spec = pl.BlockSpec((1, tile, width), lambda i, c: (0, i, 0))

    def flat(cols):
        return pl.BlockSpec((tile, cols), lambda i, c: (i, 0))

    tall = pl.BlockSpec((width, tile), lambda i, c: (0, i))
    return pl.pallas_call(
        functools.partial(ffn_kernel, padded),
        grid_spec=pltpu.PrefetchScalarGridSpec(
            num_scalar_prefetch=1,
            grid=(rows // tile,),
            in_specs=[
                token_spec,
                token_spec,
                tall,
                pl.BlockSpec((8, width), lambda i, c: (0, 0)),
                pl.BlockSpec(memory_space=pl.ANY),
            ],
            out_specs=[
                token_spec,
                tall,
                flat(padded),
                tall,
                flat(2 * padded),
                flat(width),
                flat(width),
                tall,
                pl.BlockSpec((width, extra), lambda i, c: (0, 0)),
            ],
            scratch_shapes=[
                pltpu.VMEM((1, width), F32),
                pltpu.VMEM((width, width), BF16),
                pltpu.VMEM((width, padded), BF16),
                pltpu.VMEM((width, padded), BF16),
                pltpu.VMEM((width, padded), BF16),
                pltpu.VMEM((tile, padded), F32),
                pltpu.VMEM((tile, padded), F32),
                pltpu.SemaphoreType.DMA((4,)),
            ],
        ),
        out_shape=[
            jax.ShapeDtypeStruct((1, rows, width), BF16),
            jax.ShapeDtypeStruct((width, rows), BF16),
            jax.ShapeDtypeStruct((rows, padded), BF16),
            jax.ShapeDtypeStruct((width, rows), BF16),
            jax.ShapeDtypeStruct((rows, 2 * padded), BF16),
            jax.ShapeDtypeStruct((rows, width), BF16),
            jax.ShapeDtypeStruct((rows, width), F32),
            jax.ShapeDtypeStruct((width, rows), BF16),
            jax.ShapeDtypeStruct((width, extra), BF16),
        ],
        compiler_params=pltpu.CompilerParams(vmem_limit_bytes=60 * 1024 * 1024),
        cost_estimate=cost(4 * rows * width * (width + 3 * padded)),
        name="feed_forward",
    )(count, tokens, targets, mixed, gain, late)


def weight_grad_kernel(form, pick_ref, left_ref, right_ref, *refs):
    total = dot(left_ref[...], right_ref[...], form)
    if len(refs) > 1:
        total = total + refs[0][...].astype(F32)
    refs[-1][...] = total.astype(BF16)


def weight_grad(left, right, pick, cols, tile, extra=None, form=NN):
    rows, depth = left.shape
    step = min(rows, 512)
    each = cols // tile
    left_spec = pl.BlockSpec((step, depth), lambda j, i, p: (i, 0))
    if form is NT:
        right_spec = pl.BlockSpec((tile, depth), lambda j, i, p: (p[0] * each + j, 0))
    else:
        right_spec = pl.BlockSpec((depth, tile), lambda j, i, p: (0, p[0] * each + j))
    out_spec = pl.BlockSpec((step, tile), lambda j, i, p: (i, j))
    in_specs = [left_spec, right_spec]
    operands = [left, right]
    if extra is not None:
        in_specs.append(out_spec)
        operands.append(extra)
    return pl.pallas_call(
        functools.partial(weight_grad_kernel, form),
        grid_spec=pltpu.PrefetchScalarGridSpec(
            num_scalar_prefetch=1,
            grid=(each, rows // step),
            in_specs=in_specs,
            out_specs=out_spec,
        ),
        out_shape=jax.ShapeDtypeStruct((rows, cols), BF16),
        compiler_params=VMEM_LIMIT,
        cost_estimate=cost(2 * rows * cols * depth),
        name="weight_grad",
    )(pick, *operands)


def swap_core(array):
    return lax.ppermute(array, "core", [(i, 1 - i) for i in range(2)])


def to_send(pieces, axis, dim):
    parts = lax.axis_size(axis)
    index = lax.axis_index(axis)
    return [
        lax.dynamic_index_in_dim(pieces, lax.rem(index + shift, parts), dim, keepdims=False)
        for shift in range(1, parts)
    ]


def send(pieces, axis):
    parts = lax.axis_size(axis)
    return [
        lax.ppermute(piece, axis, [(i, (i + shift) % parts) for i in range(parts)])
        for shift, piece in enumerate(pieces, 1)
    ]


def as_pieces(block):
    seq_parts, z_parts = lax.axis_size("seq"), lax.axis_size("z")
    return block.reshape(seq_parts, z_parts, 2, -1, block.shape[1])


def whole_rows(own, core):
    kept = lax.dynamic_index_in_dim(own, core, 0, keepdims=False)
    other = swap_core(lax.dynamic_index_in_dim(own, 1 - core, 0, keepdims=False))
    first = jnp.where(core == 0, kept, other)
    second = jnp.where(core == 0, other, kept)
    return first, second


def shifted_sum(array, parts, sign):
    total = jnp.zeros_like(array)
    for shift in range(1, parts):
        if sign > 0:
            pairs = [(i, i + shift) for i in range(parts - shift)]
        else:
            pairs = [(i + shift, i) for i in range(parts - shift)]
        total = total + lax.ppermute(array, "seq", pairs)
    return total


def body(
    inputs,
    targets,
    valid_count,
    gain_mix,
    w_query,
    w_key,
    w_value,
    w_out,
    gain_ffn,
    w_gate,
    w_up,
    w_down,
):
    everyone = ("seq", "z", "y", "core")
    seq_parts = lax.axis_size("seq")
    devices = lax.axis_size(everyone)
    seq_index = lax.axis_index("seq")
    batch_index = lax.axis_index(("z", "y", "core"))
    core = lax.axis_index("core")
    rows, width = inputs.shape[1:]
    hidden_units = w_gate.shape[1]
    padded = -(-hidden_units // 256) * 256
    owners = jnp.arange(valid_count.shape[0])
    count = jnp.sum(jnp.where(owners == batch_index, valid_count, 0))
    total_valid = jnp.sum(valid_count).astype(F32)
    place = 3 * lax.axis_index(everyone)
    valid_here = jnp.stack([count - seq_index * rows, place]).astype(jnp.int32)
    extra = -(-3 * devices // 128) * 128
    gains = jnp.pad(jnp.stack([gain_mix, gain_ffn], 1), ((0, 0), (0, 126)))
    early = gather_rows(jnp.concatenate([gains, w_query, w_key, w_value], 1))
    fill = ((0, 0), (0, padded - hidden_units))
    late = jnp.concatenate(
        [w_out, jnp.pad(w_gate, fill), jnp.pad(w_up, fill), jnp.pad(w_down, fill)], 1
    )
    late = lax.all_gather(late, everyone, axis=0, tiled=True)
    lead = HEADS * FEAT
    qkv, normed, flipped, gain_rows = project(inputs, early)
    tie = lax.optimization_barrier
    upper = HEADS // 2
    lower_state = local_state(qkv, 0, upper)
    lower_init = shifted_sum(lower_state, seq_parts, 1)
    qkv, lower_state = tie((qkv, lower_state))
    upper_init = shifted_sum(local_state(qkv, upper, upper), seq_parts, 1)
    filled = attention_forward(qkv, lower_init, 0, upper)
    mixed, den, saved = attention_forward(qkv, upper_init, upper, upper, filled)
    (
        result,
        normed_ffn,
        hidden,
        branch_back,
        both_back,
        attended_back,
        resid_back,
        mixed_back,
        side,
    ) = feed_forward(valid_here, inputs, targets, mixed, gain_rows, late, padded, extra)
    mine, others = jnp.reshape(core, (1,)), jnp.reshape(1 - core, (1,))
    half, out_half, qkv_cols = padded // 2, width // 2, HEADS * HROWS // 2

    nb, back = local_back_state(qkv, mixed_back, mixed, den)
    later = shifted_sum(back, seq_parts, -1)
    normed_ffn, nb = tie((normed_ffn, nb))
    gate_up_sent = weight_grad(normed_ffn, both_back, others, padded, half)
    gate_up_come = swap_core(gate_up_sent)
    branch_back, gate_up_sent = tie((branch_back, gate_up_sent))
    down_sent = weight_grad(branch_back, hidden, others, half, half)
    normed_ffn, down_sent = tie((normed_ffn, down_sent))
    gate_up = weight_grad(normed_ffn, both_back, mine, padded, half, gate_up_come)
    down_come = swap_core(down_sent)
    a_one = to_send(as_pieces(gate_up[:, :half]), "seq", 0)
    a_two = to_send(as_pieces(gate_up[:, half:]), "y", 2)
    mixed, a_one, a_two, later = tie((mixed, a_one, a_two, later))
    a_one, a_two = send(a_one, "seq"), send(a_two, "y")
    out_sent = weight_grad(mixed, attended_back, others, out_half, out_half)
    out_come = swap_core(out_sent)
    branch_back, out_sent = tie((branch_back, out_sent))
    down = weight_grad(branch_back, hidden, mine, half, half, down_come)
    mixed, down = tie((mixed, down))
    outer = weight_grad(mixed, attended_back, mine, out_half, out_half, out_come)
    block = jnp.concatenate([down, outer, side], 1)
    block, a_one, a_two = tie((block, a_one, a_two))
    own = w_query.shape[0]
    z_parts = lax.axis_size("z")
    one = jnp.stack(a_one).reshape(seq_parts - 1, z_parts, 2, 2, own, half)
    two = a_two[0].reshape(seq_parts, z_parts, 2, own, half)
    qkv_back, gate_up_pair, part = attention_backward(
        qkv, nb, saved, later, gate_up, one, two, block, own
    )
    gate_sum, up_sum = gate_up_pair[0], gate_up_pair[1]
    if own % 16 == 0 and rows % 512 == 0:
        input_back, first_pair, pair = last_gradients(
            normed, qkv_back, flipped, inputs, resid_back, gain_rows, part, own
        )
    else:
        qkv_sent = weight_grad(normed, qkv_back, others, qkv_cols, qkv_cols, None, NT)
        qkv_come = swap_core(qkv_sent)
        c_all = weight_grad(normed, qkv_back, mine, qkv_cols, qkv_cols, qkv_come, NT)
        input_back, first_pair, pair = input_gradient(
            qkv_back, flipped, inputs, resid_back, gain_rows, c_all, part, own
        )
    down_sum = jnp.concatenate([pair[0, :, :half], pair[1, :, :half]], 1)
    out_sum = jnp.concatenate(
        [pair[0, :, half : half + out_half], pair[1, :, half : half + out_half]], 1
    )
    errors = pair[:, 0, half + out_half : half + out_half + 3 * devices].astype(F32)
    loss = 2.0 * jnp.sum(errors) / (width * total_valid)
    first, second = first_pair[0], first_pair[1]
    qkv_sum = jnp.concatenate([first, second], 1).astype(F32).reshape(own, HEADS, HROWS)
    grad_query = qkv_sum[:, :, :FEAT].reshape(own, lead)
    grad_key = qkv_sum[:, :, FEAT : 2 * FEAT].reshape(own, lead)
    grad_value = qkv_sum[:, :, 2 * FEAT :].reshape(own, HEADS * HEAD_DIM)
    grad_gate = gate_sum[:, :hidden_units].astype(F32)
    grad_up = up_sum[:, :hidden_units].astype(F32)

    def gain_grad(gain, *pairs):
        total = sum(jnp.sum(w.astype(F32) * grad, 1) for w, grad in pairs)
        return total / gain.astype(F32)

    return (
        result,
        loss,
        input_back,
        gain_grad(gain_mix, (w_query, grad_query), (w_key, grad_key), (w_value, grad_value)),
        grad_query,
        grad_key,
        grad_value,
        out_sum.astype(F32),
        gain_grad(gain_ffn, (w_gate, grad_gate), (w_up, grad_up)),
        grad_gate,
        grad_up,
        down_sum[:, :hidden_units].astype(F32),
    )


def solution(mesh):
    seq_parts, fsdp_parts = mesh.shape["seq"], mesh.shape["fsdp"]
    fine = jax.sharding.Mesh(
        mesh.devices.reshape(seq_parts, fsdp_parts // 4, 2, 2), ("seq", "z", "y", "core")
    )
    both = P(("seq", "z", "y", "core"))
    rows = P(("seq", "z", "y", "core"), None)
    tokens = P(("z", "y", "core"), "seq", None)
    return jax.shard_map(
        body,
        mesh=fine,
        in_specs=(tokens, tokens, P(), both, rows, rows, rows, rows, both, rows, rows, rows),
        out_specs=(tokens, P(), tokens, both, rows, rows, rows, rows, both, rows, rows, rows),
        check_vma=False,
    )
```
